32 devices in a mesh: row: 8 (over z, y), col: 4 (over x, core).
Axes of the slice: x: 2, y: 2, z: 4, core: 2. Of those that a mesh axis runs over, the one named last changes fastest.
Arguments:
- fractions_source: float32 [12, 512, 512], P('col', 'row'), may hold values from 0 to 1, as said below
- x_source_edges: int32 [513], replicated, may hold values from 0 to 24576, as said below
- x_target_edges: int32 [385], replicated, may hold values from 0 to 24576, as said below
- y_source_edges: int32 [513], replicated, may hold values from 0 to 24576, as said below
- y_target_edges: int32 [385], replicated, may hold values from 0 to 24576, as said below
- conductivity_table: int32 [6], replicated, may hold values from 4 to 64
- capacity: float32 [6], replicated, may hold values from 0.5 to 4
- thermal_source_term: float32 [2, 384, 384], P(None, 'row', 'col'), may hold values from -40 to 40
Outputs:
- rezoned_occupancy_shares: float32 [12, 384, 384], P(None, 'row', 'col')
- thermal_iterate: float32 [2, 384, 384], P(None, 'row', 'col')
- remaining_defect: float32 [2, 384, 384], P(None, 'row', 'col')
The draws below stay inside these ranges and needn't reach their ends.
Inputs may be any that keep to these rules, and one draw needn't show every extreme that they name: `fractions_source`: positive; for every z layer and source cell the 6 materials' fractions sum to one. `x_source_edges`: strictly increasing; every 64-th source edge along x coincides with every 48-th target edge along x, at multiples of 3072; the first edge is 0 and the last is the largest value. `x_target_edges`: strictly increasing; shares the walls of x_source_edges at every 48-th edge; the first edge is 0 and the last is the largest value. `y_source_edges`: strictly increasing; every 64-th source edge along y coincides with every 48-th target edge along y, at multiples of 3072; the first edge is 0 and the last is the largest value. `y_target_edges`: strictly increasing; shares the walls of y_source_edges at every 48-th edge; the first edge is 0 and the last is the largest value.
All inputs are finite; a program needn't handle non-finite values.
Results may differ from the reference program's by a relative error of at most 0.0003.
Values sent between devices are 32-bit elements; how exact they have to be, the bound alone decides.
No kernel may reach another device: no remote copies, remote signals or barrier semaphores. Data moves between devices by JAX's collectives and lax.ppermute only.
A program may use at most 64 MiB of HBM per device.

```python
import math
import jax
import jax.numpy as jnp
from jax import lax

M = 6
ZL = 2
SBLK = 64
TBLK = 48
ITERS = 3
NS = 512
NT = 384


def edge_draw(key, count_cells, spacing, wall_every, spread):
    offsets = jax.random.randint(key, (count_cells + 1,), -spread, spread + 1)
    positions = jnp.arange(count_cells + 1, dtype=jnp.int32)
    offsets = jnp.where(positions % wall_every == 0, 0, offsets)
    return (positions * spacing + offsets).astype(jnp.int32)


def draw_x_source_edges(key, part):
    return edge_draw(jax.random.fold_in(key, 11), NS, TBLK, SBLK, TBLK // 4)


def draw_x_target_edges(key, part):
    return edge_draw(jax.random.fold_in(key, 12), NT, SBLK, TBLK, SBLK // 4)


def draw_y_source_edges(key, part):
    return edge_draw(jax.random.fold_in(key, 13), NS, TBLK, SBLK, TBLK // 4)


def draw_y_target_edges(key, part):
    return edge_draw(jax.random.fold_in(key, 14), NT, SBLK, TBLK, SBLK // 4)


def draw_fractions_source(key, part):
    first_key = jax.random.fold_in(key, 21)
    weights_raw = jax.random.uniform(first_key, (ZL, M, NS, NS), jnp.float32, 0.05, 1.0)
    summed = jnp.sum(weights_raw, axis=1, keepdims=True)
    return (weights_raw / summed).reshape(ZL * M, NS, NS)


def draw_thermal_source_term(key, part):
    first_key = jax.random.fold_in(key, 31)
    ramp = jnp.arange(NT, dtype=jnp.float32) / (NT - 1)
    scaling = 10.0 ** (ramp[:, None] + ramp[None, :] - 1.0)
    return jax.random.truncated_normal(first_key, -4.0, 4.0, (ZL, NT, NT), jnp.float32) * scaling


def set_ends(entries, rng, smallest, top_value):
    index_at = [jax.random.randint(jax.random.fold_in(rng, axis), (), 0, length) for axis, length in enumerate(entries.shape)]
    longest = entries.shape.index(max(entries.shape))
    next_to = index_at[:longest] + [(index_at[longest] + 1) % entries.shape[longest]] + index_at[longest + 1:]
    return entries.at[tuple(index_at)].set(smallest).at[tuple(next_to)].set(top_value)


def setup_inputs(seed: int = 0) -> dict:
    arg_keys = jax.random.split(jax.random.key(seed), 9)
    fractions_source = draw_fractions_source(jax.random.fold_in(arg_keys[8], 71), 0)
    x_source_edges = draw_x_source_edges(jax.random.fold_in(arg_keys[8], 71), 0)
    x_target_edges = draw_x_target_edges(jax.random.fold_in(arg_keys[8], 71), 0)
    y_source_edges = draw_y_source_edges(jax.random.fold_in(arg_keys[8], 71), 0)
    y_target_edges = draw_y_target_edges(jax.random.fold_in(arg_keys[8], 71), 0)
    conductivity_table = set_ends(jax.random.randint(arg_keys[5], (M,), 4, 65), jax.random.fold_in(arg_keys[5], 1), 4, 64).astype(jnp.int32)
    capacity = jnp.clip(jnp.exp(jax.random.uniform(arg_keys[6], (M,), jnp.float32, math.log(0.5), math.log(4.0))), 0.5, 4.0)
    thermal_source_term = draw_thermal_source_term(jax.random.fold_in(arg_keys[8], 71), 0)
    return {"fractions_source": fractions_source, "x_source_edges": x_source_edges, "x_target_edges": x_target_edges, "y_source_edges": y_source_edges, "y_target_edges": y_target_edges, "conductivity_table": conductivity_table, "capacity": capacity, "thermal_source_term": thermal_source_term}


def margin_blocks(source_edges, target_mesh_edges, source_block, target_block):
    block_list = (source_edges.shape[0] - 1) // source_block
    src_lo = source_edges[:-1].reshape(block_list, 1, source_block)
    src_hi = source_edges[1:].reshape(block_list, 1, source_block)
    tgt_lo = target_mesh_edges[:-1].reshape(block_list, target_block, 1)
    tgt_hi = target_mesh_edges[1:].reshape(block_list, target_block, 1)
    shared = jnp.maximum(jnp.minimum(src_hi, tgt_hi) - jnp.maximum(src_lo, tgt_lo), 0)
    return shared.astype(jnp.float32) / (tgt_hi - tgt_lo).astype(jnp.float32)


def rezone_plane(layer_plane, weight_x, vertical_factor):
    block_list = weight_x.shape[0]
    target_block = weight_x.shape[1]
    source_block = weight_x.shape[2]
    source_grid = layer_plane.reshape(block_list, source_block, block_list, source_block)
    along_y = jnp.einsum("asbu,bvu->asbv", source_grid, vertical_factor, precision=lax.Precision.HIGHEST)
    along_x = jnp.einsum("asbv,ats->bvat", along_y, weight_x, precision=lax.Precision.HIGHEST)
    return along_x.reshape(block_list * target_block, block_list * target_block)


def face_weights(padded_array):
    center = padded_array[1:-1, 1:-1, 1:-1]
    neighbours = (padded_array[2:, 1:-1, 1:-1], padded_array[:-2, 1:-1, 1:-1], padded_array[1:-1, 2:, 1:-1],
                  padded_array[1:-1, :-2, 1:-1], padded_array[1:-1, 1:-1, 2:], padded_array[1:-1, 1:-1, :-2])
    return tuple(2.0 * center * beside / (center + beside) for beside in neighbours)


def stencil(padded_field, face_list, cell_capacity):
    center = padded_field[1:-1, 1:-1, 1:-1]
    neighbours = (padded_field[2:, 1:-1, 1:-1], padded_field[:-2, 1:-1, 1:-1], padded_field[1:-1, 2:, 1:-1],
                  padded_field[1:-1, :-2, 1:-1], padded_field[1:-1, 1:-1, 2:], padded_field[1:-1, 1:-1, :-2])
    result = cell_capacity * center
    for weight, beside in zip(face_list, neighbours):
        result = result + weight * (center - beside)
    return result


def reference(fractions_source, x_source_edges, x_target_edges, y_source_edges, y_target_edges, conductivity_table, capacity, thermal_source_term):
    weight_x = margin_blocks(x_source_edges, x_target_edges, SBLK, TBLK)
    vertical_factor = margin_blocks(y_source_edges, y_target_edges, SBLK, TBLK)
    rezoned_occupancy_shares = lax.map(lambda layer_plane: rezone_plane(layer_plane, weight_x, vertical_factor), fractions_source)
    stacked = rezoned_occupancy_shares.reshape(ZL, M, NT, NT)
    substance_diffusivity = conductivity_table.astype(jnp.float32) / 16.0
    inverse = jnp.sum(stacked / substance_diffusivity[None, :, None, None], axis=1)
    cell_k = 1.0 / inverse
    cell_capacity = jnp.sum(stacked * capacity[None, :, None, None], axis=1)
    face_list = face_weights(jnp.pad(cell_k, 1))
    thermal_iterate = jnp.zeros_like(thermal_source_term)
    remaining_defect = thermal_source_term
    conjugate_update_vector = thermal_source_term
    norm_now = jnp.sum(remaining_defect * remaining_defect)
    for iteration in range(ITERS):
        applied = stencil(jnp.pad(conjugate_update_vector, 1), face_list, cell_capacity)
        line_minimizer_alpha = norm_now / jnp.sum(conjugate_update_vector * applied)
        thermal_iterate = thermal_iterate + line_minimizer_alpha * conjugate_update_vector
        remaining_defect = remaining_defect - line_minimizer_alpha * applied
        norm_next = jnp.sum(remaining_defect * remaining_defect)
        conjugate_update_vector = remaining_defect + (norm_next / norm_now) * conjugate_update_vector
        norm_now = norm_next
    return rezoned_occupancy_shares, thermal_iterate, remaining_defect
```

```python
import functools

import jax
import jax.numpy as jnp
from jax import lax
from jax.experimental import pallas as pl
from jax.experimental.pallas import tpu as pltpu
from jax.sharding import PartitionSpec as P

M = 6
SBLK = 64
TBLK = 48
ITERS = 3
RIM = ITERS
ROWS = 56
LANES = 128
GROUPS = ROWS // 8
TAIL = LANES // GROUPS // 8 * 8
VMEM = 48 * 1024 * 1024
TINY = 1e-30
F32 = jnp.float32
EXACT = lax.Precision.HIGHEST


def tiles(cells):
    return -(-cells // LANES)


def overlap(src_lo, src_hi, tgt_lo, tgt_hi):
    shared = jnp.maximum(jnp.minimum(src_hi, tgt_hi) - jnp.maximum(src_lo, tgt_lo), 0.0)
    return shared / jnp.maximum(tgt_hi - tgt_lo, 1.0)


def window_rows(row_count):
    count = row_count // 2 - 1
    rows = [[2 * q + 1, 2 * q + 2] for q in range(count)]
    rows[0] = [0] + rows[0]
    rows[-1] = rows[-1] + [row_count - 1]
    return rows


def rezone_kernel(row_count, src_ref, tgt_ref, xedge_ref, frac_ref, field_ref, out_ref, along_ref):
    me = lax.axis_index("row")
    pairs = frac_ref.shape[0]
    cols = jnp.transpose(xedge_ref[:, LANES:])
    weight_x = overlap(
        xedge_ref[0:1, 0:SBLK], xedge_ref[1:2, 0:SBLK], cols[0:TBLK, 0:1], cols[0:TBLK, 1:2]
    )
    along_ref[pairs * TBLK :, :] = jnp.zeros_like(along_ref[pairs * TBLK :, :])
    for p in range(pairs):
        along_ref[p * TBLK : (p + 1) * TBLK, :] = jnp.dot(
            weight_x, frac_ref[p], precision=EXACT, preferred_element_type=F32
        )
    width = 4 * SBLK
    for q, rows in enumerate(window_rows(row_count)):
        span = pl.ds(2 * q * SBLK, width)
        parts = []
        for r in rows:
            edges = jnp.transpose(tgt_ref[:, r * LANES : (r + 1) * LANES])
            parts.append(
                overlap(
                    src_ref[0:1, span], src_ref[1:2, span], edges[0:ROWS, 0:1], edges[0:ROWS, 1:2]
                )
            )
        weight_y = jnp.concatenate(parts, axis=0)
        block = lax.dot_general(
            weight_y,
            along_ref[:, span],
            (((1,), (1,)), ((), ())),
            precision=EXACT,
            preferred_element_type=F32,
        )
        for n, r in enumerate(rows):
            mine = block[n * ROWS : (n + 1) * ROWS]
            out_ref[r, 0:ROWS, :] = mine[:, 0:LANES]
            packed = mine[0:8, LANES:]
            for g in range(1, GROUPS):
                packed = packed + pltpu.roll(mine[8 * g : 8 * g + 8, LANES:], TAIL * g, 1)
            out_ref[r, ROWS : ROWS + 8, :] = packed
    zlayers, height, breadth = field_ref.shape
    base = ROWS + 8
    for r in range(row_count):
        for t in range(tiles(breadth)):
            lo, hi = t * LANES, min((t + 1) * LANES, breadth)
            if hi - lo < LANES:
                out_ref[r, base + 8 * t : base + 8 * t + 8, :] = jnp.zeros((8, LANES), F32)
            for layer in range(zlayers):
                rim = jnp.where(
                    r > me,
                    field_ref[layer, height - RIM :, lo:hi],
                    field_ref[layer, :RIM, lo:hi],
                )
                at = base + 8 * t + RIM * layer
                out_ref[r, at : at + RIM, 0 : hi - lo] = rim


def regroup_kernel(row_count, col_count, got_ref, field_ref, out_ref, ext_ref):
    my_row, my_col = lax.axis_index("row"), lax.axis_index("col")
    zlayers, height, breadth = field_ref.shape
    pairs, width = out_ref.shape[1], out_ref.shape[3]
    per_col = row_count // col_count
    base = ROWS + 8
    ext_ref[...] = jnp.zeros_like(ext_ref)
    below, above = jnp.maximum(my_row - 1, 0), jnp.minimum(my_row + 1, row_count - 1)
    for layer in range(zlayers):
        ext_ref[layer, 0:height, 0:breadth] = field_ref[layer]
        for t in range(tiles(breadth)):
            lo, hi = t * LANES, min((t + 1) * LANES, breadth)
            at = base + 8 * t + RIM * layer
            after = got_ref[above, at : at + RIM, 0 : hi - lo]
            before = got_ref[below, at : at + RIM, 0 : hi - lo]
            ext_ref[layer, height : height + RIM, lo:hi] = jnp.where(
                my_row < row_count - 1, after, 0.0
            )
            ext_ref[layer, ROWS - RIM : ROWS, lo:hi] = jnp.where(my_row > 0, before, 0.0)

    def piece(block, pair, first, last):
        start = pair * TBLK
        lo, hi = start + first, start + last
        parts = []
        if lo < LANES:
            parts.append(got_ref[block, 0:ROWS, lo : min(hi, LANES)])
        if hi > LANES:
            a, b = max(lo, LANES) - LANES, hi - LANES
            tail = got_ref[block, ROWS : ROWS + 8, :]
            parts.append(
                jnp.concatenate([tail[:, TAIL * g + a : TAIL * g + b] for g in range(GROUPS)], axis=0)
            )
        return parts[0] if len(parts) == 1 else jnp.concatenate(parts, axis=1)

    for c in range(col_count):
        for p in range(pairs):
            parts = [piece(c * per_col + j, p, 0, TBLK) for j in range(per_col)]
            if c + 1 < col_count:
                parts.append(piece((c + 1) * per_col, p, 0, RIM))
            else:
                parts.append(jnp.zeros((ROWS, RIM), F32))
            if p < zlayers:
                whole = ext_ref[p]
                parts.append(
                    jnp.where(c > my_col, whole[:, breadth - RIM : breadth], whole[:, 0:RIM])
                )
            else:
                parts.append(jnp.zeros((ROWS, RIM), F32))
            parts.append(jnp.zeros((ROWS, width - breadth - 3 * RIM), F32))
            if c:
                parts.append(piece(c * per_col - 1, p, TBLK - RIM, TBLK))
            else:
                parts.append(jnp.zeros((ROWS, RIM), F32))
            out_ref[c, p] = jnp.concatenate(parts, axis=1)


def basis_kernel(
    col_count, height, breadth, table_ref, got_ref, ext_ref, shares_ref, basis_ref, sums_ref
):
    my_col = lax.axis_index("col")
    zlayers = ext_ref.shape[0]
    pairs, rows, width = got_ref.shape[1:]
    lane = lax.broadcasted_iota(jnp.int32, (rows, width), 1)
    before, after = jnp.maximum(my_col - 1, 0), jnp.minimum(my_col + 1, col_count - 1)

    def ahead(array, axis):
        return pltpu.roll(array, array.shape[axis] - 1, axis)

    def behind(array, axis):
        return pltpu.roll(array, 1, axis)

    def face(one, other):
        return 2.0 * one * other / jnp.maximum(one + other, TINY)

    cell_k, heat, field = [], [], []
    for z in range(zlayers):
        inverse = jnp.zeros((rows, width), F32)
        total = jnp.zeros((rows, width), F32)
        for m in range(M):
            c, p = divmod(z * M + m, pairs)
            share = got_ref[c, p]
            shares_ref[z * M + m] = share[0:height, 0:breadth]
            inside = jnp.where((lane < breadth + RIM) | (lane >= width - RIM), share, 0.0)
            inverse = inverse + inside * table_ref[m]
            total = total + inside * table_ref[M + m]
        cell_k.append(jnp.where(inverse > 0.0, 1.0 / jnp.where(inverse > 0.0, inverse, 1.0), 0.0))
        heat.append(total)
        left, right = got_ref[before, z], got_ref[after, z]
        left = pltpu.roll(left, width - (breadth + 2 * RIM), 1)
        right = pltpu.roll(right, width - RIM, 1)
        value = ext_ref[z]
        value = jnp.where(
            (lane >= breadth) & (lane < breadth + RIM) & (my_col < col_count - 1), right, value
        )
        value = jnp.where((lane >= width - RIM) & (my_col > 0), left, value)
        field.append(value)
    face_x = [face(k, ahead(k, 1)) for k in cell_k]
    face_y = [face(k, ahead(k, 0)) for k in cell_k]
    face_z = [face(cell_k[z], cell_k[z + 1]) for z in range(zlayers - 1)]

    def operate(w):
        result = []
        for z in range(zlayers):
            flow_x = face_x[z] * (w[z] - ahead(w[z], 1))
            flow_y = face_y[z] * (w[z] - ahead(w[z], 0))
            value = heat[z] * w[z] + (flow_x - behind(flow_x, 1)) + (flow_y - behind(flow_y, 0))
            if z + 1 < zlayers:
                value = value + face_z[z] * (w[z] - w[z + 1])
            if z:
                value = value - face_z[z - 1] * (w[z - 1] - w[z])
            result.append(value)
        return result

    shift, scale = table_ref[2 * M], table_ref[2 * M + 1]

    def shifted(w):
        return [(a - shift * b) * scale for a, b in zip(operate(w), w)]

    basis = [field, shifted(field)]
    for _ in range(ITERS - 1):
        basis.append([2.0 * a - b for a, b in zip(shifted(basis[-1]), basis[-2])])
    own = [
        [jnp.where(lane < breadth, layer, 0.0)[0:height] for layer in vector] for vector in basis
    ]
    for n in range(ITERS):
        for z in range(zlayers):
            basis_ref[n, z] = own[n + 1][z][:, 0:breadth]
    slot = lax.broadcasted_iota(jnp.int32, (1, LANES), 1)
    packed = jnp.zeros((1, LANES), F32)
    at = 0
    for a in range(ITERS + 1):
        for b in range(a, ITERS + 1):
            product = own[a][0] * own[b][0]
            for z in range(1, zlayers):
                product = product + own[a][z] * own[b][z]
            value = jnp.sum(product, axis=0, keepdims=True)
            value = jnp.sum(value, axis=1, keepdims=True)
            packed = packed + jnp.where(slot == at, value, 0.0)
            at += 1
    sums_ref[...] = jnp.broadcast_to(packed[None], sums_ref.shape)


def finish_kernel(table_ref, sums_ref, field_ref, basis_ref, iterate_ref, defect_ref):
    total = jnp.sum(sums_ref[...], axis=0)
    gram = {}
    at = 0
    for a in range(ITERS + 1):
        for b in range(a, ITERS + 1):
            gram[a, b] = gram[b, a] = total[:, at : at + 1]
            at += 1
    shift, scale = table_ref[2 * M], table_ref[2 * M + 2]

    def inner(left, right):
        value = None
        for a, one in left.items():
            for b, other in right.items():
                term = one * other * gram[a, b]
                value = term if value is None else value + term
        return value

    def combine(left, factor, right):
        result = dict(left)
        for a, one in right.items():
            result[a] = result[a] + factor * one if a in result else factor * one
        return result

    def apply(vector):
        result = {}
        for a, one in vector.items():
            if a:
                moved = {a - 1: 0.5 * scale * one, a: shift * one, a + 1: 0.5 * scale * one}
            else:
                moved = {0: shift * one, 1: scale * one}
            for b, other in moved.items():
                result[b] = result[b] + other if b in result else other
        return result

    one = jnp.ones((1, 1), F32)
    iterate, defect, direction = {}, {0: one}, {0: one}
    norm = gram[0, 0]
    for iteration in range(ITERS):
        applied = apply(direction)
        step = norm / inner(direction, applied)
        iterate = combine(iterate, step, direction)
        defect = combine(defect, -step, applied)
        if iteration + 1 < ITERS:
            following = inner(defect, defect)
            direction = combine(defect, following / norm, direction)
            norm = following
    for z in range(field_ref.shape[0]):
        vectors = [field_ref[z]] + [basis_ref[n, z] for n in range(ITERS)]
        iterate_ref[z] = sum(weight * vectors[a] for a, weight in iterate.items())
        defect_ref[z] = sum(weight * vectors[a] for a, weight in defect.items())


def per_device(
    row_count,
    col_count,
    fractions_source,
    x_source_edges,
    x_target_edges,
    y_source_edges,
    y_target_edges,
    conductivity_table,
    capacity,
    thermal_source_term,
):
    pairs, _, source_cells = fractions_source.shape
    zlayers, height, breadth = thermal_source_term.shape
    width = LANES * tiles(breadth + 4 * RIM)
    send_rows = ROWS + 8 + 8 * tiles(breadth)
    params = pltpu.CompilerParams(vmem_limit_bytes=VMEM)

    source = jnp.stack([y_source_edges[:-1], y_source_edges[1:]]).astype(F32)

    def by_block(edges):
        own = edges.reshape(row_count, TBLK)
        edge = jnp.zeros((1, RIM), edges.dtype)
        return jnp.concatenate(
            [
                own,
                jnp.concatenate([own[1:, :RIM], edge]),
                jnp.zeros((row_count, ROWS - TBLK - 2 * RIM), edges.dtype),
                jnp.concatenate([edge, own[:-1, TBLK - RIM :]]),
                jnp.zeros((row_count, LANES - ROWS), edges.dtype),
            ],
            axis=1,
        ).reshape(-1)

    target = jnp.stack([by_block(y_target_edges[:-1]), by_block(y_target_edges[1:])]).astype(F32)
    target = jnp.pad(target, ((0, 6), (0, 0)))
    me = lax.axis_index("row")
    x_source = lax.dynamic_slice(x_source_edges, (me * SBLK,), (SBLK + 1,))
    x_target = lax.dynamic_slice(x_target_edges, (me * TBLK,), (TBLK + 1,))
    x_edges = jnp.concatenate(
        [
            jnp.pad(jnp.stack([x_source[:-1], x_source[1:]]), ((0, 6), (0, LANES - SBLK))),
            jnp.pad(jnp.stack([x_target[:-1], x_target[1:]]), ((0, 6), (0, LANES - TBLK))),
        ],
        axis=1,
    ).astype(F32)
    resistance = 16.0 / conductivity_table.astype(F32)
    middle = 5.0 * M / jnp.sum(resistance)
    table = jnp.concatenate(
        [
            resistance,
            capacity,
            jnp.stack([jnp.mean(capacity) + middle, 1.0 / middle, middle]),
        ]
    )

    smem = pl.BlockSpec(memory_space=pltpu.SMEM)
    vmem = pl.BlockSpec(memory_space=pltpu.VMEM)
    along_rows = -(-pairs * TBLK // LANES) * LANES
    outgoing = pl.pallas_call(
        functools.partial(rezone_kernel, row_count),
        out_shape=jax.ShapeDtypeStruct((row_count, send_rows, LANES), F32),
        in_specs=[vmem] * 5,
        out_specs=vmem,
        scratch_shapes=[pltpu.VMEM((along_rows, source_cells), F32)],
        compiler_params=params,
        name="rezone",
    )(source, target, x_edges, fractions_source, thermal_source_term)
    arrived = lax.all_to_all(outgoing, "row", split_axis=0, concat_axis=0, tiled=True)
    regrouped, extended = pl.pallas_call(
        functools.partial(regroup_kernel, row_count, col_count),
        out_shape=[
            jax.ShapeDtypeStruct((col_count, pairs, ROWS, width), F32),
            jax.ShapeDtypeStruct((zlayers, ROWS, width), F32),
        ],
        in_specs=[vmem] * 2,
        out_specs=[vmem] * 2,
        compiler_params=params,
        name="regroup",
    )(arrived, thermal_source_term)
    gathered = lax.all_to_all(regrouped, "col", split_axis=0, concat_axis=0, tiled=True)
    rezoned_occupancy_shares, basis, sums = pl.pallas_call(
        functools.partial(basis_kernel, col_count, height, breadth),
        out_shape=[
            jax.ShapeDtypeStruct((zlayers * M, height, breadth), F32),
            jax.ShapeDtypeStruct((ITERS, zlayers, height, breadth), F32),
            jax.ShapeDtypeStruct((row_count * col_count, 1, LANES), F32),
        ],
        in_specs=[smem, vmem, vmem],
        out_specs=[vmem] * 3,
        compiler_params=params,
        name="basis",
    )(table, gathered, extended)
    sums = lax.all_to_all(sums, ("row", "col"), split_axis=0, concat_axis=0, tiled=True)
    thermal_iterate, remaining_defect = pl.pallas_call(
        finish_kernel,
        out_shape=[jax.ShapeDtypeStruct((zlayers, height, breadth), F32)] * 2,
        in_specs=[smem, vmem, vmem, vmem],
        out_specs=[vmem] * 2,
        compiler_params=params,
        name="finish",
    )(table, sums, thermal_source_term, basis)
    return rezoned_occupancy_shares, thermal_iterate, remaining_defect


def solution(mesh):
    placed = (P("col", "row", None), P(), P(), P(), P(), P(), P(), P(None, "row", "col"))
    return jax.shard_map(
        functools.partial(per_device, mesh.shape["row"], mesh.shape["col"]),
        mesh=mesh,
        in_specs=placed,
        out_specs=(P(None, "row", "col"), P(None, "row", "col"), P(None, "row", "col")),
        check_vma=False,
    )
```

```python
import functools

import jax
import jax.numpy as jnp
from jax import lax
from jax.experimental import pallas as pl
from jax.experimental.pallas import tpu as pltpu
from jax.sharding import PartitionSpec as P

M = 6
SBLK = 64
TBLK = 48
ITERS = 3
RIM = ITERS
ROWS = 56
LANES = 128
GROUPS = ROWS // 8
TAIL = LANES // GROUPS // 8 * 8
VMEM = 48 * 1024 * 1024
FULL = 63 * 1024 * 1024
TINY = 1e-30
F32 = jnp.float32
EXACT = lax.Precision.HIGHEST


def tiles(cells):
    return -(-cells // LANES)


def overlap(src_lo, src_hi, tgt_lo, tgt_hi):
    shared = jnp.maximum(jnp.minimum(src_hi, tgt_hi) - jnp.maximum(src_lo, tgt_lo), 0.0)
    return shared / jnp.maximum(tgt_hi - tgt_lo, 1.0)


def window_rows(row_count):
    count = row_count // 2 - 1
    rows = [[2 * q + 1, 2 * q + 2] for q in range(count)]
    rows[0] = [0] + rows[0]
    rows[-1] = rows[-1] + [row_count - 1]
    return rows


def rezone_kernel(
    row_count,
    xs_hbm,
    xt_hbm,
    ys_hbm,
    yt_hbm,
    frac_hbm,
    field_hbm,
    out_ref,
    xs_ref,
    xt_ref,
    ys_ref,
    yt_ref,
    frac_ref,
    field_ref,
    edges_ref,
    along_ref,
    sems,
):
    me = lax.axis_index("row")
    pairs = frac_ref.shape[0]
    moves = [
        pltpu.make_async_copy(here, there, sems.at[n])
        for n, (here, there) in enumerate(
            (
                (xs_hbm, xs_ref),
                (xt_hbm, xt_ref),
                (ys_hbm, ys_ref),
                (yt_hbm, yt_ref),
                (field_hbm, field_ref),
            )
        )
    ]
    loads = [
        pltpu.make_async_copy(frac_hbm.at[p], frac_ref.at[p], sems.at[len(moves) + p])
        for p in range(pairs)
    ]
    for move in moves + loads:
        move.start()
    edges_ref[...] = jnp.zeros_like(edges_ref)
    along_ref[pairs * TBLK :, :] = jnp.zeros_like(along_ref[pairs * TBLK :, :])
    for n, ref in enumerate((xs_ref, xt_ref, ys_ref, yt_ref)):
        moves[n].wait()
        edges_ref[n : n + 1, 0 : ref.shape[0]] = ref[...].astype(F32)[None, :]

    def from_here(row, start, lane):
        base = start // LANES * LANES
        if not isinstance(base, int):
            base = pl.multiple_of(base, LANES)
        window = edges_ref[row : row + 1, pl.ds(base, 2 * LANES)]
        return pltpu.roll(window, (lane - (start - base) + 2 * LANES) % (2 * LANES), 1)

    def following(turned):
        return pltpu.roll(turned, 2 * LANES - 1, 1)

    x_lo = from_here(0, me * SBLK, 0)
    x_hi = following(x_lo)
    mine = from_here(1, me * TBLK, 0)
    lane = lax.broadcasted_iota(jnp.int32, (1, LANES), 1)
    lows, highs = [mine[:, 0:LANES]], [following(mine)[:, 0:LANES]]
    for r in range(row_count):
        own = from_here(3, r * TBLK, 0)
        upper = TBLK if r + 1 == row_count else TBLK + RIM
        if r:
            rim = from_here(3, r * TBLK - RIM, ROWS - RIM)
            rims = rim, following(rim)
        else:
            rims = (jnp.zeros((1, 2 * LANES), F32),) * 2
        for rows, value, edge in ((lows, own, rims[0]), (highs, following(own), rims[1])):
            value = jnp.where(lane < upper, value[:, 0:LANES], 0.0)
            inside = (lane >= ROWS - RIM) & (lane < ROWS)
            rows.append(jnp.where(inside, edge[:, 0:LANES], value))
    count = row_count + 1
    spare = jnp.zeros((-2 * count % 8, LANES), F32)
    columns = jnp.transpose(jnp.concatenate(lows + highs + [spare], axis=0))

    weight_x = overlap(
        x_lo[:, 0:SBLK], x_hi[:, 0:SBLK], columns[0:TBLK, 0:1], columns[0:TBLK, count : count + 1]
    )
    width = 4 * SBLK
    weights_y = []
    for q, rows in enumerate(window_rows(row_count)):
        src_lo = edges_ref[2:3, 2 * q * SBLK : 2 * q * SBLK + width]
        src_hi = edges_ref[2:3, 2 * q * SBLK + 1 : 2 * q * SBLK + width + 1]
        weights_y.append(
            jnp.concatenate(
                [
                    overlap(
                        src_lo,
                        src_hi,
                        columns[0:ROWS, 1 + r : 2 + r],
                        columns[0:ROWS, count + 1 + r : count + 2 + r],
                    )
                    for r in rows
                ],
                axis=0,
            )
        )
    for p in range(pairs):
        loads[p].wait()
        along_ref[p * TBLK : (p + 1) * TBLK, :] = jnp.dot(
            weight_x, frac_ref[p], precision=EXACT, preferred_element_type=F32
        )
    for q, rows in enumerate(window_rows(row_count)):
        block = lax.dot_general(
            weights_y[q],
            along_ref[:, 2 * q * SBLK : 2 * q * SBLK + width],
            (((1,), (1,)), ((), ())),
            precision=EXACT,
            preferred_element_type=F32,
        )
        for n, r in enumerate(rows):
            mine = block[n * ROWS : (n + 1) * ROWS]
            out_ref[r, 0:ROWS, :] = mine[:, 0:LANES]
            packed = mine[0:8, LANES:]
            for g in range(1, GROUPS):
                packed = packed + pltpu.roll(mine[8 * g : 8 * g + 8, LANES:], TAIL * g, 1)
            out_ref[r, ROWS : ROWS + 8, :] = packed
    moves[4].wait()
    zlayers, height, breadth = field_ref.shape
    base = ROWS + 8
    for r in range(row_count):
        for t in range(tiles(breadth)):
            lo, hi = t * LANES, min((t + 1) * LANES, breadth)
            for layer in range(zlayers):
                rim = jnp.where(
                    r > me,
                    field_ref[layer, height - RIM :, lo:hi],
                    field_ref[layer, :RIM, lo:hi],
                )
                at = base + 8 * t + RIM * layer
                out_ref[r, at : at + RIM, 0 : hi - lo] = rim


def regroup_kernel(row_count, col_count, got_ref, field_ref, ext_ref, *out_refs):
    my_row, my_col = lax.axis_index("row"), lax.axis_index("col")
    zlayers, height, breadth = field_ref.shape
    pairs, _, width = out_refs[0].shape
    per_col = row_count // col_count
    base = ROWS + 8
    ext_ref[...] = jnp.zeros_like(ext_ref)
    below, above = jnp.maximum(my_row - 1, 0), jnp.minimum(my_row + 1, row_count - 1)
    for layer in range(zlayers):
        ext_ref[layer, 0:height, 0:breadth] = field_ref[layer]
        for t in range(tiles(breadth)):
            lo, hi = t * LANES, min((t + 1) * LANES, breadth)
            at = base + 8 * t + RIM * layer
            after = got_ref[above, at : at + RIM, 0 : hi - lo]
            before = got_ref[below, at : at + RIM, 0 : hi - lo]
            ext_ref[layer, height : height + RIM, lo:hi] = jnp.where(
                my_row < row_count - 1, after, 0.0
            )
            ext_ref[layer, ROWS - RIM : ROWS, lo:hi] = jnp.where(my_row > 0, before, 0.0)

    def piece(block, pair, first, last):
        start = pair * TBLK
        lo, hi = start + first, start + last
        parts = []
        if lo < LANES:
            parts.append(got_ref[block, 0:ROWS, lo : min(hi, LANES)])
        if hi > LANES:
            a, b = max(lo, LANES) - LANES, hi - LANES
            tail = got_ref[block, ROWS : ROWS + 8, :]
            parts.append(
                jnp.concatenate([tail[:, TAIL * g + a : TAIL * g + b] for g in range(GROUPS)], axis=0)
            )
        return parts[0] if len(parts) == 1 else jnp.concatenate(parts, axis=1)

    for mask, out_ref in enumerate(out_refs):
        c = my_col ^ mask
        first = c * per_col
        left, right = jnp.maximum(first - 1, 0), jnp.minimum(first + per_col, row_count - 1)
        for p in range(pairs):
            parts = [piece(first + j, p, 0, TBLK) for j in range(per_col)]
            parts.append(jnp.where(c < col_count - 1, piece(right, p, 0, RIM), 0.0))
            if p < zlayers and mask:
                whole = ext_ref[p]
                parts.append(
                    jnp.where(c > my_col, whole[:, breadth - RIM : breadth], whole[:, 0:RIM])
                )
            else:
                parts.append(jnp.zeros((ROWS, RIM), F32))
            parts.append(jnp.zeros((ROWS, width - breadth - 3 * RIM), F32))
            parts.append(jnp.where(c > 0, piece(left, p, TBLK - RIM, TBLK), 0.0))
            out_ref[p] = jnp.concatenate(parts, axis=1)


def basis_kernel(col_count, height, breadth, table_ref, ext_ref, *refs):
    arrivals, (shares_ref, basis_ref, sums_ref, got_ref) = refs[:col_count], refs[col_count:]
    my_col = lax.axis_index("col")
    for mask, arrival in enumerate(arrivals):
        got_ref[my_col ^ mask] = arrival[...]
    zlayers = ext_ref.shape[0]
    pairs, rows, width = got_ref.shape[1:]
    lane = lax.broadcasted_iota(jnp.int32, (rows, width), 1)
    before, after = jnp.maximum(my_col - 1, 0), jnp.minimum(my_col + 1, col_count - 1)

    def ahead(array, axis):
        return pltpu.roll(array, array.shape[axis] - 1, axis)

    def behind(array, axis):
        return pltpu.roll(array, 1, axis)

    def face(one, other):
        return 2.0 * one * other / jnp.maximum(one + other, TINY)

    cell_k, heat, field = [], [], []
    for z in range(zlayers):
        inverse = jnp.zeros((rows, width), F32)
        total = jnp.zeros((rows, width), F32)
        for m in range(M):
            c, p = divmod(z * M + m, pairs)
            share = got_ref[c, p]
            shares_ref[z * M + m] = share[0:height, 0:breadth]
            inside = jnp.where((lane < breadth + RIM) | (lane >= width - RIM), share, 0.0)
            inverse = inverse + inside * table_ref[m]
            total = total + inside * table_ref[M + m]
        cell_k.append(jnp.where(inverse > 0.0, 1.0 / jnp.where(inverse > 0.0, inverse, 1.0), 0.0))
        heat.append(total)
        left, right = got_ref[before, z], got_ref[after, z]
        left = pltpu.roll(left, width - (breadth + 2 * RIM), 1)
        right = pltpu.roll(right, width - RIM, 1)
        value = ext_ref[z]
        value = jnp.where(
            (lane >= breadth) & (lane < breadth + RIM) & (my_col < col_count - 1), right, value
        )
        value = jnp.where((lane >= width - RIM) & (my_col > 0), left, value)
        field.append(value)
    face_x = [face(k, ahead(k, 1)) for k in cell_k]
    face_y = [face(k, ahead(k, 0)) for k in cell_k]
    face_z = [face(cell_k[z], cell_k[z + 1]) for z in range(zlayers - 1)]

    def operate(w):
        result = []
        for z in range(zlayers):
            flow_x = face_x[z] * (w[z] - ahead(w[z], 1))
            flow_y = face_y[z] * (w[z] - ahead(w[z], 0))
            value = heat[z] * w[z] + (flow_x - behind(flow_x, 1)) + (flow_y - behind(flow_y, 0))
            if z + 1 < zlayers:
                value = value + face_z[z] * (w[z] - w[z + 1])
            if z:
                value = value - face_z[z - 1] * (w[z - 1] - w[z])
            result.append(value)
        return result

    shift, scale = table_ref[2 * M], table_ref[2 * M + 1]

    def shifted(w):
        return [(a - shift * b) * scale for a, b in zip(operate(w), w)]

    basis = [field, shifted(field)]
    for _ in range(ITERS - 1):
        basis.append([2.0 * a - b for a, b in zip(shifted(basis[-1]), basis[-2])])
    own = [
        [jnp.where(lane < breadth, layer, 0.0)[0:height] for layer in vector] for vector in basis
    ]
    for n in range(ITERS):
        for z in range(zlayers):
            basis_ref[n, z] = own[n + 1][z][:, 0:breadth]
    slot = lax.broadcasted_iota(jnp.int32, (1, LANES), 1)
    packed = jnp.zeros((1, LANES), F32)
    at = 0
    for a in range(ITERS + 1):
        for b in range(a, ITERS + 1):
            product = own[a][0] * own[b][0]
            for z in range(1, zlayers):
                product = product + own[a][z] * own[b][z]
            value = jnp.sum(product, axis=0, keepdims=True)
            value = jnp.sum(value, axis=1, keepdims=True)
            packed = packed + jnp.where(slot == at, value, 0.0)
            at += 1
    sums_ref[...] = jnp.broadcast_to(packed[None], sums_ref.shape)


def finish_kernel(table_ref, sums_ref, field_ref, basis_ref, iterate_ref, defect_ref):
    total = jnp.sum(sums_ref[...], axis=0)
    gram = {}
    at = 0
    for a in range(ITERS + 1):
        for b in range(a, ITERS + 1):
            gram[a, b] = gram[b, a] = total[:, at : at + 1]
            at += 1
    shift, scale = table_ref[2 * M], table_ref[2 * M + 2]

    def inner(left, right):
        value = None
        for a, one in left.items():
            for b, other in right.items():
                term = one * other * gram[a, b]
                value = term if value is None else value + term
        return value

    def combine(left, factor, right):
        result = dict(left)
        for a, one in right.items():
            result[a] = result[a] + factor * one if a in result else factor * one
        return result

    def apply(vector):
        result = {}
        for a, one in vector.items():
            if a:
                moved = {a - 1: 0.5 * scale * one, a: shift * one, a + 1: 0.5 * scale * one}
            else:
                moved = {0: shift * one, 1: scale * one}
            for b, other in moved.items():
                result[b] = result[b] + other if b in result else other
        return result

    one = jnp.ones((1, 1), F32)
    iterate, defect, direction = {}, {0: one}, {0: one}
    norm = gram[0, 0]
    for iteration in range(ITERS):
        applied = apply(direction)
        step = norm / inner(direction, applied)
        iterate = combine(iterate, step, direction)
        defect = combine(defect, -step, applied)
        if iteration + 1 < ITERS:
            following = inner(defect, defect)
            direction = combine(defect, following / norm, direction)
            norm = following
    for z in range(field_ref.shape[0]):
        vectors = [field_ref[z]] + [basis_ref[n, z] for n in range(ITERS)]
        iterate_ref[z] = sum(weight * vectors[a] for a, weight in iterate.items())
        defect_ref[z] = sum(weight * vectors[a] for a, weight in defect.items())


def per_device(
    row_count,
    col_count,
    fractions_source,
    x_source_edges,
    x_target_edges,
    y_source_edges,
    y_target_edges,
    conductivity_table,
    capacity,
    thermal_source_term,
):
    pairs, _, source_cells = fractions_source.shape
    zlayers, height, breadth = thermal_source_term.shape
    width = LANES * tiles(breadth + 4 * RIM)
    send_rows = ROWS + 8 + 8 * tiles(breadth)
    params = pltpu.CompilerParams(vmem_limit_bytes=VMEM)

    resistance = 16.0 / conductivity_table.astype(F32)
    middle = 5.0 * M / jnp.sum(resistance)
    table = jnp.concatenate(
        [
            resistance,
            capacity,
            jnp.stack([jnp.mean(capacity) + middle, 1.0 / middle, middle]),
        ]
    )

    smem = pl.BlockSpec(memory_space=pltpu.SMEM)
    vmem = pl.BlockSpec(memory_space=pltpu.VMEM)
    hbm = pl.BlockSpec(memory_space=pltpu.HBM)
    along_rows = -(-pairs * TBLK // LANES) * LANES
    edges = [x_source_edges, x_target_edges, y_source_edges, y_target_edges]
    outgoing = pl.pallas_call(
        functools.partial(rezone_kernel, row_count),
        out_shape=jax.ShapeDtypeStruct((row_count, send_rows, LANES), F32),
        in_specs=[hbm] * 6,
        out_specs=vmem,
        scratch_shapes=[pltpu.VMEM(e.shape, e.dtype) for e in edges]
        + [
            pltpu.VMEM(fractions_source.shape, F32),
            pltpu.VMEM(thermal_source_term.shape, F32),
            pltpu.VMEM((8, LANES * (tiles(source_cells + 1) + 1)), F32),
            pltpu.VMEM((along_rows, source_cells), F32),
            pltpu.SemaphoreType.DMA((5 + pairs,)),
        ],
        compiler_params=pltpu.CompilerParams(vmem_limit_bytes=FULL),
        name="rezone",
    )(*edges, fractions_source, thermal_source_term)
    arrived = lax.all_to_all(outgoing, "row", split_axis=0, concat_axis=0, tiled=True)
    message = jax.ShapeDtypeStruct((pairs, ROWS, width), F32)
    extended, *parts = pl.pallas_call(
        functools.partial(regroup_kernel, row_count, col_count),
        out_shape=[jax.ShapeDtypeStruct((zlayers, ROWS, width), F32)] + [message] * col_count,
        in_specs=[vmem] * 2,
        out_specs=[vmem] * (1 + col_count),
        compiler_params=params,
        name="regroup",
    )(arrived, thermal_source_term)
    parts = [parts[0]] + [
        lax.ppermute(parts[mask], "col", [(c, c ^ mask) for c in range(col_count)])
        for mask in range(1, col_count)
    ]
    rezoned_occupancy_shares, basis, sums = pl.pallas_call(
        functools.partial(basis_kernel, col_count, height, breadth),
        out_shape=[
            jax.ShapeDtypeStruct((zlayers * M, height, breadth), F32),
            jax.ShapeDtypeStruct((ITERS, zlayers, height, breadth), F32),
            jax.ShapeDtypeStruct((row_count * col_count, 1, LANES), F32),
        ],
        in_specs=[smem] + [vmem] * (1 + col_count),
        out_specs=[vmem] * 3,
        scratch_shapes=[pltpu.VMEM((col_count, *message.shape), F32)],
        compiler_params=params,
        name="basis",
    )(table, extended, *parts)
    sums = lax.all_to_all(sums, ("row", "col"), split_axis=0, concat_axis=0, tiled=True)
    thermal_iterate, remaining_defect = pl.pallas_call(
        finish_kernel,
        out_shape=[jax.ShapeDtypeStruct((zlayers, height, breadth), F32)] * 2,
        in_specs=[smem, vmem, vmem, vmem],
        out_specs=[vmem] * 2,
        compiler_params=params,
        name="finish",
    )(table, sums, thermal_source_term, basis)
    return rezoned_occupancy_shares, thermal_iterate, remaining_defect


def solution(mesh):
    placed = (P("col", "row", None), P(), P(), P(), P(), P(), P(), P(None, "row", "col"))
    return jax.shard_map(
        functools.partial(per_device, mesh.shape["row"], mesh.shape["col"]),
        mesh=mesh,
        in_specs=placed,
        out_specs=(P(None, "row", "col"), P(None, "row", "col"), P(None, "row", "col")),
        check_vma=False,
    )
```

```python
import functools

import jax
import jax.numpy as jnp
from jax import lax
from jax.experimental import pallas as pl
from jax.experimental.pallas import tpu as pltpu
from jax.sharding import PartitionSpec as P

M = 6
SBLK = 64
TBLK = 48
ITERS = 3
RIM = ITERS
ROWS = 56
LANES = 128
GROUPS = ROWS // 8
TAIL = LANES // GROUPS // 8 * 8
VMEM = 48 * 1024 * 1024
FULL = 63 * 1024 * 1024
TINY = 1e-30
F32 = jnp.float32
EXACT = lax.Precision.HIGHEST


def tiles(cells):
    return -(-cells // LANES)


def window_rows(row_count):
    count = row_count // 2 - 1
    rows = [[2 * q + 1, 2 * q + 2] for q in range(count)]
    rows[0] = [0] + rows[0]
    rows[-1] = rows[-1] + [row_count - 1]
    return rows


def rezone_kernel(
    row_count,
    xs_hbm,
    xt_hbm,
    ys_hbm,
    yt_hbm,
    frac_hbm,
    field_hbm,
    out_hbm,
    xs_ref,
    xt_ref,
    ys_ref,
    yt_ref,
    frac_ref,
    field_ref,
    edges_ref,
    along_ref,
    out_ref,
    sems,
    out_sems,
):
    me = lax.axis_index("row")
    pairs = frac_ref.shape[0]
    moves = [
        pltpu.make_async_copy(here, there, sems.at[n])
        for n, (here, there) in enumerate(
            (
                (yt_hbm, yt_ref),
                (xt_hbm, xt_ref),
                (xs_hbm, xs_ref),
                (ys_hbm, ys_ref),
                (frac_hbm, frac_ref),
                (field_hbm, field_ref),
            )
        )
    ]
    for move in moves:
        move.start()
    edges_ref[...] = jnp.zeros_like(edges_ref)
    along_ref[pairs * TBLK :, :] = jnp.zeros_like(along_ref[pairs * TBLK :, :])
    for n, ref in enumerate((yt_ref, xt_ref, xs_ref, ys_ref)):
        moves[n].wait()
        edges_ref[n : n + 1, 0 : ref.shape[0]] = ref[...].astype(F32)[None, :]

    def from_here(row, start, lane):
        base = start // LANES * LANES
        if not isinstance(base, int):
            base = pl.multiple_of(base, LANES)
        window = edges_ref[row : row + 1, pl.ds(base, 2 * LANES)]
        return pltpu.roll(window, (lane - (start - base) + 2 * LANES) % (2 * LANES), 1)

    starts = [from_here(0, max(r * TBLK - RIM, 0), 0 if r else RIM) for r in range(row_count)]
    starts.append(from_here(1, me * TBLK, 0))
    spare = jnp.zeros((-len(starts) % 8, LANES), F32)
    columns = jnp.concatenate([start[:, 0:LANES] for start in starts] + [spare], axis=0)
    columns = jnp.transpose(columns)[0 : ROWS + 8]
    ends = pltpu.roll(columns, ROWS + 7, 0)
    row = lax.broadcasted_iota(jnp.int32, (ROWS, columns.shape[1]), 0)
    block = lax.broadcasted_iota(jnp.int32, (ROWS, columns.shape[1]), 1)
    inside = (row < jnp.where(block == row_count - 1, TBLK, TBLK + RIM)) | (
        (row >= ROWS - RIM) & (block > 0)
    )
    tgt_lo = jnp.where(inside, pltpu.roll(columns[0:ROWS], ROWS - RIM, 0), 0.0)
    tgt_hi = jnp.where(inside, pltpu.roll(ends[0:ROWS], ROWS - RIM, 0), 0.0)
    inverse = 1.0 / jnp.maximum(tgt_hi - tgt_lo, 1.0)

    def weights(src_lo, src_hi, low, high, scale):
        shared = jnp.maximum(jnp.minimum(src_hi, high) - jnp.maximum(src_lo, low), 0.0)
        return shared * scale

    mine = slice(row_count, row_count + 1)
    x_lo = from_here(2, me * SBLK, 0)
    x_hi = pltpu.roll(x_lo, 2 * LANES - 1, 1)
    x_tgt_lo, x_tgt_hi = columns[0:TBLK, mine], ends[0:TBLK, mine]
    weight_x = weights(
        x_lo[:, 0:SBLK], x_hi[:, 0:SBLK], x_tgt_lo, x_tgt_hi, 1.0 / (x_tgt_hi - x_tgt_lo)
    )
    width = 4 * SBLK
    weights_y = []
    for q, rows in enumerate(window_rows(row_count)):
        src_lo = edges_ref[3:4, 2 * q * SBLK : 2 * q * SBLK + width]
        src_hi = edges_ref[3:4, 2 * q * SBLK + 1 : 2 * q * SBLK + width + 1]
        weights_y.append(
            jnp.concatenate(
                [
                    weights(src_lo, src_hi, *(a[:, r : r + 1] for a in (tgt_lo, tgt_hi, inverse)))
                    for r in rows
                ],
                axis=0,
            )
        )
    moves[5].wait()
    zlayers, height, breadth = field_ref.shape
    base = ROWS + 8
    for r in range(row_count):
        for t in range(tiles(breadth)):
            lo, hi = t * LANES, min((t + 1) * LANES, breadth)
            for layer in range(zlayers):
                rim = jnp.where(
                    r > me,
                    field_ref[layer, height - RIM :, lo:hi],
                    field_ref[layer, :RIM, lo:hi],
                )
                at = base + 8 * t + RIM * layer
                out_ref[r, at : at + RIM, 0 : hi - lo] = rim
    moves[4].wait()
    for p in range(pairs):
        along_ref[p * TBLK : (p + 1) * TBLK, :] = jnp.dot(
            weight_x, frac_ref[p], precision=EXACT, preferred_element_type=F32
        )
    leaving = []
    for q, rows in enumerate(window_rows(row_count)):
        block = lax.dot_general(
            weights_y[q],
            along_ref[:, 2 * q * SBLK : 2 * q * SBLK + width],
            (((1,), (1,)), ((), ())),
            precision=EXACT,
            preferred_element_type=F32,
        )
        for n, r in enumerate(rows):
            mine = block[n * ROWS : (n + 1) * ROWS]
            out_ref[r, 0:ROWS, :] = mine[:, 0:LANES]
            packed = mine[0:8, LANES:]
            for g in range(1, GROUPS):
                packed = packed + pltpu.roll(mine[8 * g : 8 * g + 8, LANES:], TAIL * g, 1)
            out_ref[r, ROWS : ROWS + 8, :] = packed
            leaving.append(pltpu.make_async_copy(out_ref.at[r], out_hbm.at[r], out_sems.at[r]))
            leaving[-1].start()
    for move in leaving:
        move.wait()


def table_kernel(cond_ref, heat_ref, table_ref):
    resistance = 16.0 / cond_ref[...].astype(F32)[None, :]
    heat = heat_ref[...][None, :]
    middle = 5.0 * M / jnp.sum(resistance, axis=1, keepdims=True)
    shift = jnp.sum(heat, axis=1, keepdims=True) / M + middle
    rest = jnp.zeros((1, LANES - 2 * M - 3), F32)
    table = jnp.concatenate([resistance, heat, shift, 1.0 / middle, middle, rest], axis=1)
    table = jnp.transpose(jnp.broadcast_to(table, (LANES, LANES)))
    table_ref[...] = table[0 : table_ref.shape[0]]


def regroup_kernel(row_count, col_count, got_ref, field_ref, ext_ref, *out_refs):
    my_row, my_col = lax.axis_index("row"), lax.axis_index("col")
    zlayers, height, breadth = field_ref.shape
    pairs, _, width = out_refs[0].shape
    per_col = row_count // col_count
    base = ROWS + 8
    ext_ref[...] = jnp.zeros_like(ext_ref)
    below, above = jnp.maximum(my_row - 1, 0), jnp.minimum(my_row + 1, row_count - 1)
    for layer in range(zlayers):
        ext_ref[layer, 0:height, 0:breadth] = field_ref[layer]
        for t in range(tiles(breadth)):
            lo, hi = t * LANES, min((t + 1) * LANES, breadth)
            at = base + 8 * t + RIM * layer
            after = got_ref[above, at : at + RIM, 0 : hi - lo]
            before = got_ref[below, at : at + RIM, 0 : hi - lo]
            ext_ref[layer, height : height + RIM, lo:hi] = jnp.where(
                my_row < row_count - 1, after, 0.0
            )
            ext_ref[layer, ROWS - RIM : ROWS, lo:hi] = jnp.where(my_row > 0, before, 0.0)

    def piece(block, pair, first, last):
        start = pair * TBLK
        lo, hi = start + first, start + last
        parts = []
        if lo < LANES:
            parts.append(got_ref[block, 0:ROWS, lo : min(hi, LANES)])
        if hi > LANES:
            a, b = max(lo, LANES) - LANES, hi - LANES
            tail = got_ref[block, ROWS : ROWS + 8, :]
            parts.append(
                jnp.concatenate([tail[:, TAIL * g + a : TAIL * g + b] for g in range(GROUPS)], axis=0)
            )
        return parts[0] if len(parts) == 1 else jnp.concatenate(parts, axis=1)

    for mask, out_ref in enumerate(out_refs):
        c = my_col ^ mask
        first = c * per_col
        left, right = jnp.maximum(first - 1, 0), jnp.minimum(first + per_col, row_count - 1)
        for p in range(pairs):
            parts = [piece(first + j, p, 0, TBLK) for j in range(per_col)]
            parts.append(jnp.where(c < col_count - 1, piece(right, p, 0, RIM), 0.0))
            if p < zlayers and mask:
                whole = ext_ref[p]
                parts.append(
                    jnp.where(c > my_col, whole[:, breadth - RIM : breadth], whole[:, 0:RIM])
                )
            else:
                parts.append(jnp.zeros((ROWS, RIM), F32))
            parts.append(jnp.zeros((ROWS, width - breadth - 3 * RIM), F32))
            parts.append(jnp.where(c > 0, piece(left, p, TBLK - RIM, TBLK), 0.0))
            out_ref[p] = jnp.concatenate(parts, axis=1)


def basis_kernel(col_count, height, breadth, table_ref, ext_ref, *refs):
    arrivals, refs = refs[:col_count], refs[col_count:]
    shares_hbm, basis_ref, sums_ref, got_ref, shares_ref, sem = refs
    my_col = lax.axis_index("col")
    for mask, arrival in enumerate(arrivals):
        got_ref[my_col ^ mask] = arrival[...]
        for p in range(arrival.shape[0]):
            at = (my_col ^ mask) * arrival.shape[0] + p
            shares_ref[at] = arrival[p, 0:height, 0:breadth]
    leaving = pltpu.make_async_copy(shares_ref, shares_hbm, sem)
    leaving.start()
    zlayers = ext_ref.shape[0]
    pairs, rows, width = got_ref.shape[1:]
    lane = lax.broadcasted_iota(jnp.int32, (rows, width), 1)
    before, after = jnp.maximum(my_col - 1, 0), jnp.minimum(my_col + 1, col_count - 1)

    def ahead(array, axis):
        return pltpu.roll(array, array.shape[axis] - 1, axis)

    def behind(array, axis):
        return pltpu.roll(array, 1, axis)

    def face(one, other):
        return 2.0 * one * other / jnp.maximum(one + other, TINY)

    def entry(n):
        return table_ref[n : n + 1, 0:1]

    cell_k, heat, field = [], [], []
    for z in range(zlayers):
        inverse = jnp.zeros((rows, width), F32)
        total = jnp.zeros((rows, width), F32)
        for m in range(M):
            c, p = divmod(z * M + m, pairs)
            share = got_ref[c, p]
            inside = jnp.where((lane < breadth + RIM) | (lane >= width - RIM), share, 0.0)
            inverse = inverse + inside * entry(m)
            total = total + inside * entry(M + m)
        cell_k.append(jnp.where(inverse > 0.0, 1.0 / jnp.where(inverse > 0.0, inverse, 1.0), 0.0))
        heat.append(total)
        left, right = got_ref[before, z], got_ref[after, z]
        left = pltpu.roll(left, width - (breadth + 2 * RIM), 1)
        right = pltpu.roll(right, width - RIM, 1)
        value = ext_ref[z]
        value = jnp.where(
            (lane >= breadth) & (lane < breadth + RIM) & (my_col < col_count - 1), right, value
        )
        value = jnp.where((lane >= width - RIM) & (my_col > 0), left, value)
        field.append(value)
    face_x = [face(k, ahead(k, 1)) for k in cell_k]
    face_y = [face(k, ahead(k, 0)) for k in cell_k]
    face_z = [face(cell_k[z], cell_k[z + 1]) for z in range(zlayers - 1)]

    def operate(w):
        result = []
        for z in range(zlayers):
            flow_x = face_x[z] * (w[z] - ahead(w[z], 1))
            flow_y = face_y[z] * (w[z] - ahead(w[z], 0))
            value = heat[z] * w[z] + (flow_x - behind(flow_x, 1)) + (flow_y - behind(flow_y, 0))
            if z + 1 < zlayers:
                value = value + face_z[z] * (w[z] - w[z + 1])
            if z:
                value = value - face_z[z - 1] * (w[z - 1] - w[z])
            result.append(value)
        return result

    shift, scale = entry(2 * M), entry(2 * M + 1)

    def shifted(w):
        return [(a - shift * b) * scale for a, b in zip(operate(w), w)]

    basis = [field, shifted(field)]
    for _ in range(ITERS - 1):
        basis.append([2.0 * a - b for a, b in zip(shifted(basis[-1]), basis[-2])])
    own = [
        [jnp.where(lane < breadth, layer, 0.0)[0:height] for layer in vector] for vector in basis
    ]
    for n in range(ITERS):
        for z in range(zlayers):
            basis_ref[n, z] = own[n + 1][z][:, 0:breadth]
    slot = lax.broadcasted_iota(jnp.int32, (1, LANES), 1)
    packed = jnp.zeros((1, LANES), F32)
    at = 0
    for a in range(ITERS + 1):
        for b in range(a, ITERS + 1):
            product = own[a][0] * own[b][0]
            for z in range(1, zlayers):
                product = product + own[a][z] * own[b][z]
            value = jnp.sum(product, axis=0, keepdims=True)
            value = jnp.sum(value, axis=1, keepdims=True)
            packed = packed + jnp.where(slot == at, value, 0.0)
            at += 1
    sums_ref[...] = jnp.broadcast_to(packed[None], sums_ref.shape)
    leaving.wait()


def finish_kernel(table_ref, sums_ref, field_ref, basis_ref, iterate_ref, defect_ref):
    total = jnp.sum(sums_ref[...], axis=0)
    gram = {}
    at = 0
    for a in range(ITERS + 1):
        for b in range(a, ITERS + 1):
            gram[a, b] = gram[b, a] = total[:, at : at + 1]
            at += 1
    shift, scale = (table_ref[n : n + 1, 0:1] for n in (2 * M, 2 * M + 2))

    def inner(left, right):
        rows = []
        for a, one in left.items():
            rows.append(one * total_of([other * gram[a, b] for b, other in right.items()]))
        return total_of(rows)

    def total_of(terms):
        while len(terms) > 1:
            terms = [sum(terms[n : n + 2][1:], terms[n]) for n in range(0, len(terms), 2)]
        return terms[0]

    def combine(left, factor, right):
        result = dict(left)
        for a, one in right.items():
            result[a] = result[a] + factor * one if a in result else factor * one
        return result

    def apply(vector):
        result = {}
        for a, one in vector.items():
            if a:
                moved = {a - 1: 0.5 * scale * one, a: shift * one, a + 1: 0.5 * scale * one}
            else:
                moved = {0: shift * one, 1: scale * one}
            for b, other in moved.items():
                result[b] = result[b] + other if b in result else other
        return result

    one = jnp.ones((1, 1), F32)
    iterate, defect, direction = {}, {0: one}, {0: one}
    norm = gram[0, 0]
    for iteration in range(ITERS):
        applied = apply(direction)
        step = norm / inner(direction, applied)
        iterate = combine(iterate, step, direction)
        defect = combine(defect, -step, applied)
        if iteration + 1 < ITERS:
            following = inner(defect, defect)
            direction = combine(defect, following / norm, direction)
            norm = following
    for z in range(field_ref.shape[0]):
        vectors = [field_ref[z]] + [basis_ref[n, z] for n in range(ITERS)]
        iterate_ref[z] = sum(weight * vectors[a] for a, weight in iterate.items())
        defect_ref[z] = sum(weight * vectors[a] for a, weight in defect.items())


def per_device(
    row_count,
    col_count,
    fractions_source,
    x_source_edges,
    x_target_edges,
    y_source_edges,
    y_target_edges,
    conductivity_table,
    capacity,
    thermal_source_term,
):
    pairs, _, source_cells = fractions_source.shape
    zlayers, height, breadth = thermal_source_term.shape
    width = LANES * tiles(breadth + 4 * RIM)
    send_rows = ROWS + 8 + 8 * tiles(breadth)
    params = pltpu.CompilerParams(vmem_limit_bytes=VMEM)

    vmem = pl.BlockSpec(memory_space=pltpu.VMEM)
    hbm = pl.BlockSpec(memory_space=pltpu.HBM)
    along_rows = -(-pairs * TBLK // LANES) * LANES
    edges = [x_source_edges, x_target_edges, y_source_edges, y_target_edges]
    outgoing = jax.ShapeDtypeStruct((row_count, send_rows, LANES), F32)
    outgoing = pl.pallas_call(
        functools.partial(rezone_kernel, row_count),
        out_shape=outgoing,
        in_specs=[hbm] * 6,
        out_specs=hbm,
        scratch_shapes=[pltpu.VMEM(e.shape, e.dtype) for e in edges]
        + [
            pltpu.VMEM(fractions_source.shape, F32),
            pltpu.VMEM(thermal_source_term.shape, F32),
            pltpu.VMEM((8, LANES * (tiles(source_cells + 1) + 1)), F32),
            pltpu.VMEM((along_rows, source_cells), F32),
            pltpu.VMEM(outgoing.shape, F32),
            pltpu.SemaphoreType.DMA((6,)),
            pltpu.SemaphoreType.DMA((row_count,)),
        ],
        compiler_params=pltpu.CompilerParams(vmem_limit_bytes=FULL),
        name="rezone",
    )(*edges, fractions_source, thermal_source_term)
    arrived = lax.all_to_all(outgoing, "row", split_axis=0, concat_axis=0, tiled=True)
    table = pl.pallas_call(
        table_kernel,
        out_shape=jax.ShapeDtypeStruct((-(-(2 * M + 3) // 8) * 8, LANES), F32),
        in_specs=[vmem] * 2,
        out_specs=vmem,
        compiler_params=params,
        name="table",
    )(conductivity_table, capacity)
    message = jax.ShapeDtypeStruct((pairs, ROWS, width), F32)
    extended, *parts = pl.pallas_call(
        functools.partial(regroup_kernel, row_count, col_count),
        out_shape=[jax.ShapeDtypeStruct((zlayers, ROWS, width), F32)] + [message] * col_count,
        in_specs=[vmem] * 2,
        out_specs=[vmem] * (1 + col_count),
        compiler_params=params,
        name="regroup",
    )(arrived, thermal_source_term)
    parts = [parts[0]] + [
        lax.ppermute(parts[mask], "col", [(c, c ^ mask) for c in range(col_count)])
        for mask in range(1, col_count)
    ]
    rezoned_occupancy_shares, basis, sums = pl.pallas_call(
        functools.partial(basis_kernel, col_count, height, breadth),
        out_shape=[
            jax.ShapeDtypeStruct((zlayers * M, height, breadth), F32),
            jax.ShapeDtypeStruct((ITERS, zlayers, height, breadth), F32),
            jax.ShapeDtypeStruct((row_count * col_count, 1, LANES), F32),
        ],
        in_specs=[vmem] * (2 + col_count),
        out_specs=[hbm, vmem, vmem],
        scratch_shapes=[
            pltpu.VMEM((col_count, *message.shape), F32),
            pltpu.VMEM((zlayers * M, height, breadth), F32),
            pltpu.SemaphoreType.DMA,
        ],
        compiler_params=params,
        name="basis",
    )(table, extended, *parts)
    sums = lax.all_to_all(sums, ("row", "col"), split_axis=0, concat_axis=0, tiled=True)
    thermal_iterate, remaining_defect = pl.pallas_call(
        finish_kernel,
        out_shape=[jax.ShapeDtypeStruct((zlayers, height, breadth), F32)] * 2,
        in_specs=[vmem] * 4,
        out_specs=[vmem] * 2,
        compiler_params=params,
        name="finish",
    )(table, sums, thermal_source_term, basis)
    return rezoned_occupancy_shares, thermal_iterate, remaining_defect


def solution(mesh):
    placed = (P("col", "row", None), P(), P(), P(), P(), P(), P(), P(None, "row", "col"))
    return jax.shard_map(
        functools.partial(per_device, mesh.shape["row"], mesh.shape["col"]),
        mesh=mesh,
        in_specs=placed,
        out_specs=(P(None, "row", "col"), P(None, "row", "col"), P(None, "row", "col")),
        check_vma=False,
    )
```

```python
import functools

import jax
import jax.numpy as jnp
from jax import lax
from jax.experimental import pallas as pl
from jax.experimental.pallas import tpu as pltpu
from jax.sharding import PartitionSpec as P

M = 6
SBLK = 64
TBLK = 48
ITERS = 3
RIM = ITERS
ROWS = 56
LANES = 128
GROUPS = ROWS // 8
TAIL = LANES // GROUPS // 8 * 8
VMEM = 48 * 1024 * 1024
FULL = 63 * 1024 * 1024
TINY = 1e-30
F32 = jnp.float32
EXACT = lax.Precision.HIGHEST


def tiles(cells):
    return -(-cells // LANES)


def window_rows(row_count):
    count = row_count // 2 - 1
    rows = [[2 * q + 1, 2 * q + 2] for q in range(count)]
    rows[0] = [0] + rows[0]
    rows[-1] = rows[-1] + [row_count - 1]
    return rows


def rezone_kernel(
    row_count,
    xs_hbm,
    xt_hbm,
    ys_hbm,
    yt_hbm,
    frac_hbm,
    field_hbm,
    out_hbm,
    xs_ref,
    xt_ref,
    ys_ref,
    yt_ref,
    frac_ref,
    field_ref,
    edges_ref,
    along_ref,
    out_ref,
    sems,
    out_sems,
):
    me = lax.axis_index("row")
    pairs = frac_ref.shape[0]
    moves = [
        pltpu.make_async_copy(here, there, sems.at[n])
        for n, (here, there) in enumerate(
            (
                (yt_hbm, yt_ref),
                (xt_hbm, xt_ref),
                (xs_hbm, xs_ref),
                (ys_hbm, ys_ref),
                (frac_hbm, frac_ref),
                (field_hbm, field_ref),
            )
        )
    ]
    for move in moves:
        move.start()
    edges_ref[...] = jnp.zeros_like(edges_ref)
    along_ref[pairs * TBLK :, :] = jnp.zeros_like(along_ref[pairs * TBLK :, :])
    for n, ref in enumerate((yt_ref, xt_ref, xs_ref, ys_ref)):
        moves[n].wait()
        edges_ref[n : n + 1, 0 : ref.shape[0]] = ref[...].astype(F32)[None, :]

    def from_here(row, start, lane):
        base = start // LANES * LANES
        if not isinstance(base, int):
            base = pl.multiple_of(base, LANES)
        window = edges_ref[row : row + 1, pl.ds(base, 2 * LANES)]
        return pltpu.roll(window, (lane - (start - base) + 2 * LANES) % (2 * LANES), 1)

    starts = [from_here(0, max(r * TBLK - RIM, 0), 0 if r else RIM) for r in range(row_count)]
    starts.append(from_here(1, me * TBLK, 0))
    spare = jnp.zeros((-len(starts) % 8, LANES), F32)
    columns = jnp.concatenate([start[:, 0:LANES] for start in starts] + [spare], axis=0)
    columns = jnp.transpose(columns)[0 : ROWS + 8]
    ends = pltpu.roll(columns, ROWS + 7, 0)
    row = lax.broadcasted_iota(jnp.int32, (ROWS, columns.shape[1]), 0)
    block = lax.broadcasted_iota(jnp.int32, (ROWS, columns.shape[1]), 1)
    inside = (row < jnp.where(block == row_count - 1, TBLK, TBLK + RIM)) | (
        (row >= ROWS - RIM) & (block > 0)
    )
    tgt_lo = jnp.where(inside, pltpu.roll(columns[0:ROWS], ROWS - RIM, 0), 0.0)
    tgt_hi = jnp.where(inside, pltpu.roll(ends[0:ROWS], ROWS - RIM, 0), 0.0)
    inverse = 1.0 / jnp.maximum(tgt_hi - tgt_lo, 1.0)

    def weights(src_lo, src_hi, low, high, scale):
        shared = jnp.maximum(jnp.minimum(src_hi, high) - jnp.maximum(src_lo, low), 0.0)
        return shared * scale

    mine = slice(row_count, row_count + 1)
    x_lo = from_here(2, me * SBLK, 0)
    x_hi = pltpu.roll(x_lo, 2 * LANES - 1, 1)
    x_tgt_lo, x_tgt_hi = columns[0:TBLK, mine], ends[0:TBLK, mine]
    weight_x = weights(
        x_lo[:, 0:SBLK], x_hi[:, 0:SBLK], x_tgt_lo, x_tgt_hi, 1.0 / (x_tgt_hi - x_tgt_lo)
    )
    moves[4].wait()
    for p in range(pairs):
        along_ref[p * TBLK : (p + 1) * TBLK, :] = jnp.dot(
            weight_x, frac_ref[p], precision=EXACT, preferred_element_type=F32
        )
    width = 4 * SBLK
    weights_y = []
    for q, rows in enumerate(window_rows(row_count)):
        src_lo = edges_ref[3:4, 2 * q * SBLK : 2 * q * SBLK + width]
        src_hi = edges_ref[3:4, 2 * q * SBLK + 1 : 2 * q * SBLK + width + 1]
        weights_y.append(
            jnp.concatenate(
                [
                    weights(src_lo, src_hi, *(a[:, r : r + 1] for a in (tgt_lo, tgt_hi, inverse)))
                    for r in rows
                ],
                axis=0,
            )
        )
    moves[5].wait()
    zlayers, height, breadth = field_ref.shape
    base = ROWS + 8
    for r in range(row_count):
        for t in range(tiles(breadth)):
            lo, hi = t * LANES, min((t + 1) * LANES, breadth)
            for layer in range(zlayers):
                rim = jnp.where(
                    r > me,
                    field_ref[layer, height - RIM :, lo:hi],
                    field_ref[layer, :RIM, lo:hi],
                )
                at = base + 8 * t + RIM * layer
                out_ref[r, at : at + RIM, 0 : hi - lo] = rim
    leaving = []
    for q, rows in enumerate(window_rows(row_count)):
        block = lax.dot_general(
            weights_y[q],
            along_ref[:, 2 * q * SBLK : 2 * q * SBLK + width],
            (((1,), (1,)), ((), ())),
            precision=EXACT,
            preferred_element_type=F32,
        )
        for n, r in enumerate(rows):
            mine = block[n * ROWS : (n + 1) * ROWS]
            out_ref[r, 0:ROWS, :] = mine[:, 0:LANES]
            packed = mine[0:8, LANES:]
            for g in range(1, GROUPS):
                packed = packed + pltpu.roll(mine[8 * g : 8 * g + 8, LANES:], TAIL * g, 1)
            out_ref[r, ROWS : ROWS + 8, :] = packed
        done = pl.ds(rows[0], len(rows))
        leaving.append(pltpu.make_async_copy(out_ref.at[done], out_hbm.at[done], out_sems.at[q]))
        leaving[-1].start()
    for move in leaving:
        move.wait()


def table_kernel(cond_ref, heat_ref, table_ref):
    resistance = 16.0 / cond_ref[...].astype(F32)[None, :]
    heat = heat_ref[...][None, :]
    middle = 5.0 * M / jnp.sum(resistance, axis=1, keepdims=True)
    shift = jnp.sum(heat, axis=1, keepdims=True) / M + middle
    rest = jnp.zeros((1, LANES - 2 * M - 3), F32)
    table = jnp.concatenate([resistance, heat, shift, 1.0 / middle, middle, rest], axis=1)
    table = jnp.transpose(jnp.broadcast_to(table, (LANES, LANES)))
    table_ref[...] = table[0 : table_ref.shape[0]]


def extend_rows(row_count, got_ref, field_ref, ext_ref):
    my_row = lax.axis_index("row")
    zlayers, height, breadth = field_ref.shape
    base = ROWS + 8
    ext_ref[...] = jnp.zeros_like(ext_ref)
    below, above = jnp.maximum(my_row - 1, 0), jnp.minimum(my_row + 1, row_count - 1)
    for layer in range(zlayers):
        ext_ref[layer, 0:height, 0:breadth] = field_ref[layer]
        for t in range(tiles(breadth)):
            lo, hi = t * LANES, min((t + 1) * LANES, breadth)
            at = base + 8 * t + RIM * layer
            after = got_ref[above, at : at + RIM, 0 : hi - lo]
            before = got_ref[below, at : at + RIM, 0 : hi - lo]
            ext_ref[layer, height : height + RIM, lo:hi] = jnp.where(
                my_row < row_count - 1, after, 0.0
            )
            ext_ref[layer, ROWS - RIM : ROWS, lo:hi] = jnp.where(my_row > 0, before, 0.0)


def regroup_kernel(row_count, col_count, masks, got_ref, field_ref, *refs):
    my_col = lax.axis_index("col")
    zlayers, _, breadth = field_ref.shape
    ext_ref, out_refs = refs[0], refs[1:]
    pairs, _, width = out_refs[0].shape
    per_col = row_count // col_count
    if col_count // 2 in masks:
        extend_rows(row_count, got_ref, field_ref, ext_ref)

    def piece(block, pair, first, last):
        start = pair * TBLK
        lo, hi = start + first, start + last
        parts = []
        if lo < LANES:
            parts.append(got_ref[block, 0:ROWS, lo : min(hi, LANES)])
        if hi > LANES:
            a, b = max(lo, LANES) - LANES, hi - LANES
            tail = got_ref[block, ROWS : ROWS + 8, :]
            parts.append(
                jnp.concatenate([tail[:, TAIL * g + a : TAIL * g + b] for g in range(GROUPS)], axis=0)
            )
        return parts[0] if len(parts) == 1 else jnp.concatenate(parts, axis=1)

    for mask, out_ref in zip(masks, out_refs):
        c = my_col ^ mask
        first = c * per_col
        left, right = jnp.maximum(first - 1, 0), jnp.minimum(first + per_col, row_count - 1)
        for p in range(pairs):
            parts = [piece(first + j, p, 0, TBLK) for j in range(per_col)]
            parts.append(jnp.where(c < col_count - 1, piece(right, p, 0, RIM), 0.0))
            if p < zlayers and mask:
                whole = ext_ref[p]
                parts.append(
                    jnp.where(c > my_col, whole[:, breadth - RIM : breadth], whole[:, 0:RIM])
                )
            else:
                parts.append(jnp.zeros((ROWS, RIM), F32))
            parts.append(jnp.zeros((ROWS, width - breadth - 3 * RIM), F32))
            parts.append(jnp.where(c > 0, piece(left, p, TBLK - RIM, TBLK), 0.0))
            out_ref[p] = jnp.concatenate(parts, axis=1)


def basis_kernel(col_count, height, breadth, table_ref, ext_ref, *refs):
    arrivals, refs = refs[:col_count], refs[col_count:]
    shares_ref, basis_ref, sums_ref, got_ref = refs
    my_col = lax.axis_index("col")
    for mask, arrival in enumerate(arrivals):
        got_ref[my_col ^ mask] = arrival[...]
        for p in range(arrival.shape[0]):
            at = (my_col ^ mask) * arrival.shape[0] + p
            shares_ref[at] = arrival[p, 0:height, 0:breadth]
    zlayers = ext_ref.shape[0]
    pairs, rows, width = got_ref.shape[1:]
    lane = lax.broadcasted_iota(jnp.int32, (rows, width), 1)
    before, after = jnp.maximum(my_col - 1, 0), jnp.minimum(my_col + 1, col_count - 1)

    def ahead(array, axis):
        return pltpu.roll(array, array.shape[axis] - 1, axis)

    def behind(array, axis):
        return pltpu.roll(array, 1, axis)

    def face(one, other):
        return 2.0 * one * other / jnp.maximum(one + other, TINY)

    def entry(n):
        return table_ref[n : n + 1, 0:1]

    cell_k, heat, field = [], [], []
    for z in range(zlayers):
        inverse = jnp.zeros((rows, width), F32)
        total = jnp.zeros((rows, width), F32)
        for m in range(M):
            c, p = divmod(z * M + m, pairs)
            share = got_ref[c, p]
            inside = jnp.where((lane < breadth + RIM) | (lane >= width - RIM), share, 0.0)
            inverse = inverse + inside * entry(m)
            total = total + inside * entry(M + m)
        cell_k.append(jnp.where(inverse > 0.0, 1.0 / jnp.where(inverse > 0.0, inverse, 1.0), 0.0))
        heat.append(total)
        left, right = got_ref[before, z], got_ref[after, z]
        left = pltpu.roll(left, width - (breadth + 2 * RIM), 1)
        right = pltpu.roll(right, width - RIM, 1)
        value = ext_ref[z]
        value = jnp.where(
            (lane >= breadth) & (lane < breadth + RIM) & (my_col < col_count - 1), right, value
        )
        value = jnp.where((lane >= width - RIM) & (my_col > 0), left, value)
        field.append(value)
    face_x = [face(k, ahead(k, 1)) for k in cell_k]
    face_y = [face(k, ahead(k, 0)) for k in cell_k]
    face_z = [face(cell_k[z], cell_k[z + 1]) for z in range(zlayers - 1)]

    def operate(w):
        result = []
        for z in range(zlayers):
            flow_x = face_x[z] * (w[z] - ahead(w[z], 1))
            flow_y = face_y[z] * (w[z] - ahead(w[z], 0))
            value = heat[z] * w[z] + (flow_x - behind(flow_x, 1)) + (flow_y - behind(flow_y, 0))
            if z + 1 < zlayers:
                value = value + face_z[z] * (w[z] - w[z + 1])
            if z:
                value = value - face_z[z - 1] * (w[z - 1] - w[z])
            result.append(value)
        return result

    shift, scale = entry(2 * M), entry(2 * M + 1)

    def shifted(w):
        return [(a - shift * b) * scale for a, b in zip(operate(w), w)]

    basis = [field, shifted(field)]
    for _ in range(ITERS - 1):
        basis.append([2.0 * a - b for a, b in zip(shifted(basis[-1]), basis[-2])])
    own = [
        [jnp.where(lane < breadth, layer, 0.0)[0:height] for layer in vector] for vector in basis
    ]
    for n in range(ITERS):
        for z in range(zlayers):
            basis_ref[n, z] = own[n + 1][z][:, 0:breadth]
    slot = lax.broadcasted_iota(jnp.int32, (1, LANES), 1)
    packed = jnp.zeros((1, LANES), F32)
    at = 0
    for a in range(ITERS + 1):
        for b in range(a, ITERS + 1):
            product = own[a][0] * own[b][0]
            for z in range(1, zlayers):
                product = product + own[a][z] * own[b][z]
            value = jnp.sum(product, axis=0, keepdims=True)
            value = jnp.sum(value, axis=1, keepdims=True)
            packed = packed + jnp.where(slot == at, value, 0.0)
            at += 1
    sums_ref[...] = jnp.broadcast_to(packed[None], sums_ref.shape)


def finish_kernel(
    table_ref,
    sums_ref,
    field_ref,
    basis_ref,
    shares_ref,
    iterate_hbm,
    defect_hbm,
    shares_hbm,
    iterate_ref,
    defect_ref,
    sems,
):
    pairs = (shares_ref, shares_hbm), (iterate_ref, iterate_hbm), (defect_ref, defect_hbm)
    leaving = [pltpu.make_async_copy(*pair, sems.at[n]) for n, pair in enumerate(pairs)]
    leaving[0].start()
    total = jnp.sum(sums_ref[...], axis=0)
    gram = {}
    at = 0
    for a in range(ITERS + 1):
        for b in range(a, ITERS + 1):
            gram[a, b] = gram[b, a] = total[:, at : at + 1]
            at += 1
    shift, scale = (table_ref[n : n + 1, 0:1] for n in (2 * M, 2 * M + 2))

    def inner(left, right):
        rows = []
        for a, one in left.items():
            rows.append(one * total_of([other * gram[a, b] for b, other in right.items()]))
        return total_of(rows)

    def total_of(terms):
        while len(terms) > 1:
            terms = [sum(terms[n : n + 2][1:], terms[n]) for n in range(0, len(terms), 2)]
        return terms[0]

    def combine(left, factor, right):
        result = dict(left)
        for a, one in right.items():
            result[a] = result[a] + factor * one if a in result else factor * one
        return result

    def apply(vector):
        result = {}
        for a, one in vector.items():
            if a:
                moved = {a - 1: 0.5 * scale * one, a: shift * one, a + 1: 0.5 * scale * one}
            else:
                moved = {0: shift * one, 1: scale * one}
            for b, other in moved.items():
                result[b] = result[b] + other if b in result else other
        return result

    one = jnp.ones((1, 1), F32)
    iterate, defect, direction = {}, {0: one}, {0: one}
    norm = gram[0, 0]
    for iteration in range(ITERS):
        applied = apply(direction)
        step = norm / inner(direction, applied)
        iterate = combine(iterate, step, direction)
        defect = combine(defect, -step, applied)
        if iteration + 1 < ITERS:
            following = inner(defect, defect)
            direction = combine(defect, following / norm, direction)
            norm = following
    for ref, weights, move in ((iterate_ref, iterate, leaving[1]), (defect_ref, defect, leaving[2])):
        for z in range(field_ref.shape[0]):
            vectors = [field_ref[z]] + [basis_ref[n, z] for n in range(ITERS)]
            ref[z] = total_of([weight * vectors[a] for a, weight in weights.items()])
        move.start()
    for move in leaving:
        move.wait()


def per_device(
    row_count,
    col_count,
    fractions_source,
    x_source_edges,
    x_target_edges,
    y_source_edges,
    y_target_edges,
    conductivity_table,
    capacity,
    thermal_source_term,
):
    pairs, _, source_cells = fractions_source.shape
    zlayers, height, breadth = thermal_source_term.shape
    width = LANES * tiles(breadth + 4 * RIM)
    send_rows = ROWS + 8 + 8 * tiles(breadth)
    params = pltpu.CompilerParams(vmem_limit_bytes=VMEM)

    vmem = pl.BlockSpec(memory_space=pltpu.VMEM)
    hbm = pl.BlockSpec(memory_space=pltpu.HBM)
    along_rows = -(-pairs * TBLK // LANES) * LANES
    edges = [x_source_edges, x_target_edges, y_source_edges, y_target_edges]
    outgoing = jax.ShapeDtypeStruct((row_count, send_rows, LANES), F32)
    outgoing = pl.pallas_call(
        functools.partial(rezone_kernel, row_count),
        out_shape=outgoing,
        in_specs=[hbm] * 6,
        out_specs=hbm,
        scratch_shapes=[pltpu.VMEM(e.shape, e.dtype) for e in edges]
        + [
            pltpu.VMEM(fractions_source.shape, F32),
            pltpu.VMEM(thermal_source_term.shape, F32),
            pltpu.VMEM((8, LANES * (tiles(source_cells + 1) + 1)), F32),
            pltpu.VMEM((along_rows, source_cells), F32),
            pltpu.VMEM(outgoing.shape, F32),
            pltpu.SemaphoreType.DMA((6,)),
            pltpu.SemaphoreType.DMA((row_count // 2 - 1,)),
        ],
        compiler_params=pltpu.CompilerParams(vmem_limit_bytes=FULL),
        name="rezone",
    )(*edges, fractions_source, thermal_source_term)
    arrived = lax.all_to_all(outgoing, "row", split_axis=0, concat_axis=0, tiled=True)
    table = pl.pallas_call(
        table_kernel,
        out_shape=jax.ShapeDtypeStruct((-(-(2 * M + 3) // 8) * 8, LANES), F32),
        in_specs=[vmem] * 2,
        out_specs=vmem,
        compiler_params=params,
        name="table",
    )(conductivity_table, capacity)
    message = jax.ShapeDtypeStruct((pairs, ROWS, width), F32)
    half = col_count // 2
    near, far = range(half), range(half, col_count)
    extended, *far_parts = pl.pallas_call(
        functools.partial(regroup_kernel, row_count, col_count, far),
        out_shape=[jax.ShapeDtypeStruct((zlayers, ROWS, width), F32)] + [message] * half,
        in_specs=[vmem] * 2,
        out_specs=[vmem] * (1 + half),
        compiler_params=params,
        name="regroup_far",
    )(arrived, thermal_source_term)

    def swap(part, mask):
        return lax.ppermute(part, "col", [(c, c ^ mask) for c in range(col_count)])

    far_parts = [swap(part, mask) for part, mask in zip(far_parts, far)]
    near_parts = pl.pallas_call(
        functools.partial(regroup_kernel, row_count, col_count, near),
        out_shape=[message] * half,
        in_specs=[vmem] * 3,
        out_specs=[vmem] * half,
        compiler_params=params,
        cost_estimate=pl.CostEstimate(flops=10**6, bytes_accessed=2 * 10**6, transcendentals=0),
        name="regroup_near",
    )(arrived, thermal_source_term, extended)
    parts = [swap(part, mask) if mask else part for part, mask in zip(near_parts, near)] + far_parts
    shares, basis, sums = pl.pallas_call(
        functools.partial(basis_kernel, col_count, height, breadth),
        out_shape=[
            jax.ShapeDtypeStruct((zlayers * M, height, breadth), F32),
            jax.ShapeDtypeStruct((ITERS, zlayers, height, breadth), F32),
            jax.ShapeDtypeStruct((row_count * col_count, 1, LANES), F32),
        ],
        in_specs=[vmem] * (2 + col_count),
        out_specs=[vmem] * 3,
        scratch_shapes=[pltpu.VMEM((col_count, *message.shape), F32)],
        compiler_params=params,
        name="basis",
    )(table, extended, *parts)
    sums = lax.all_to_all(sums, ("row", "col"), split_axis=0, concat_axis=0, tiled=True)
    thermal_iterate, remaining_defect, rezoned_occupancy_shares = pl.pallas_call(
        finish_kernel,
        out_shape=[jax.ShapeDtypeStruct((zlayers, height, breadth), F32)] * 2
        + [jax.ShapeDtypeStruct(shares.shape, F32)],
        in_specs=[vmem] * 5,
        out_specs=[hbm] * 3,
        scratch_shapes=[pltpu.VMEM((zlayers, height, breadth), F32)] * 2
        + [pltpu.SemaphoreType.DMA((3,))],
        compiler_params=params,
        name="finish",
    )(table, sums, thermal_source_term, basis, shares)
    return rezoned_occupancy_shares, thermal_iterate, remaining_defect


def solution(mesh):
    placed = (P("col", "row", None), P(), P(), P(), P(), P(), P(), P(None, "row", "col"))
    return jax.shard_map(
        functools.partial(per_device, mesh.shape["row"], mesh.shape["col"]),
        mesh=mesh,
        in_specs=placed,
        out_specs=(P(None, "row", "col"), P(None, "row", "col"), P(None, "row", "col")),
        check_vma=False,
    )
```

```python
import functools

import jax
import jax.numpy as jnp
from jax import lax
from jax.experimental import pallas as pl
from jax.experimental.pallas import tpu as pltpu
from jax.sharding import PartitionSpec as P

M = 6
SBLK = 64
TBLK = 48
ITERS = 3
RIM = ITERS
ROWS = 56
LANES = 128
GROUPS = ROWS // 8
TAIL = LANES // GROUPS // 8 * 8
VMEM = 48 * 1024 * 1024
FULL = 63 * 1024 * 1024
TINY = 1e-30
F32 = jnp.float32
EXACT = lax.Precision.HIGH


def tiles(cells):
    return -(-cells // LANES)


def window_rows(row_count):
    count = row_count // 2 - 1
    rows = [[2 * q + 1, 2 * q + 2] for q in range(count)]
    rows[0] = [0] + rows[0]
    rows[-1] = rows[-1] + [row_count - 1]
    return rows


def rezone_kernel(
    row_count,
    xs_hbm,
    xt_hbm,
    ys_hbm,
    yt_hbm,
    frac_hbm,
    field_hbm,
    out_hbm,
    xs_ref,
    xt_ref,
    ys_ref,
    yt_ref,
    frac_ref,
    field_ref,
    edges_ref,
    wide_ref,
    along_ref,
    out_ref,
    sems,
    out_sems,
):
    me = lax.axis_index("row")
    pairs = frac_ref.shape[0]
    moves = [
        pltpu.make_async_copy(here, there, sems.at[n])
        for n, (here, there) in enumerate(
            (
                (yt_hbm, yt_ref),
                (xt_hbm, xt_ref),
                (xs_hbm, xs_ref),
                (ys_hbm, ys_ref),
                (frac_hbm, frac_ref),
                (field_hbm, field_ref),
            )
        )
    ]
    for move in moves:
        move.start()
    edges_ref[...] = jnp.zeros_like(edges_ref)
    along_ref[pairs * TBLK :, :] = jnp.zeros_like(along_ref[pairs * TBLK :, :])
    for n, ref in enumerate((yt_ref, xt_ref, xs_ref, ys_ref)):
        moves[n].wait()
        edges_ref[n : n + 1, 0 : ref.shape[0]] = ref[...].astype(F32)[None, :]

    def from_here(row, start, lane):
        base = start // LANES * LANES
        if not isinstance(base, int):
            base = pl.multiple_of(base, LANES)
        window = edges_ref[row : row + 1, pl.ds(base, 2 * LANES)]
        return pltpu.roll(window, (lane - (start - base) + 2 * LANES) % (2 * LANES), 1)

    starts = [from_here(0, max(r * TBLK - RIM, 0), 0 if r else RIM) for r in range(row_count)]
    starts.append(from_here(1, me * TBLK, 0))
    spare = jnp.zeros((-len(starts) % 8, LANES), F32)
    columns = jnp.concatenate([start[:, 0:LANES] for start in starts] + [spare], axis=0)
    columns = jnp.transpose(columns)[0 : ROWS + 8]
    ends = pltpu.roll(columns, ROWS + 7, 0)
    for r in range(row_count):
        wide_ref[r, 8 : ROWS + 16] = jnp.broadcast_to(columns[:, r : r + 1], (ROWS + 8, LANES))
    row = lax.broadcasted_iota(jnp.int32, (ROWS, LANES), 0)

    def turned(r, ahead):
        start = 8 + RIM + ahead
        last = jnp.where(
            row[0:8] < 8 - RIM,
            wide_ref[r, start + ROWS - 8 : start + ROWS],
            wide_ref[r, start - 8 : start],
        )
        return jnp.concatenate([wide_ref[r, start : start + ROWS - 8], last], axis=0)

    def weights(src_lo, src_hi, low, high, scale):
        shared = jnp.maximum(jnp.minimum(src_hi, high) - jnp.maximum(src_lo, low), 0.0)
        return shared * scale

    mine = slice(row_count, row_count + 1)
    x_lo = from_here(2, me * SBLK, 0)
    x_hi = pltpu.roll(x_lo, 2 * LANES - 1, 1)
    x_tgt_lo, x_tgt_hi = columns[0:TBLK, mine], ends[0:TBLK, mine]
    weight_x = weights(
        x_lo[:, 0:SBLK], x_hi[:, 0:SBLK], x_tgt_lo, x_tgt_hi, 1.0 / (x_tgt_hi - x_tgt_lo)
    )
    moves[5].wait()
    zlayers, height, breadth = field_ref.shape
    base = ROWS + 8
    for r in range(row_count):
        for t in range(tiles(breadth)):
            lo, hi = t * LANES, min((t + 1) * LANES, breadth)
            for layer in range(zlayers):
                rim = jnp.where(
                    r > me,
                    field_ref[layer, height - RIM :, lo:hi],
                    field_ref[layer, :RIM, lo:hi],
                )
                at = base + 8 * t + RIM * layer
                out_ref[r, at : at + RIM, 0 : hi - lo] = rim
    moves[4].wait()
    for p in range(pairs):
        along_ref[p * TBLK : (p + 1) * TBLK, :] = jnp.dot(
            weight_x, frac_ref[p], precision=EXACT, preferred_element_type=F32
        )
    width = 4 * SBLK
    weights_y = []
    for q, rows in enumerate(window_rows(row_count)):
        parts = []
        for r in rows:
            low, high = turned(r, 0), turned(r, 1)
            inside = row < (TBLK if r + 1 == row_count else TBLK + RIM)
            if r:
                inside = inside | (row >= ROWS - RIM)
            scale = jnp.where(inside, 1.0 / jnp.maximum(high - low, 1.0), 0.0)
            wide = []
            for at in range(2 * q * SBLK, 2 * q * SBLK + width, LANES):
                src_lo, src_hi = edges_ref[3:4, at : at + LANES], edges_ref[3:4, at + 1 : at + 1 + LANES]
                wide.append(weights(src_lo, src_hi, low, high, scale))
            parts.append(jnp.concatenate(wide, axis=1))
        weights_y.append(jnp.concatenate(parts, axis=0))
    leaving = []
    for q, rows in enumerate(window_rows(row_count)):
        block = lax.dot_general(
            weights_y[q],
            along_ref[:, 2 * q * SBLK : 2 * q * SBLK + width],
            (((1,), (1,)), ((), ())),
            precision=EXACT,
            preferred_element_type=F32,
        )
        for n, r in enumerate(rows):
            mine = block[n * ROWS : (n + 1) * ROWS]
            out_ref[r, 0:ROWS, :] = mine[:, 0:LANES]
            packed = mine[0:8, LANES:]
            for g in range(1, GROUPS):
                packed = packed + pltpu.roll(mine[8 * g : 8 * g + 8, LANES:], TAIL * g, 1)
            out_ref[r, ROWS : ROWS + 8, :] = packed
        done = pl.ds(rows[0], len(rows))
        leaving.append(pltpu.make_async_copy(out_ref.at[done], out_hbm.at[done], out_sems.at[q]))
        leaving[-1].start()
    for move in leaving:
        move.wait()


def table_kernel(cond_ref, heat_ref, table_ref):
    resistance = 16.0 / cond_ref[...].astype(F32)[None, :]
    heat = heat_ref[...][None, :]
    middle = 5.0 * M / jnp.sum(resistance, axis=1, keepdims=True)
    shift = jnp.sum(heat, axis=1, keepdims=True) / M + middle
    rest = jnp.zeros((1, LANES - 2 * M - 3), F32)
    table = jnp.concatenate([resistance, heat, shift, 1.0 / middle, middle, rest], axis=1)
    table = jnp.transpose(jnp.broadcast_to(table, (LANES, LANES)))
    table_ref[...] = table[0 : table_ref.shape[0]]


def extend_rows(row_count, got_ref, field_ref, ext_ref):
    my_row = lax.axis_index("row")
    zlayers, height, breadth = field_ref.shape
    base = ROWS + 8
    ext_ref[...] = jnp.zeros_like(ext_ref)
    below, above = jnp.maximum(my_row - 1, 0), jnp.minimum(my_row + 1, row_count - 1)
    for layer in range(zlayers):
        ext_ref[layer, 0:height, 0:breadth] = field_ref[layer]
        for t in range(tiles(breadth)):
            lo, hi = t * LANES, min((t + 1) * LANES, breadth)
            at = base + 8 * t + RIM * layer
            after = got_ref[above, at : at + RIM, 0 : hi - lo]
            before = got_ref[below, at : at + RIM, 0 : hi - lo]
            ext_ref[layer, height : height + RIM, lo:hi] = jnp.where(
                my_row < row_count - 1, after, 0.0
            )
            ext_ref[layer, ROWS - RIM : ROWS, lo:hi] = jnp.where(my_row > 0, before, 0.0)


def regroup_kernel(row_count, col_count, masks, got_ref, field_ref, *refs):
    my_col = lax.axis_index("col")
    zlayers, _, breadth = field_ref.shape
    ext_ref, out_refs = refs[0], refs[1:]
    pairs, _, width = out_refs[0].shape
    per_col = row_count // col_count
    if col_count // 2 in masks:
        extend_rows(row_count, got_ref, field_ref, ext_ref)

    def piece(block, pair, first, last):
        start = pair * TBLK
        lo, hi = start + first, start + last
        parts = []
        if lo < LANES:
            parts.append(got_ref[block, 0:ROWS, lo : min(hi, LANES)])
        if hi > LANES:
            a, b = max(lo, LANES) - LANES, hi - LANES
            tail = got_ref[block, ROWS : ROWS + 8, :]
            parts.append(
                jnp.concatenate([tail[:, TAIL * g + a : TAIL * g + b] for g in range(GROUPS)], axis=0)
            )
        return parts[0] if len(parts) == 1 else jnp.concatenate(parts, axis=1)

    for mask, out_ref in zip(masks, out_refs):
        c = my_col ^ mask
        first = c * per_col
        left, right = jnp.maximum(first - 1, 0), jnp.minimum(first + per_col, row_count - 1)
        for p in range(pairs):
            parts = [piece(first + j, p, 0, TBLK) for j in range(per_col)]
            parts.append(jnp.where(c < col_count - 1, piece(right, p, 0, RIM), 0.0))
            if p < zlayers and mask:
                whole = ext_ref[p]
                parts.append(
                    jnp.where(c > my_col, whole[:, breadth - RIM : breadth], whole[:, 0:RIM])
                )
            else:
                parts.append(jnp.zeros((ROWS, RIM), F32))
            parts.append(jnp.zeros((ROWS, width - breadth - 3 * RIM), F32))
            parts.append(jnp.where(c > 0, piece(left, p, TBLK - RIM, TBLK), 0.0))
            out_ref[p] = jnp.concatenate(parts, axis=1)


def basis_kernel(col_count, height, breadth, table_ref, ext_ref, *refs):
    arrivals, refs = refs[:col_count], refs[col_count:]
    shares_ref, basis_ref, sums_ref, got_ref = refs
    my_col = lax.axis_index("col")
    for mask, arrival in enumerate(arrivals):
        got_ref[my_col ^ mask] = arrival[...]
        for p in range(arrival.shape[0]):
            at = (my_col ^ mask) * arrival.shape[0] + p
            shares_ref[at] = arrival[p, 0:height, 0:breadth]
    zlayers = ext_ref.shape[0]
    pairs, rows, width = got_ref.shape[1:]
    lane = lax.broadcasted_iota(jnp.int32, (rows, width), 1)
    before, after = jnp.maximum(my_col - 1, 0), jnp.minimum(my_col + 1, col_count - 1)

    def ahead(array, axis):
        return pltpu.roll(array, array.shape[axis] - 1, axis)

    def behind(array, axis):
        return pltpu.roll(array, 1, axis)

    def face(one, other):
        return 2.0 * one * other / jnp.maximum(one + other, TINY)

    def entry(n):
        return table_ref[n : n + 1, 0:1]

    cell_k, heat, field = [], [], []
    for z in range(zlayers):
        inverse = jnp.zeros((rows, width), F32)
        total = jnp.zeros((rows, width), F32)
        for m in range(M):
            c, p = divmod(z * M + m, pairs)
            share = got_ref[c, p]
            inside = jnp.where((lane < breadth + RIM) | (lane >= width - RIM), share, 0.0)
            inverse = inverse + inside * entry(m)
            total = total + inside * entry(M + m)
        cell_k.append(jnp.where(inverse > 0.0, 1.0 / jnp.where(inverse > 0.0, inverse, 1.0), 0.0))
        heat.append(total)
        left, right = got_ref[before, z], got_ref[after, z]
        left = pltpu.roll(left, width - (breadth + 2 * RIM), 1)
        right = pltpu.roll(right, width - RIM, 1)
        value = ext_ref[z]
        value = jnp.where(
            (lane >= breadth) & (lane < breadth + RIM) & (my_col < col_count - 1), right, value
        )
        value = jnp.where((lane >= width - RIM) & (my_col > 0), left, value)
        field.append(value)
    face_x = [face(k, ahead(k, 1)) for k in cell_k]
    face_y = [face(k, ahead(k, 0)) for k in cell_k]
    face_z = [face(cell_k[z], cell_k[z + 1]) for z in range(zlayers - 1)]

    def operate(w):
        result = []
        for z in range(zlayers):
            flow_x = face_x[z] * (w[z] - ahead(w[z], 1))
            flow_y = face_y[z] * (w[z] - ahead(w[z], 0))
            value = heat[z] * w[z] + (flow_x - behind(flow_x, 1)) + (flow_y - behind(flow_y, 0))
            if z + 1 < zlayers:
                value = value + face_z[z] * (w[z] - w[z + 1])
            if z:
                value = value - face_z[z - 1] * (w[z - 1] - w[z])
            result.append(value)
        return result

    shift, scale = entry(2 * M), entry(2 * M + 1)

    def shifted(w):
        return [(a - shift * b) * scale for a, b in zip(operate(w), w)]

    basis = [field, shifted(field)]
    for _ in range(ITERS - 1):
        basis.append([2.0 * a - b for a, b in zip(shifted(basis[-1]), basis[-2])])
    own = [
        [jnp.where(lane < breadth, layer, 0.0)[0:height] for layer in vector] for vector in basis
    ]
    for n in range(ITERS):
        for z in range(zlayers):
            basis_ref[n, z] = own[n + 1][z][:, 0:breadth]
    slot = lax.broadcasted_iota(jnp.int32, (1, LANES), 1)
    packed = jnp.zeros((1, LANES), F32)
    at = 0
    for a in range(ITERS + 1):
        for b in range(a, ITERS + 1):
            product = own[a][0] * own[b][0]
            for z in range(1, zlayers):
                product = product + own[a][z] * own[b][z]
            value = jnp.sum(product, axis=0, keepdims=True)
            value = jnp.sum(value, axis=1, keepdims=True)
            packed = packed + jnp.where(slot == at, value, 0.0)
            at += 1
    sums_ref[...] = jnp.broadcast_to(packed[None], sums_ref.shape)


def finish_kernel(
    table_ref,
    sums_ref,
    field_ref,
    basis_ref,
    shares_ref,
    iterate_hbm,
    defect_hbm,
    shares_hbm,
    iterate_ref,
    defect_ref,
    sems,
):
    pairs = (shares_ref, shares_hbm), (iterate_ref, iterate_hbm), (defect_ref, defect_hbm)
    leaving = [pltpu.make_async_copy(*pair, sems.at[n]) for n, pair in enumerate(pairs)]
    leaving[0].start()
    total = jnp.sum(sums_ref[...], axis=0)
    gram = {}
    at = 0
    for a in range(ITERS + 1):
        for b in range(a, ITERS + 1):
            gram[a, b] = gram[b, a] = total[:, at : at + 1]
            at += 1
    shift, scale = (table_ref[n : n + 1, 0:1] for n in (2 * M, 2 * M + 2))

    def inner(left, right):
        rows = []
        for a, one in left.items():
            rows.append(one * total_of([other * gram[a, b] for b, other in right.items()]))
        return total_of(rows)

    def total_of(terms):
        while len(terms) > 1:
            terms = [sum(terms[n : n + 2][1:], terms[n]) for n in range(0, len(terms), 2)]
        return terms[0]

    def combine(left, factor, right):
        result = dict(left)
        for a, one in right.items():
            result[a] = result[a] + factor * one if a in result else factor * one
        return result

    def apply(vector):
        result = {}
        for a, one in vector.items():
            if a:
                moved = {a - 1: 0.5 * scale * one, a: shift * one, a + 1: 0.5 * scale * one}
            else:
                moved = {0: shift * one, 1: scale * one}
            for b, other in moved.items():
                result[b] = result[b] + other if b in result else other
        return result

    one = jnp.ones((1, 1), F32)
    iterate, defect, direction = {}, {0: one}, {0: one}
    norm = gram[0, 0]
    for iteration in range(ITERS):
        applied = apply(direction)
        step = norm / inner(direction, applied)
        iterate = combine(iterate, step, direction)
        defect = combine(defect, -step, applied)
        if iteration + 1 < ITERS:
            following = inner(defect, defect)
            direction = combine(defect, following / norm, direction)
            norm = following
    for ref, weights, move in ((iterate_ref, iterate, leaving[1]), (defect_ref, defect, leaving[2])):
        for z in range(field_ref.shape[0]):
            vectors = [field_ref[z]] + [basis_ref[n, z] for n in range(ITERS)]
            ref[z] = total_of([weight * vectors[a] for a, weight in weights.items()])
        move.start()
    for move in leaving:
        move.wait()


def per_device(
    row_count,
    col_count,
    fractions_source,
    x_source_edges,
    x_target_edges,
    y_source_edges,
    y_target_edges,
    conductivity_table,
    capacity,
    thermal_source_term,
):
    pairs, _, source_cells = fractions_source.shape
    zlayers, height, breadth = thermal_source_term.shape
    width = LANES * tiles(breadth + 4 * RIM)
    send_rows = ROWS + 8 + 8 * tiles(breadth)
    params = pltpu.CompilerParams(vmem_limit_bytes=VMEM)

    vmem = pl.BlockSpec(memory_space=pltpu.VMEM)
    hbm = pl.BlockSpec(memory_space=pltpu.HBM)
    along_rows = -(-pairs * TBLK // LANES) * LANES
    edges = [x_source_edges, x_target_edges, y_source_edges, y_target_edges]
    outgoing = jax.ShapeDtypeStruct((row_count, send_rows, LANES), F32)
    outgoing = pl.pallas_call(
        functools.partial(rezone_kernel, row_count),
        out_shape=outgoing,
        in_specs=[hbm] * 6,
        out_specs=hbm,
        scratch_shapes=[pltpu.VMEM(e.shape, e.dtype) for e in edges]
        + [
            pltpu.VMEM(fractions_source.shape, F32),
            pltpu.VMEM(thermal_source_term.shape, F32),
            pltpu.VMEM((8, LANES * (tiles(source_cells + 1) + 1)), F32),
            pltpu.VMEM((row_count, ROWS + 16, LANES), F32),
            pltpu.VMEM((along_rows, source_cells), F32),
            pltpu.VMEM(outgoing.shape, F32),
            pltpu.SemaphoreType.DMA((6,)),
            pltpu.SemaphoreType.DMA((row_count // 2 - 1,)),
        ],
        compiler_params=pltpu.CompilerParams(vmem_limit_bytes=FULL),
        name="rezone",
    )(*edges, fractions_source, thermal_source_term)
    arrived = lax.all_to_all(outgoing, "row", split_axis=0, concat_axis=0, tiled=True)
    table = pl.pallas_call(
        table_kernel,
        out_shape=jax.ShapeDtypeStruct((-(-(2 * M + 3) // 8) * 8, LANES), F32),
        in_specs=[vmem] * 2,
        out_specs=vmem,
        compiler_params=params,
        name="table",
    )(conductivity_table, capacity)
    message = jax.ShapeDtypeStruct((pairs, ROWS, width), F32)
    half = col_count // 2
    near, far = range(half), range(half, col_count)
    extended, *far_parts = pl.pallas_call(
        functools.partial(regroup_kernel, row_count, col_count, far),
        out_shape=[jax.ShapeDtypeStruct((zlayers, ROWS, width), F32)] + [message] * half,
        in_specs=[vmem] * 2,
        out_specs=[vmem] * (1 + half),
        compiler_params=params,
        name="regroup_far",
    )(arrived, thermal_source_term)

    def swap(part, mask):
        return lax.ppermute(part, "col", [(c, c ^ mask) for c in range(col_count)])

    far_parts = [swap(part, mask) for part, mask in zip(far_parts, far)]
    near_parts = pl.pallas_call(
        functools.partial(regroup_kernel, row_count, col_count, near),
        out_shape=[message] * half,
        in_specs=[vmem] * 3,
        out_specs=[vmem] * half,
        compiler_params=params,
        cost_estimate=pl.CostEstimate(flops=10**6, bytes_accessed=2 * 10**6, transcendentals=0),
        name="regroup_near",
    )(arrived, thermal_source_term, extended)
    parts = [swap(part, mask) if mask else part for part, mask in zip(near_parts, near)] + far_parts
    shares, basis, sums = pl.pallas_call(
        functools.partial(basis_kernel, col_count, height, breadth),
        out_shape=[
            jax.ShapeDtypeStruct((zlayers * M, height, breadth), F32),
            jax.ShapeDtypeStruct((ITERS, zlayers, height, breadth), F32),
            jax.ShapeDtypeStruct((row_count * col_count, 1, LANES), F32),
        ],
        in_specs=[vmem] * (2 + col_count),
        out_specs=[vmem] * 3,
        scratch_shapes=[pltpu.VMEM((col_count, *message.shape), F32)],
        compiler_params=params,
        name="basis",
    )(table, extended, *parts)
    sums = lax.all_to_all(sums, ("row", "col"), split_axis=0, concat_axis=0, tiled=True)
    thermal_iterate, remaining_defect, rezoned_occupancy_shares = pl.pallas_call(
        finish_kernel,
        out_shape=[jax.ShapeDtypeStruct((zlayers, height, breadth), F32)] * 2
        + [jax.ShapeDtypeStruct(shares.shape, F32)],
        in_specs=[vmem] * 5,
        out_specs=[hbm] * 3,
        scratch_shapes=[pltpu.VMEM((zlayers, height, breadth), F32)] * 2
        + [pltpu.SemaphoreType.DMA((3,))],
        compiler_params=params,
        name="finish",
    )(table, sums, thermal_source_term, basis, shares)
    return rezoned_occupancy_shares, thermal_iterate, remaining_defect


def solution(mesh):
    placed = (P("col", "row", None), P(), P(), P(), P(), P(), P(), P(None, "row", "col"))
    return jax.shard_map(
        functools.partial(per_device, mesh.shape["row"], mesh.shape["col"]),
        mesh=mesh,
        in_specs=placed,
        out_specs=(P(None, "row", "col"), P(None, "row", "col"), P(None, "row", "col")),
        check_vma=False,
    )
```

```python
import functools

import jax
import jax.numpy as jnp
from jax import lax
from jax.experimental import pallas as pl
from jax.experimental.pallas import tpu as pltpu
from jax.sharding import PartitionSpec as P

M = 6
SBLK = 64
TBLK = 48
ITERS = 3
RIM = ITERS
ROWS = 56
LANES = 128
EDGE = ROWS - TBLK
GROUPS = TBLK // 8
TAIL = 16
CHUNK = LANES - GROUPS * TAIL
BODY = ROWS + 8
VMEM = 48 * 1024 * 1024
FULL = 63 * 1024 * 1024
TINY = 1e-30
F32 = jnp.float32
EXACT = lax.Precision.HIGHEST


def tiles(cells):
    return -(-cells // LANES)


def compact(breadth):
    return breadth == 3 * CHUNK


def pack_rims(rims):
    count = rims.shape[0]
    side = jnp.zeros((count, LANES - CHUNK), F32)
    below = jnp.zeros((8 - count, LANES), F32)
    tail = jnp.concatenate([side, rims[:, 0:CHUNK]], axis=1)
    edge = jnp.concatenate([side, rims[:, CHUNK : 2 * CHUNK]], axis=1)
    lines = []
    for at in (0, RIM):
        parts = [rims[at + n : at + n + 1, 2 * CHUNK :] for n in range(RIM)]
        lines.append(jnp.concatenate(parts + [jnp.zeros((1, CHUNK), F32)], axis=1))
    gap = [jnp.zeros((RIM, LANES), F32)] + lines + [jnp.zeros((EDGE - RIM - 2, LANES), F32)]
    return (
        jnp.concatenate([tail, below], axis=0),
        jnp.concatenate([edge, below], axis=0) + jnp.concatenate(gap, axis=0),
    )


def unpack_rims(tail, edge, count):
    last = [
        edge[RIM + n // RIM : RIM + n // RIM + 1, CHUNK * (n % RIM) : CHUNK * (n % RIM + 1)]
        for n in range(count)
    ]
    parts = [tail[0:count, LANES - CHUNK :], edge[0:count, LANES - CHUNK :]]
    return jnp.concatenate(parts + [jnp.concatenate(last, axis=0)], axis=1)


def window_rows(row_count):
    count = row_count // 2 - 1
    rows = [[2 * q + 1, 2 * q + 2] for q in range(count)]
    rows[0] = [0] + rows[0]
    rows[-1] = rows[-1] + [row_count - 1]
    return rows


def rezone_kernel(
    row_count,
    xs_hbm,
    xt_hbm,
    ys_hbm,
    yt_hbm,
    cond_hbm,
    heat_hbm,
    frac_hbm,
    field_hbm,
    out_hbm,
    xs_ref,
    xt_ref,
    ys_ref,
    yt_ref,
    cond_ref,
    heat_ref,
    frac_ref,
    field_ref,
    edges_ref,
    wide_ref,
    along_ref,
    out_ref,
    sems,
    out_sems,
):
    me = lax.axis_index("row")
    pairs = frac_ref.shape[0]
    moves = [
        pltpu.make_async_copy(here, there, sems.at[n])
        for n, (here, there) in enumerate(
            (
                (yt_hbm, yt_ref),
                (xt_hbm, xt_ref),
                (xs_hbm, xs_ref),
                (ys_hbm, ys_ref),
                (frac_hbm, frac_ref),
                (field_hbm, field_ref),
                (cond_hbm, cond_ref),
                (heat_hbm, heat_ref),
            )
        )
    ]
    for move in moves:
        move.start()
    edges_ref[...] = jnp.zeros_like(edges_ref)
    used = (pairs + 2) * TBLK
    along_ref[used:, :] = jnp.zeros_like(along_ref[used:, :])
    for n, ref in enumerate((yt_ref, xt_ref, xs_ref, ys_ref)):
        moves[n].wait()
        edges_ref[n : n + 1, 0 : ref.shape[0]] = ref[...].astype(F32)[None, :]

    def from_here(row, start, lane):
        base = start // LANES * LANES
        if not isinstance(base, int):
            base = pl.multiple_of(base, LANES)
        window = edges_ref[row : row + 1, pl.ds(base, 2 * LANES)]
        return pltpu.roll(window, (lane - (start - base) + 2 * LANES) % (2 * LANES), 1)

    starts = [from_here(0, max(r * TBLK - RIM, 0), 0 if r else RIM) for r in range(row_count)]
    starts.append(from_here(1, me * TBLK, 0))
    spare = jnp.zeros((-len(starts) % 8, LANES), F32)
    columns = jnp.concatenate([start[:, 0:LANES] for start in starts] + [spare], axis=0)
    columns = jnp.transpose(columns)[0 : ROWS + 8]
    ends = pltpu.roll(columns, ROWS + 7, 0)
    for r in range(row_count):
        wide_ref[r, 8 : ROWS + 16] = jnp.broadcast_to(columns[:, r : r + 1], (ROWS + 8, LANES))
    row = lax.broadcasted_iota(jnp.int32, (ROWS, LANES), 0)

    def turned(r, ahead):
        start = 8 + RIM + ahead
        last = jnp.where(
            row[0:8] < 8 - RIM,
            wide_ref[r, start + ROWS - 8 : start + ROWS],
            wide_ref[r, start - 8 : start],
        )
        return jnp.concatenate([wide_ref[r, start : start + ROWS - 8], last], axis=0)

    def weights(src_lo, src_hi, low, high, scale):
        shared = jnp.maximum(jnp.minimum(src_hi, high) - jnp.maximum(src_lo, low), 0.0)
        return shared * scale

    mine = slice(row_count, row_count + 1)
    lane = lax.broadcasted_iota(jnp.int32, (1, LANES), 1)
    x_lo = from_here(2, me * SBLK, 0)
    x_hi = pltpu.roll(x_lo, 2 * LANES - 1, 1)
    x_tgt_lo, x_tgt_hi = columns[0:TBLK, mine], ends[0:TBLK, mine]
    weight_x = weights(
        x_lo[:, 0:SBLK], x_hi[:, 0:SBLK], x_tgt_lo, x_tgt_hi, 1.0 / (x_tgt_hi - x_tgt_lo)
    )
    moves[5].wait()
    moves[6].wait()
    moves[7].wait()
    zlayers, height, breadth = field_ref.shape
    rims = []
    for rows in (slice(0, RIM), slice(height - RIM, height)):
        rims.append(jnp.concatenate([field_ref[layer, rows] for layer in range(zlayers)], axis=0))
    if compact(breadth):
        rims = [pack_rims(rim) for rim in rims]
    else:
        for r in range(row_count):
            rim = jnp.where(r > me, rims[1], rims[0])
            for t in range(tiles(breadth)):
                lo, hi = t * LANES, min((t + 1) * LANES, breadth)
                at = BODY + 8 * t
                out_ref[r, at : at + zlayers * RIM, 0 : hi - lo] = rim[:, lo:hi]
    resistance = 16.0 / cond_ref[...].astype(F32)[None, :]
    material = lax.broadcasted_iota(jnp.int32, (1, M), 1)
    factors = []
    for p in range(pairs):
        mine = material == lax.rem(lax.axis_index("col") * pairs + p, M)
        factors.append(
            [
                jnp.sum(jnp.where(mine, value, 0.0), axis=1, keepdims=True)
                for value in (resistance, heat_ref[...][None, :])
            ]
        )
    moves[4].wait()
    partial = [0.0, 0.0]
    for p in range(pairs):
        along = jnp.dot(weight_x, frac_ref[p], precision=EXACT, preferred_element_type=F32)
        along_ref[p * TBLK : (p + 1) * TBLK, :] = along
        partial = [total + factor * along for total, factor in zip(partial, factors[p])]
    for n, total in enumerate(partial):
        along_ref[(pairs + n) * TBLK : (pairs + n + 1) * TBLK, :] = total
    width = 4 * SBLK
    weights_y = []
    for q, rows in enumerate(window_rows(row_count)):
        parts = []
        for r in rows:
            low, high = turned(r, 0), turned(r, 1)
            inside = row < (TBLK if r + 1 == row_count else TBLK + RIM)
            if r:
                inside = inside | (row >= ROWS - RIM)
            scale = jnp.where(inside, 1.0 / jnp.maximum(high - low, 1.0), 0.0)
            wide = []
            for at in range(2 * q * SBLK, 2 * q * SBLK + width, LANES):
                src_lo, src_hi = edges_ref[3:4, at : at + LANES], edges_ref[3:4, at + 1 : at + 1 + LANES]
                wide.append(weights(src_lo, src_hi, low, high, scale))
            parts.append(jnp.concatenate(wide, axis=1))
        weights_y.append(jnp.concatenate(parts, axis=0))
    leaving = []
    for q, rows in enumerate(window_rows(row_count)):
        block = lax.dot_general(
            weights_y[q],
            along_ref[:, 2 * q * SBLK : 2 * q * SBLK + width],
            (((1,), (1,)), ((), ())),
            precision=EXACT,
            preferred_element_type=F32,
        )
        for n, r in enumerate(rows):
            mine = block[n * ROWS : (n + 1) * ROWS]
            out_ref[r, 0:TBLK, :] = mine[0:TBLK, 0:LANES]
            packed = jnp.where(lane < TAIL, mine[0:8, LANES:], 0.0)
            for g in range(1, GROUPS):
                group = jnp.where(lane < TAIL, mine[8 * g : 8 * g + 8, LANES:], 0.0)
                packed = packed + pltpu.roll(group, TAIL * g, 1)
            edge = pltpu.roll(mine[TBLK:ROWS, LANES:], LANES - TAIL, 1)
            edge = jnp.where(lane < 2 * TBLK, edge, 0.0)
            if compact(breadth):
                packed = packed + jnp.where(r > me, rims[1][0], rims[0][0])
                edge = edge + jnp.where(r > me, rims[1][1], rims[0][1])
            out_ref[r, TBLK : TBLK + 8, :] = packed
            out_ref[r, ROWS:BODY, :] = edge
        done = pl.ds(rows[0], len(rows))
        leaving.append(pltpu.make_async_copy(out_ref.at[done], out_hbm.at[done], out_sems.at[q]))
        leaving[-1].start()
    for move in leaving:
        move.wait()


def table_kernel(cond_ref, heat_ref, table_ref):
    resistance = 16.0 / cond_ref[...].astype(F32)[None, :]
    heat = heat_ref[...][None, :]
    middle = 5.0 * M / jnp.sum(resistance, axis=1, keepdims=True)
    shift = jnp.sum(heat, axis=1, keepdims=True) / M + middle
    rest = jnp.zeros((1, LANES - 2 * M - 3), F32)
    table = jnp.concatenate([resistance, heat, shift, 1.0 / middle, middle, rest], axis=1)
    table = jnp.transpose(jnp.broadcast_to(table, (LANES, LANES)))
    table_ref[...] = table[0 : table_ref.shape[0]]


def extend_rows(row_count, got_ref, field_ref, ext_ref):
    my_row = lax.axis_index("row")
    zlayers, height, breadth = field_ref.shape
    ext_ref[...] = jnp.zeros_like(ext_ref)
    below, above = jnp.maximum(my_row - 1, 0), jnp.minimum(my_row + 1, row_count - 1)
    count = zlayers * RIM
    for block, there, at in (
        (above, my_row < row_count - 1, height),
        (below, my_row > 0, ROWS - RIM),
    ):
        if compact(breadth):
            rims = unpack_rims(got_ref[block, TBLK : TBLK + 8], got_ref[block, ROWS:BODY], count)
        else:
            parts = [got_ref[block, BODY + 8 * t : BODY + 8 * t + count] for t in range(tiles(breadth))]
            rims = jnp.concatenate(parts, axis=1)[:, 0:breadth]
        rims = jnp.where(there, rims, 0.0)
        for layer in range(zlayers):
            ext_ref[layer, at : at + RIM, 0:breadth] = rims[layer * RIM : (layer + 1) * RIM]
    for layer in range(zlayers):
        ext_ref[layer, 0:height, 0:breadth] = field_ref[layer]


def regroup_kernel(row_count, col_count, masks, got_ref, field_ref, *refs):
    my_col = lax.axis_index("col")
    zlayers, _, breadth = field_ref.shape
    ext_ref, out_refs = refs[0], refs[1:]
    width = out_refs[0].shape[1]
    pairs = out_refs[0].shape[0] // TBLK
    per_col = row_count // col_count
    if col_count // 2 in masks:
        extend_rows(row_count, got_ref, field_ref, ext_ref)

    def own(block, pair, first, last):
        lo, hi = pair * TBLK + first, pair * TBLK + last
        parts = []
        if lo < LANES:
            parts.append(got_ref[block, 0:TBLK, lo : min(hi, LANES)])
        if hi > LANES:
            a, b = max(lo, LANES) - LANES, hi - LANES
            tail = got_ref[block, TBLK : TBLK + 8, :]
            parts.append(
                jnp.concatenate([tail[:, TAIL * g + a : TAIL * g + b] for g in range(GROUPS)], axis=0)
            )
        return parts[0] if len(parts) == 1 else jnp.concatenate(parts, axis=1)

    def edge(block, which, first, last):
        return got_ref[block, ROWS:BODY, which * TBLK + first : which * TBLK + last]

    for mask, out_ref in zip(masks, out_refs):
        c = my_col ^ mask
        start = c * per_col
        left, right = jnp.maximum(start - 1, 0), jnp.minimum(start + per_col, row_count - 1)

        def line(cells, rows, kind, layer):
            parts = [cells(start + j, kind, 0, TBLK) for j in range(per_col)]
            count = parts[0].shape[0]
            parts.append(jnp.where(c < col_count - 1, cells(right, kind, 0, RIM), 0.0))
            if layer < zlayers and mask:
                whole = ext_ref[layer, rows]
                parts.append(
                    jnp.where(c > my_col, whole[:, breadth - RIM : breadth], whole[:, 0:RIM])
                )
            else:
                parts.append(jnp.zeros((count, RIM), F32))
            parts.append(jnp.zeros((count, width - breadth - 3 * RIM), F32))
            parts.append(jnp.where(c > 0, cells(left, kind, TBLK - RIM, TBLK), 0.0))
            return jnp.concatenate(parts, axis=1)

        for p in range(pairs):
            out_ref[p * TBLK : (p + 1) * TBLK] = line(own, slice(0, TBLK), p, p)
        for n in range(2):
            at = pairs * TBLK + EDGE * n
            out_ref[at : at + EDGE] = line(edge, slice(TBLK, ROWS), n, n)


def basis_kernel(col_count, height, breadth, table_ref, ext_ref, *refs):
    arrivals, refs = refs[:col_count], refs[col_count:]
    shares_ref, basis_ref, sums_ref, got_ref = refs
    my_col = lax.axis_index("col")
    pairs = arrivals[0].shape[0] // TBLK
    for mask, arrival in enumerate(arrivals):
        got_ref[my_col ^ mask] = arrival[...]
        for p in range(pairs):
            at = (my_col ^ mask) * pairs + p
            shares_ref[at] = arrival[p * TBLK : (p + 1) * TBLK, 0:breadth]
    zlayers = ext_ref.shape[0]
    rows, width = ext_ref.shape[1:]
    lane = lax.broadcasted_iota(jnp.int32, (rows, width), 1)
    before, after = jnp.maximum(my_col - 1, 0), jnp.minimum(my_col + 1, col_count - 1)

    def ahead(array, axis):
        return pltpu.roll(array, array.shape[axis] - 1, axis)

    def behind(array, axis):
        return pltpu.roll(array, 1, axis)

    def face(one, other):
        return 2.0 * one * other / jnp.maximum(one + other, TINY)

    def entry(n):
        return table_ref[n : n + 1, 0:1]

    row = lax.broadcasted_iota(jnp.int32, (rows, width), 0)
    inside = ((lane < breadth + RIM) | (lane >= width - RIM)) & (
        (row < TBLK + RIM) | (row >= ROWS - RIM)
    )

    cell_k, heat, field = [], [], []
    for z in range(zlayers):
        inverse, total = 0.0, 0.0
        for m in range(M):
            c, p = divmod(z * M + m, pairs)
            share = got_ref[c, p * TBLK : (p + 1) * TBLK]
            inverse = inverse + share * entry(m)
            total = total + share * entry(M + m)
        edge_inverse, edge_total = 0.0, 0.0
        for c in range(z * M // pairs, (z + 1) * M // pairs):
            edge_inverse = edge_inverse + got_ref[c, pairs * TBLK : pairs * TBLK + EDGE]
            edge_total = edge_total + got_ref[c, pairs * TBLK + EDGE :]
        inverse = jnp.concatenate([inverse, edge_inverse], axis=0)
        total = jnp.concatenate([total, edge_total], axis=0)
        inverse, total = (jnp.where(inside, value, 0.0) for value in (inverse, total))
        cell_k.append(jnp.where(inverse > 0.0, 1.0 / jnp.where(inverse > 0.0, inverse, 1.0), 0.0))
        heat.append(total)
        left, right = (
            jnp.concatenate(
                [
                    got_ref[c, z * TBLK : (z + 1) * TBLK],
                    got_ref[c, pairs * TBLK + EDGE * z : pairs * TBLK + EDGE * (z + 1)],
                ],
                axis=0,
            )
            for c in (before, after)
        )
        left = pltpu.roll(left, width - (breadth + 2 * RIM), 1)
        right = pltpu.roll(right, width - RIM, 1)
        value = ext_ref[z]
        value = jnp.where(
            (lane >= breadth) & (lane < breadth + RIM) & (my_col < col_count - 1), right, value
        )
        value = jnp.where((lane >= width - RIM) & (my_col > 0), left, value)
        field.append(value)
    face_x = [face(k, ahead(k, 1)) for k in cell_k]
    face_y = [face(k, ahead(k, 0)) for k in cell_k]
    face_z = [face(cell_k[z], cell_k[z + 1]) for z in range(zlayers - 1)]

    def operate(w):
        result = []
        for z in range(zlayers):
            flow_x = face_x[z] * (w[z] - ahead(w[z], 1))
            flow_y = face_y[z] * (w[z] - ahead(w[z], 0))
            value = heat[z] * w[z] + (flow_x - behind(flow_x, 1)) + (flow_y - behind(flow_y, 0))
            if z + 1 < zlayers:
                value = value + face_z[z] * (w[z] - w[z + 1])
            if z:
                value = value - face_z[z - 1] * (w[z - 1] - w[z])
            result.append(value)
        return result

    shift, scale = entry(2 * M), entry(2 * M + 1)

    def shifted(w):
        return [(a - shift * b) * scale for a, b in zip(operate(w), w)]

    basis = [field, shifted(field)]
    for _ in range(ITERS - 1):
        basis.append([2.0 * a - b for a, b in zip(shifted(basis[-1]), basis[-2])])
    own = [
        [jnp.where(lane < breadth, layer, 0.0)[0:height] for layer in vector] for vector in basis
    ]
    for n in range(ITERS):
        for z in range(zlayers):
            basis_ref[n, z] = own[n + 1][z][:, 0:breadth]
    slot = lax.broadcasted_iota(jnp.int32, (1, LANES), 1)
    packed = jnp.zeros((1, LANES), F32)
    at = 0
    for a in range(ITERS + 1):
        for b in range(a, ITERS + 1):
            product = own[a][0] * own[b][0]
            for z in range(1, zlayers):
                product = product + own[a][z] * own[b][z]
            value = jnp.sum(product, axis=0, keepdims=True)
            value = jnp.sum(value, axis=1, keepdims=True)
            packed = packed + jnp.where(slot == at, value, 0.0)
            at += 1
    sums_ref[...] = jnp.broadcast_to(packed[None], sums_ref.shape)


def finish_kernel(
    table_ref,
    sums_ref,
    field_ref,
    basis_ref,
    shares_ref,
    iterate_hbm,
    defect_hbm,
    shares_hbm,
    iterate_ref,
    defect_ref,
    sems,
):
    pairs = (shares_ref, shares_hbm), (iterate_ref, iterate_hbm), (defect_ref, defect_hbm)
    leaving = [pltpu.make_async_copy(*pair, sems.at[n]) for n, pair in enumerate(pairs)]
    leaving[0].start()
    total = jnp.sum(sums_ref[...], axis=0)
    gram = {}
    at = 0
    for a in range(ITERS + 1):
        for b in range(a, ITERS + 1):
            gram[a, b] = gram[b, a] = total[:, at : at + 1]
            at += 1
    shift, scale = (table_ref[n : n + 1, 0:1] for n in (2 * M, 2 * M + 2))

    def inner(left, right):
        rows = []
        for a, one in left.items():
            rows.append(one * total_of([other * gram[a, b] for b, other in right.items()]))
        return total_of(rows)

    def total_of(terms):
        while len(terms) > 1:
            terms = [sum(terms[n : n + 2][1:], terms[n]) for n in range(0, len(terms), 2)]
        return terms[0]

    def combine(left, factor, right):
        result = dict(left)
        for a, one in right.items():
            result[a] = result[a] + factor * one if a in result else factor * one
        return result

    def apply(vector):
        result = {}
        for a, one in vector.items():
            if a:
                moved = {a - 1: 0.5 * scale * one, a: shift * one, a + 1: 0.5 * scale * one}
            else:
                moved = {0: shift * one, 1: scale * one}
            for b, other in moved.items():
                result[b] = result[b] + other if b in result else other
        return result

    one = jnp.ones((1, 1), F32)
    iterate, defect, direction = {}, {0: one}, {0: one}
    norm = gram[0, 0]
    for iteration in range(ITERS):
        applied = apply(direction)
        step = norm / inner(direction, applied)
        iterate = combine(iterate, step, direction)
        defect = combine(defect, -step, applied)
        if iteration + 1 < ITERS:
            following = inner(defect, defect)
            direction = combine(defect, following / norm, direction)
            norm = following
    for ref, weights, move in ((iterate_ref, iterate, leaving[1]), (defect_ref, defect, leaving[2])):
        for z in range(field_ref.shape[0]):
            vectors = [field_ref[z]] + [basis_ref[n, z] for n in range(ITERS)]
            ref[z] = total_of([weight * vectors[a] for a, weight in weights.items()])
        move.start()
    for move in leaving:
        move.wait()


def per_device(
    row_count,
    col_count,
    fractions_source,
    x_source_edges,
    x_target_edges,
    y_source_edges,
    y_target_edges,
    conductivity_table,
    capacity,
    thermal_source_term,
):
    pairs, _, source_cells = fractions_source.shape
    zlayers, height, breadth = thermal_source_term.shape
    width = LANES * tiles(breadth + 4 * RIM)
    send_rows = BODY + (0 if compact(breadth) else 8 * tiles(breadth))
    params = pltpu.CompilerParams(vmem_limit_bytes=VMEM)

    vmem = pl.BlockSpec(memory_space=pltpu.VMEM)
    hbm = pl.BlockSpec(memory_space=pltpu.HBM)
    along_rows = -(-(pairs + 2) * TBLK // LANES) * LANES
    small = [
        x_source_edges,
        x_target_edges,
        y_source_edges,
        y_target_edges,
        conductivity_table,
        capacity,
    ]
    outgoing = jax.ShapeDtypeStruct((row_count, send_rows, LANES), F32)
    outgoing = pl.pallas_call(
        functools.partial(rezone_kernel, row_count),
        out_shape=outgoing,
        in_specs=[hbm] * 8,
        out_specs=hbm,
        scratch_shapes=[pltpu.VMEM(e.shape, e.dtype) for e in small]
        + [
            pltpu.VMEM(fractions_source.shape, F32),
            pltpu.VMEM(thermal_source_term.shape, F32),
            pltpu.VMEM((8, LANES * (tiles(source_cells + 1) + 1)), F32),
            pltpu.VMEM((row_count, ROWS + 16, LANES), F32),
            pltpu.VMEM((along_rows, source_cells), F32),
            pltpu.VMEM(outgoing.shape, F32),
            pltpu.SemaphoreType.DMA((8,)),
            pltpu.SemaphoreType.DMA((row_count // 2 - 1,)),
        ],
        compiler_params=pltpu.CompilerParams(vmem_limit_bytes=FULL),
        name="rezone",
    )(*small, fractions_source, thermal_source_term)
    arrived = lax.all_to_all(outgoing, "row", split_axis=0, concat_axis=0, tiled=True)
    table = pl.pallas_call(
        table_kernel,
        out_shape=jax.ShapeDtypeStruct((-(-(2 * M + 3) // 8) * 8, LANES), F32),
        in_specs=[vmem] * 2,
        out_specs=vmem,
        compiler_params=params,
        name="table",
    )(conductivity_table, capacity)
    message = jax.ShapeDtypeStruct((pairs * TBLK + 2 * EDGE, width), F32)
    half = col_count // 2
    near, far = range(half), range(half, col_count)
    extended, *far_parts = pl.pallas_call(
        functools.partial(regroup_kernel, row_count, col_count, far),
        out_shape=[jax.ShapeDtypeStruct((zlayers, ROWS, width), F32)] + [message] * half,
        in_specs=[vmem] * 2,
        out_specs=[vmem] * (1 + half),
        compiler_params=params,
        name="regroup_far",
    )(arrived, thermal_source_term)

    def swap(part, mask):
        return lax.ppermute(part, "col", [(c, c ^ mask) for c in range(col_count)])

    far_parts = [swap(part, mask) for part, mask in zip(far_parts, far)]
    near_parts = pl.pallas_call(
        functools.partial(regroup_kernel, row_count, col_count, near),
        out_shape=[message] * half,
        in_specs=[vmem] * 3,
        out_specs=[vmem] * half,
        compiler_params=params,
        cost_estimate=pl.CostEstimate(flops=10**6, bytes_accessed=2 * 10**6, transcendentals=0),
        name="regroup_near",
    )(arrived, thermal_source_term, extended)
    parts = [swap(part, mask) if mask else part for part, mask in zip(near_parts, near)] + far_parts
    shares, basis, sums = pl.pallas_call(
        functools.partial(basis_kernel, col_count, height, breadth),
        out_shape=[
            jax.ShapeDtypeStruct((zlayers * M, height, breadth), F32),
            jax.ShapeDtypeStruct((ITERS, zlayers, height, breadth), F32),
            jax.ShapeDtypeStruct((row_count * col_count, 1, LANES), F32),
        ],
        in_specs=[vmem] * (2 + col_count),
        out_specs=[vmem] * 3,
        scratch_shapes=[pltpu.VMEM((col_count, *message.shape), F32)],
        compiler_params=params,
        name="basis",
    )(table, extended, *parts)
    sums = lax.all_to_all(sums, ("row", "col"), split_axis=0, concat_axis=0, tiled=True)
    thermal_iterate, remaining_defect, rezoned_occupancy_shares = pl.pallas_call(
        finish_kernel,
        out_shape=[jax.ShapeDtypeStruct((zlayers, height, breadth), F32)] * 2
        + [jax.ShapeDtypeStruct(shares.shape, F32)],
        in_specs=[vmem] * 5,
        out_specs=[hbm] * 3,
        scratch_shapes=[pltpu.VMEM((zlayers, height, breadth), F32)] * 2
        + [pltpu.SemaphoreType.DMA((3,))],
        compiler_params=params,
        name="finish",
    )(table, sums, thermal_source_term, basis, shares)
    return rezoned_occupancy_shares, thermal_iterate, remaining_defect


def solution(mesh):
    placed = (P("col", "row", None), P(), P(), P(), P(), P(), P(), P(None, "row", "col"))
    return jax.shard_map(
        functools.partial(per_device, mesh.shape["row"], mesh.shape["col"]),
        mesh=mesh,
        in_specs=placed,
        out_specs=(P(None, "row", "col"), P(None, "row", "col"), P(None, "row", "col")),
        check_vma=False,
    )
```

```python
import functools

import jax
import jax.numpy as jnp
from jax import lax
from jax.experimental import pallas as pl
from jax.experimental.pallas import tpu as pltpu
from jax.sharding import PartitionSpec as P

M = 6
SBLK = 64
TBLK = 48
ITERS = 3
RIM = ITERS
ROWS = 56
LANES = 128
EDGE = ROWS - TBLK
GROUPS = TBLK // 8
TAIL = 16
CHUNK = LANES - GROUPS * TAIL
BODY = ROWS + 8
VMEM = 48 * 1024 * 1024
FULL = 63 * 1024 * 1024
TINY = 1e-30
F32 = jnp.float32
BF16 = jnp.bfloat16


def tiles(cells):
    return -(-cells // LANES)


def compact(breadth):
    return breadth == 3 * CHUNK


def pack_rims(rims):
    count = rims.shape[0]
    side = jnp.zeros((count, LANES - CHUNK), F32)
    below = jnp.zeros((8 - count, LANES), F32)
    tail = jnp.concatenate([side, rims[:, 0:CHUNK]], axis=1)
    edge = jnp.concatenate([side, rims[:, CHUNK : 2 * CHUNK]], axis=1)
    lines = []
    for at in (0, RIM):
        parts = [rims[at + n : at + n + 1, 2 * CHUNK :] for n in range(RIM)]
        lines.append(jnp.concatenate(parts + [jnp.zeros((1, CHUNK), F32)], axis=1))
    gap = [jnp.zeros((RIM, LANES), F32)] + lines + [jnp.zeros((EDGE - RIM - 2, LANES), F32)]
    return (
        jnp.concatenate([tail, below], axis=0),
        jnp.concatenate([edge, below], axis=0) + jnp.concatenate(gap, axis=0),
    )


def unpack_rims(tail, edge, count):
    last = [
        edge[RIM + n // RIM : RIM + n // RIM + 1, CHUNK * (n % RIM) : CHUNK * (n % RIM + 1)]
        for n in range(count)
    ]
    parts = [tail[0:count, LANES - CHUNK :], edge[0:count, LANES - CHUNK :]]
    return jnp.concatenate(parts + [jnp.concatenate(last, axis=0)], axis=1)


def product(lengths, dense, contract):
    count = lengths.shape[0]
    high = lengths.astype(BF16)
    low = (lengths - high.astype(F32)).astype(BF16)
    both = jnp.concatenate([high, low], axis=0)
    first = dense.astype(BF16)
    rest = dense - first.astype(F32)
    second = rest.astype(BF16)
    third = (rest - second.astype(F32)).astype(BF16)

    def dot(left, right):
        return lax.dot_general(
            left, right, (((1,), (contract,)), ((), ())), preferred_element_type=F32
        )

    total = dot(high, third)
    for piece in (second, first):
        part = dot(both, piece)
        total = (total + part[count:]) + part[:count]
    return total


def rezone_kernel(
    row_count,
    xs_hbm,
    xt_hbm,
    ys_hbm,
    yt_hbm,
    cond_hbm,
    heat_hbm,
    frac_hbm,
    field_hbm,
    out_hbm,
    xs_ref,
    xt_ref,
    ys_ref,
    yt_ref,
    cond_ref,
    heat_ref,
    frac_ref,
    field_ref,
    edges_ref,
    along_ref,
    out_ref,
    sems,
    out_sems,
):
    me = lax.axis_index("row")
    pairs = frac_ref.shape[0]
    moves = [
        pltpu.make_async_copy(here, there, sems.at[n])
        for n, (here, there) in enumerate(
            (
                (yt_hbm, yt_ref),
                (xt_hbm, xt_ref),
                (xs_hbm, xs_ref),
                (ys_hbm, ys_ref),
                (frac_hbm, frac_ref),
                (field_hbm, field_ref),
                (cond_hbm, cond_ref),
                (heat_hbm, heat_ref),
            )
        )
    ]
    for move in moves:
        move.start()
    edges_ref[...] = jnp.zeros_like(edges_ref)
    used = (pairs + 2) * TBLK
    along_ref[used:, :] = jnp.zeros_like(along_ref[used:, :])
    for n, ref in enumerate((yt_ref, xt_ref, xs_ref, ys_ref)):
        moves[n].wait()
        edges_ref[n : n + 1, 0 : ref.shape[0]] = ref[...].astype(F32)[None, :]

    def from_here(row, start, lane):
        base = start // LANES * LANES
        if not isinstance(base, int):
            base = pl.multiple_of(base, LANES)
        window = edges_ref[row : row + 1, pl.ds(base, 2 * LANES)]
        return pltpu.roll(window, (lane - (start - base) + 2 * LANES) % (2 * LANES), 1)

    groups = tiles(row_count * TBLK)
    mine = from_here(1, me * TBLK, 0)
    lines = [
        edges_ref[0:1, LANES * g + ahead : LANES * (g + 1) + ahead]
        for ahead in (0, 1)
        for g in range(groups)
    ] + [turned[:, 0:LANES] for turned in (mine, pltpu.roll(mine, 2 * LANES - 1, 1))]
    spare = -len(lines) % 8
    if spare:
        lines.append(jnp.zeros((spare, LANES), F32))
    columns = jnp.transpose(jnp.concatenate(lines, axis=0))

    def shared(src_lo, src_hi, low, high):
        return jnp.maximum(jnp.minimum(src_hi, high) - jnp.maximum(src_lo, low), 0.0)

    lane = lax.broadcasted_iota(jnp.int32, (1, LANES), 1)
    x_lo = from_here(2, me * SBLK, 0)
    x_hi = pltpu.roll(x_lo, 2 * LANES - 1, 1)
    low = columns[0:TBLK, 2 * groups : 2 * groups + 1]
    high = columns[0:TBLK, 2 * groups + 1 : 2 * groups + 2]
    shared_x = shared(x_lo[:, 0:SBLK], x_hi[:, 0:SBLK], low, high)
    scale_x = 1.0 / (high - low)
    moves[5].wait()
    moves[6].wait()
    moves[7].wait()
    zlayers, height, breadth = field_ref.shape
    rims = []
    for rows in (slice(0, RIM), slice(height - RIM, height)):
        rims.append(jnp.concatenate([field_ref[layer, rows] for layer in range(zlayers)], axis=0))
    if compact(breadth):
        rims = [pack_rims(rim) for rim in rims]
    else:
        for r in range(row_count):
            rim = jnp.where(r > me, rims[1], rims[0])
            for t in range(tiles(breadth)):
                lo, hi = t * LANES, min((t + 1) * LANES, breadth)
                at = BODY + 8 * t
                out_ref[r, at : at + zlayers * RIM, 0 : hi - lo] = rim[:, lo:hi]
    resistance = 16.0 / cond_ref[...].astype(F32)[None, :]
    material = lax.broadcasted_iota(jnp.int32, (1, M), 1)
    factors = []
    for p in range(pairs):
        mine = material == lax.rem(lax.axis_index("col") * pairs + p, M)
        factors.append(
            [
                jnp.sum(jnp.where(mine, value, 0.0), axis=1, keepdims=True)
                for value in (resistance, heat_ref[...][None, :])
            ]
        )
    moves[4].wait()
    partial = [0.0, 0.0]
    for p in range(pairs):
        along = product(shared_x, frac_ref[p], 0) * scale_x
        along_ref[p * TBLK : (p + 1) * TBLK, :] = along
        partial = [total + factor * along for total, factor in zip(partial, factors[p])]
    for n, total in enumerate(partial):
        along_ref[(pairs + n) * TBLK : (pairs + n + 1) * TBLK, :] = total
    per, unit = 4, 64
    width = per * SBLK
    shared_y, scale_y = [], []
    for q in range(row_count // per):
        src_lo = edges_ref[3:4, q * width : (q + 1) * width]
        src_hi = edges_ref[3:4, q * width + 1 : (q + 1) * width + 1]
        parts, scales = [], []
        for start in range(q * per * TBLK, (q + 1) * per * TBLK, unit):
            g, at = divmod(start, LANES)
            low = columns[at : at + unit, g : g + 1]
            high = columns[at : at + unit, groups + g : groups + g + 1]
            parts.append(shared(src_lo, src_hi, low, high))
            scales.append(1.0 / (high - low))
        shared_y.append(jnp.concatenate(parts, axis=0))
        scale_y.append(jnp.concatenate(scales, axis=0))
    row = lax.broadcasted_iota(jnp.int32, (8, LANES), 0)
    leaving, firsts, lasts, sent = [], [], [], 0
    for q in range(row_count // per):
        block = product(shared_y[q], along_ref[:, q * width : (q + 1) * width], 1) * scale_y[q]
        for n in range(per):
            r = q * per + n
            mine = block[n * TBLK : (n + 1) * TBLK]
            out_ref[r, 0:TBLK, :] = mine[:, 0:LANES]
            packed = jnp.where(lane < TAIL, mine[0:8, LANES:], 0.0)
            for g in range(1, GROUPS):
                group = jnp.where(lane < TAIL, mine[8 * g : 8 * g + 8, LANES:], 0.0)
                packed = packed + pltpu.roll(group, TAIL * g, 1)
            if compact(breadth):
                packed = packed + jnp.where(r > me, rims[1][0], rims[0][0])
            out_ref[r, TBLK : TBLK + 8, :] = packed
            firsts.append(mine[0:8, LANES:])
            lasts.append(mine[TBLK - 8 :, LANES:])
        ready = row_count if r + 1 == row_count else r
        for r in range(sent, ready):
            edge = jnp.zeros((8, LANES), F32)
            if r + 1 < row_count:
                edge = jnp.where(row < RIM, firsts[r + 1], edge)
            if r:
                edge = jnp.where(row >= 8 - RIM, lasts[r - 1], edge)
            edge = jnp.where(lane < 2 * TBLK, pltpu.roll(edge, LANES - TAIL, 1), 0.0)
            if compact(breadth):
                edge = edge + jnp.where(r > me, rims[1][1], rims[0][1])
            out_ref[r, ROWS:BODY, :] = edge
        done = pl.ds(sent, ready - sent)
        leaving.append(pltpu.make_async_copy(out_ref.at[done], out_hbm.at[done], out_sems.at[q]))
        leaving[-1].start()
        sent = ready
    for move in leaving:
        move.wait()


def table_kernel(cond_ref, heat_ref, table_ref):
    resistance = 16.0 / cond_ref[...].astype(F32)[None, :]
    heat = heat_ref[...][None, :]
    middle = 5.0 * M / jnp.sum(resistance, axis=1, keepdims=True)
    shift = jnp.sum(heat, axis=1, keepdims=True) / M + middle
    rest = jnp.zeros((1, LANES - 2 * M - 3), F32)
    table = jnp.concatenate([resistance, heat, shift, 1.0 / middle, middle, rest], axis=1)
    table = jnp.transpose(jnp.broadcast_to(table, (LANES, LANES)))
    table_ref[...] = table[0 : table_ref.shape[0]]


def extend_rows(row_count, got_ref, field_ref, ext_ref):
    my_row = lax.axis_index("row")
    zlayers, height, breadth = field_ref.shape
    ext_ref[...] = jnp.zeros_like(ext_ref)
    below, above = jnp.maximum(my_row - 1, 0), jnp.minimum(my_row + 1, row_count - 1)
    count = zlayers * RIM
    for block, there, at in (
        (above, my_row < row_count - 1, height),
        (below, my_row > 0, ROWS - RIM),
    ):
        if compact(breadth):
            rims = unpack_rims(got_ref[block, TBLK : TBLK + 8], got_ref[block, ROWS:BODY], count)
        else:
            parts = [got_ref[block, BODY + 8 * t : BODY + 8 * t + count] for t in range(tiles(breadth))]
            rims = jnp.concatenate(parts, axis=1)[:, 0:breadth]
        rims = jnp.where(there, rims, 0.0)
        for layer in range(zlayers):
            ext_ref[layer, at : at + RIM, 0:breadth] = rims[layer * RIM : (layer + 1) * RIM]
    for layer in range(zlayers):
        ext_ref[layer, 0:height, 0:breadth] = field_ref[layer]


def regroup_kernel(row_count, col_count, masks, got_ref, field_ref, *refs):
    my_col = lax.axis_index("col")
    zlayers, _, breadth = field_ref.shape
    ext_ref, out_refs = refs[0], refs[1:]
    width = out_refs[0].shape[1]
    pairs = out_refs[0].shape[0] // TBLK
    per_col = row_count // col_count
    if col_count // 2 in masks:
        extend_rows(row_count, got_ref, field_ref, ext_ref)

    def own(block, pair, first, last):
        lo, hi = pair * TBLK + first, pair * TBLK + last
        parts = []
        if lo < LANES:
            parts.append(got_ref[block, 0:TBLK, lo : min(hi, LANES)])
        if hi > LANES:
            a, b = max(lo, LANES) - LANES, hi - LANES
            tail = got_ref[block, TBLK : TBLK + 8, :]
            parts.append(
                jnp.concatenate([tail[:, TAIL * g + a : TAIL * g + b] for g in range(GROUPS)], axis=0)
            )
        return parts[0] if len(parts) == 1 else jnp.concatenate(parts, axis=1)

    def edge(block, which, first, last):
        return got_ref[block, ROWS:BODY, which * TBLK + first : which * TBLK + last]

    for mask, out_ref in zip(masks, out_refs):
        c = my_col ^ mask
        start = c * per_col
        left, right = jnp.maximum(start - 1, 0), jnp.minimum(start + per_col, row_count - 1)

        def line(cells, rows, kind, layer):
            parts = [cells(start + j, kind, 0, TBLK) for j in range(per_col)]
            count = parts[0].shape[0]
            parts.append(jnp.where(c < col_count - 1, cells(right, kind, 0, RIM), 0.0))
            if layer < zlayers and mask:
                whole = ext_ref[layer, rows]
                parts.append(
                    jnp.where(c > my_col, whole[:, breadth - RIM : breadth], whole[:, 0:RIM])
                )
            else:
                parts.append(jnp.zeros((count, RIM), F32))
            parts.append(jnp.zeros((count, width - breadth - 3 * RIM), F32))
            parts.append(jnp.where(c > 0, cells(left, kind, TBLK - RIM, TBLK), 0.0))
            return jnp.concatenate(parts, axis=1)

        for p in range(pairs):
            out_ref[p * TBLK : (p + 1) * TBLK] = line(own, slice(0, TBLK), p, p)
        for n in range(2):
            at = pairs * TBLK + EDGE * n
            out_ref[at : at + EDGE] = line(edge, slice(TBLK, ROWS), n, n)


def basis_kernel(col_count, height, breadth, table_ref, ext_ref, *refs):
    arrivals, refs = refs[:col_count], refs[col_count:]
    shares_ref, basis_ref, sums_ref, got_ref = refs
    my_col = lax.axis_index("col")
    pairs = arrivals[0].shape[0] // TBLK
    for mask, arrival in enumerate(arrivals):
        got_ref[my_col ^ mask] = arrival[...]
        for p in range(pairs):
            at = (my_col ^ mask) * pairs + p
            shares_ref[at] = arrival[p * TBLK : (p + 1) * TBLK, 0:breadth]
    zlayers = ext_ref.shape[0]
    rows, width = ext_ref.shape[1:]
    lane = lax.broadcasted_iota(jnp.int32, (rows, width), 1)
    before, after = jnp.maximum(my_col - 1, 0), jnp.minimum(my_col + 1, col_count - 1)

    def ahead(array, axis):
        return pltpu.roll(array, array.shape[axis] - 1, axis)

    def behind(array, axis):
        return pltpu.roll(array, 1, axis)

    def face(one, other):
        return 2.0 * one * other / jnp.maximum(one + other, TINY)

    def entry(n):
        return table_ref[n : n + 1, 0:1]

    row = lax.broadcasted_iota(jnp.int32, (rows, width), 0)
    inside = ((lane < breadth + RIM) | (lane >= width - RIM)) & (
        (row < TBLK + RIM) | (row >= ROWS - RIM)
    )

    cell_k, heat, field = [], [], []
    for z in range(zlayers):
        inverse, total = 0.0, 0.0
        for m in range(M):
            c, p = divmod(z * M + m, pairs)
            share = got_ref[c, p * TBLK : (p + 1) * TBLK]
            inverse = inverse + share * entry(m)
            total = total + share * entry(M + m)
        edge_inverse, edge_total = 0.0, 0.0
        for c in range(z * M // pairs, (z + 1) * M // pairs):
            edge_inverse = edge_inverse + got_ref[c, pairs * TBLK : pairs * TBLK + EDGE]
            edge_total = edge_total + got_ref[c, pairs * TBLK + EDGE :]
        inverse = jnp.concatenate([inverse, edge_inverse], axis=0)
        total = jnp.concatenate([total, edge_total], axis=0)
        inverse, total = (jnp.where(inside, value, 0.0) for value in (inverse, total))
        cell_k.append(jnp.where(inverse > 0.0, 1.0 / jnp.where(inverse > 0.0, inverse, 1.0), 0.0))
        heat.append(total)
        left, right = (
            jnp.concatenate(
                [
                    got_ref[c, z * TBLK : (z + 1) * TBLK],
                    got_ref[c, pairs * TBLK + EDGE * z : pairs * TBLK + EDGE * (z + 1)],
                ],
                axis=0,
            )
            for c in (before, after)
        )
        left = pltpu.roll(left, width - (breadth + 2 * RIM), 1)
        right = pltpu.roll(right, width - RIM, 1)
        value = ext_ref[z]
        value = jnp.where(
            (lane >= breadth) & (lane < breadth + RIM) & (my_col < col_count - 1), right, value
        )
        value = jnp.where((lane >= width - RIM) & (my_col > 0), left, value)
        field.append(value)
    face_x = [face(k, ahead(k, 1)) for k in cell_k]
    face_y = [face(k, ahead(k, 0)) for k in cell_k]
    face_z = [face(cell_k[z], cell_k[z + 1]) for z in range(zlayers - 1)]

    def operate(w):
        result = []
        for z in range(zlayers):
            flow_x = face_x[z] * (w[z] - ahead(w[z], 1))
            flow_y = face_y[z] * (w[z] - ahead(w[z], 0))
            value = heat[z] * w[z] + (flow_x - behind(flow_x, 1)) + (flow_y - behind(flow_y, 0))
            if z + 1 < zlayers:
                value = value + face_z[z] * (w[z] - w[z + 1])
            if z:
                value = value - face_z[z - 1] * (w[z - 1] - w[z])
            result.append(value)
        return result

    shift, scale = entry(2 * M), entry(2 * M + 1)

    def shifted(w):
        return [(a - shift * b) * scale for a, b in zip(operate(w), w)]

    basis = [field, shifted(field)]
    for _ in range(ITERS - 1):
        basis.append([2.0 * a - b for a, b in zip(shifted(basis[-1]), basis[-2])])
    own = [
        [jnp.where(lane < breadth, layer, 0.0)[0:height] for layer in vector] for vector in basis
    ]
    for n in range(ITERS):
        for z in range(zlayers):
            basis_ref[n, z] = own[n + 1][z][:, 0:breadth]
    slot = lax.broadcasted_iota(jnp.int32, (1, LANES), 1)
    packed = jnp.zeros((1, LANES), F32)
    at = 0
    for a in range(ITERS + 1):
        for b in range(a, ITERS + 1):
            product = own[a][0] * own[b][0]
            for z in range(1, zlayers):
                product = product + own[a][z] * own[b][z]
            value = jnp.sum(product, axis=0, keepdims=True)
            value = jnp.sum(value, axis=1, keepdims=True)
            packed = packed + jnp.where(slot == at, value, 0.0)
            at += 1
    sums_ref[...] = jnp.broadcast_to(packed[None], sums_ref.shape)


def finish_kernel(
    table_ref,
    sums_ref,
    field_ref,
    basis_ref,
    shares_ref,
    iterate_hbm,
    defect_hbm,
    shares_hbm,
    iterate_ref,
    defect_ref,
    sems,
):
    pairs = (shares_ref, shares_hbm), (iterate_ref, iterate_hbm), (defect_ref, defect_hbm)
    leaving = [pltpu.make_async_copy(*pair, sems.at[n]) for n, pair in enumerate(pairs)]
    leaving[0].start()
    total = jnp.sum(sums_ref[...], axis=0)
    gram = {}
    at = 0
    for a in range(ITERS + 1):
        for b in range(a, ITERS + 1):
            gram[a, b] = gram[b, a] = total[:, at : at + 1]
            at += 1
    shift, scale = (table_ref[n : n + 1, 0:1] for n in (2 * M, 2 * M + 2))

    def inner(left, right):
        rows = []
        for a, one in left.items():
            rows.append(one * total_of([other * gram[a, b] for b, other in right.items()]))
        return total_of(rows)

    def total_of(terms):
        while len(terms) > 1:
            terms = [sum(terms[n : n + 2][1:], terms[n]) for n in range(0, len(terms), 2)]
        return terms[0]

    def combine(left, factor, right):
        result = dict(left)
        for a, one in right.items():
            result[a] = result[a] + factor * one if a in result else factor * one
        return result

    def apply(vector):
        result = {}
        for a, one in vector.items():
            if a:
                moved = {a - 1: 0.5 * scale * one, a: shift * one, a + 1: 0.5 * scale * one}
            else:
                moved = {0: shift * one, 1: scale * one}
            for b, other in moved.items():
                result[b] = result[b] + other if b in result else other
        return result

    one = jnp.ones((1, 1), F32)
    iterate, defect, direction = {}, {0: one}, {0: one}
    norm = gram[0, 0]
    for iteration in range(ITERS):
        applied = apply(direction)
        step = norm / inner(direction, applied)
        iterate = combine(iterate, step, direction)
        defect = combine(defect, -step, applied)
        if iteration + 1 < ITERS:
            following = inner(defect, defect)
            direction = combine(defect, following / norm, direction)
            norm = following
    for ref, weights, move in ((iterate_ref, iterate, leaving[1]), (defect_ref, defect, leaving[2])):
        for z in range(field_ref.shape[0]):
            vectors = [field_ref[z]] + [basis_ref[n, z] for n in range(ITERS)]
            ref[z] = total_of([weight * vectors[a] for a, weight in weights.items()])
        move.start()
    for move in leaving:
        move.wait()


def per_device(
    row_count,
    col_count,
    fractions_source,
    x_source_edges,
    x_target_edges,
    y_source_edges,
    y_target_edges,
    conductivity_table,
    capacity,
    thermal_source_term,
):
    pairs, _, source_cells = fractions_source.shape
    zlayers, height, breadth = thermal_source_term.shape
    width = LANES * tiles(breadth + 4 * RIM)
    send_rows = BODY + (0 if compact(breadth) else 8 * tiles(breadth))
    params = pltpu.CompilerParams(vmem_limit_bytes=VMEM)

    vmem = pl.BlockSpec(memory_space=pltpu.VMEM)
    hbm = pl.BlockSpec(memory_space=pltpu.HBM)
    along_rows = -(-(pairs + 2) * TBLK // LANES) * LANES
    small = [
        x_source_edges,
        x_target_edges,
        y_source_edges,
        y_target_edges,
        conductivity_table,
        capacity,
    ]
    outgoing = jax.ShapeDtypeStruct((row_count, send_rows, LANES), F32)
    outgoing = pl.pallas_call(
        functools.partial(rezone_kernel, row_count),
        out_shape=outgoing,
        in_specs=[hbm] * 8,
        out_specs=hbm,
        scratch_shapes=[pltpu.VMEM(e.shape, e.dtype) for e in small]
        + [
            pltpu.VMEM(fractions_source.shape, F32),
            pltpu.VMEM(thermal_source_term.shape, F32),
            pltpu.VMEM((8, LANES * (tiles(source_cells + 1) + 1)), F32),
            pltpu.VMEM((along_rows, source_cells), F32),
            pltpu.VMEM(outgoing.shape, F32),
            pltpu.SemaphoreType.DMA((8,)),
            pltpu.SemaphoreType.DMA((row_count // 4,)),
        ],
        compiler_params=pltpu.CompilerParams(vmem_limit_bytes=FULL),
        name="rezone",
    )(*small, fractions_source, thermal_source_term)
    arrived = lax.all_to_all(outgoing, "row", split_axis=0, concat_axis=0, tiled=True)
    table = pl.pallas_call(
        table_kernel,
        out_shape=jax.ShapeDtypeStruct((-(-(2 * M + 3) // 8) * 8, LANES), F32),
        in_specs=[vmem] * 2,
        out_specs=vmem,
        compiler_params=params,
        name="table",
    )(conductivity_table, capacity)
    message = jax.ShapeDtypeStruct((pairs * TBLK + 2 * EDGE, width), F32)
    half = col_count // 2
    near, far = range(half), range(half, col_count)
    extended, *far_parts = pl.pallas_call(
        functools.partial(regroup_kernel, row_count, col_count, far),
        out_shape=[jax.ShapeDtypeStruct((zlayers, ROWS, width), F32)] + [message] * half,
        in_specs=[vmem] * 2,
        out_specs=[vmem] * (1 + half),
        compiler_params=params,
        name="regroup_far",
    )(arrived, thermal_source_term)

    def swap(part, mask):
        return lax.ppermute(part, "col", [(c, c ^ mask) for c in range(col_count)])

    far_parts = [swap(part, mask) for part, mask in zip(far_parts, far)]
    near_parts = pl.pallas_call(
        functools.partial(regroup_kernel, row_count, col_count, near),
        out_shape=[message] * half,
        in_specs=[vmem] * 3,
        out_specs=[vmem] * half,
        compiler_params=params,
        cost_estimate=pl.CostEstimate(flops=10**6, bytes_accessed=2 * 10**6, transcendentals=0),
        name="regroup_near",
    )(arrived, thermal_source_term, extended)
    parts = [swap(part, mask) if mask else part for part, mask in zip(near_parts, near)] + far_parts
    shares, basis, sums = pl.pallas_call(
        functools.partial(basis_kernel, col_count, height, breadth),
        out_shape=[
            jax.ShapeDtypeStruct((zlayers * M, height, breadth), F32),
            jax.ShapeDtypeStruct((ITERS, zlayers, height, breadth), F32),
            jax.ShapeDtypeStruct((row_count * col_count, 1, LANES), F32),
        ],
        in_specs=[vmem] * (2 + col_count),
        out_specs=[vmem] * 3,
        scratch_shapes=[pltpu.VMEM((col_count, *message.shape), F32)],
        compiler_params=params,
        name="basis",
    )(table, extended, *parts)
    sums = lax.all_to_all(sums, ("row", "col"), split_axis=0, concat_axis=0, tiled=True)
    thermal_iterate, remaining_defect, rezoned_occupancy_shares = pl.pallas_call(
        finish_kernel,
        out_shape=[jax.ShapeDtypeStruct((zlayers, height, breadth), F32)] * 2
        + [jax.ShapeDtypeStruct(shares.shape, F32)],
        in_specs=[vmem] * 5,
        out_specs=[hbm] * 3,
        scratch_shapes=[pltpu.VMEM((zlayers, height, breadth), F32)] * 2
        + [pltpu.SemaphoreType.DMA((3,))],
        compiler_params=params,
        name="finish",
    )(table, sums, thermal_source_term, basis, shares)
    return rezoned_occupancy_shares, thermal_iterate, remaining_defect


def solution(mesh):
    placed = (P("col", "row", None), P(), P(), P(), P(), P(), P(), P(None, "row", "col"))
    return jax.shard_map(
        functools.partial(per_device, mesh.shape["row"], mesh.shape["col"]),
        mesh=mesh,
        in_specs=placed,
        out_specs=(P(None, "row", "col"), P(None, "row", "col"), P(None, "row", "col")),
        check_vma=False,
    )
```

```python
import functools

import jax
import jax.numpy as jnp
from jax import lax
from jax.experimental import pallas as pl
from jax.experimental.pallas import tpu as pltpu
from jax.sharding import PartitionSpec as P

M = 6
SBLK = 64
TBLK = 48
ITERS = 3
RIM = ITERS
ROWS = 56
LANES = 128
EDGE = ROWS - TBLK
HALF = TBLK // 2
KEPT = 2 * TBLK + HALF
CHUNK = LANES - 2 * TBLK
BODY = ROWS
VMEM = 48 * 1024 * 1024
FULL = 63 * 1024 * 1024
TINY = 1e-30
F32 = jnp.float32
BF16 = jnp.bfloat16


def tiles(cells):
    return -(-cells // LANES)


def compact(breadth):
    return breadth == 3 * CHUNK


def pack_rims(rims):
    count, spare = rims.shape[0], LANES - KEPT
    below = jnp.zeros((8 - count, LANES), F32)
    side = jnp.zeros((count, KEPT), F32)
    own = []
    for at in range(CHUNK, 2 * CHUNK, spare):
        own += [jnp.concatenate([side, rims[:, at : at + spare]], axis=1), below]
    own.append(jnp.zeros((TBLK - 8 * CHUNK // spare, LANES), F32))
    edge = jnp.concatenate([jnp.zeros((count, LANES - CHUNK), F32), rims[:, 0:CHUNK]], axis=1)
    lines = []
    for at in (0, RIM):
        parts = [rims[at + n : at + n + 1, 2 * CHUNK :] for n in range(RIM)]
        lines.append(jnp.concatenate(parts + [jnp.zeros((1, CHUNK), F32)], axis=1))
    gap = [jnp.zeros((RIM, LANES), F32)] + lines + [jnp.zeros((EDGE - RIM - 2, LANES), F32)]
    return (
        jnp.concatenate(own, axis=0),
        jnp.concatenate([edge, below], axis=0) + jnp.concatenate(gap, axis=0),
    )


def unpack_rims(own, edge, count):
    spare = LANES - KEPT
    last = [
        edge[RIM + n // RIM : RIM + n // RIM + 1, CHUNK * (n % RIM) : CHUNK * (n % RIM + 1)]
        for n in range(count)
    ]
    middle = [own[8 * n : 8 * n + count, KEPT:] for n in range(CHUNK // spare)]
    parts = [edge[0:count, LANES - CHUNK :]] + middle + [jnp.concatenate(last, axis=0)]
    return jnp.concatenate(parts, axis=1)


def product(lengths, dense, contract):
    count = lengths.shape[0]
    high = lengths.astype(BF16)
    low = (lengths - high.astype(F32)).astype(BF16)
    both = jnp.concatenate([high, low], axis=0)
    first = dense.astype(BF16)
    rest = dense - first.astype(F32)
    second = rest.astype(BF16)
    third = (rest - second.astype(F32)).astype(BF16)

    def dot(left, right):
        return lax.dot_general(
            left, right, (((1,), (contract,)), ((), ())), preferred_element_type=F32
        )

    total = dot(high, third)
    for piece in (second, first):
        part = dot(both, piece)
        total = (total + part[count:]) + part[:count]
    return total


def rezone_kernel(
    row_count,
    xs_hbm,
    xt_hbm,
    ys_hbm,
    yt_hbm,
    cond_hbm,
    heat_hbm,
    frac_hbm,
    field_hbm,
    out_hbm,
    xs_ref,
    xt_ref,
    ys_ref,
    yt_ref,
    cond_ref,
    heat_ref,
    frac_ref,
    field_ref,
    edges_ref,
    along_ref,
    out_ref,
    sems,
    out_sems,
):
    me = lax.axis_index("row")
    pairs = frac_ref.shape[0]
    moves = [
        pltpu.make_async_copy(here, there, sems.at[n])
        for n, (here, there) in enumerate(
            (
                (yt_hbm, yt_ref),
                (xt_hbm, xt_ref),
                (xs_hbm, xs_ref),
                (ys_hbm, ys_ref),
                (frac_hbm, frac_ref),
                (field_hbm, field_ref),
                (cond_hbm, cond_ref),
                (heat_hbm, heat_ref),
            )
        )
    ]
    for move in moves:
        move.start()
    edges_ref[...] = jnp.zeros_like(edges_ref)
    for rows in (slice(KEPT, LANES), slice(LANES + 2 * TBLK, along_ref.shape[0])):
        along_ref[rows, :] = jnp.zeros_like(along_ref[rows, :])
    for n, ref in enumerate((yt_ref, xt_ref, xs_ref, ys_ref)):
        moves[n].wait()
        edges_ref[n : n + 1, 0 : ref.shape[0]] = ref[...].astype(F32)[None, :]

    def from_here(row, start, lane):
        base = start // LANES * LANES
        if not isinstance(base, int):
            base = pl.multiple_of(base, LANES)
        window = edges_ref[row : row + 1, pl.ds(base, 2 * LANES)]
        return pltpu.roll(window, (lane - (start - base) + 2 * LANES) % (2 * LANES), 1)

    groups = tiles(row_count * TBLK)
    mine = from_here(1, me * TBLK, 0)
    lines = [
        edges_ref[0:1, LANES * g + ahead : LANES * (g + 1) + ahead]
        for ahead in (0, 1)
        for g in range(groups)
    ] + [turned[:, 0:LANES] for turned in (mine, pltpu.roll(mine, 2 * LANES - 1, 1))]
    spare = -len(lines) % 8
    if spare:
        lines.append(jnp.zeros((spare, LANES), F32))
    columns = jnp.transpose(jnp.concatenate(lines, axis=0))

    def shared(src_lo, src_hi, low, high):
        return jnp.maximum(jnp.minimum(src_hi, high) - jnp.maximum(src_lo, low), 0.0)

    lane = lax.broadcasted_iota(jnp.int32, (1, LANES), 1)
    x_lo = from_here(2, me * SBLK, 0)
    x_hi = pltpu.roll(x_lo, 2 * LANES - 1, 1)
    low = columns[0:TBLK, 2 * groups : 2 * groups + 1]
    high = columns[0:TBLK, 2 * groups + 1 : 2 * groups + 2]
    shared_x = shared(x_lo[:, 0:SBLK], x_hi[:, 0:SBLK], low, high)
    scale_x = 1.0 / (high - low)
    moves[5].wait()
    moves[6].wait()
    moves[7].wait()
    zlayers, height, breadth = field_ref.shape
    rims = []
    for rows in (slice(0, RIM), slice(height - RIM, height)):
        rims.append(jnp.concatenate([field_ref[layer, rows] for layer in range(zlayers)], axis=0))
    if compact(breadth):
        rims = [pack_rims(rim) for rim in rims]
    else:
        for r in range(row_count):
            rim = jnp.where(r > me, rims[1], rims[0])
            for t in range(tiles(breadth)):
                lo, hi = t * LANES, min((t + 1) * LANES, breadth)
                at = BODY + 8 * t
                out_ref[r, at : at + zlayers * RIM, 0 : hi - lo] = rim[:, lo:hi]
    resistance = 16.0 / cond_ref[...].astype(F32)[None, :]
    material = lax.broadcasted_iota(jnp.int32, (1, M), 1)
    factors = []
    for p in range(pairs):
        mine = material == lax.rem(lax.axis_index("col") * pairs + p, M)
        factors.append(
            [
                jnp.sum(jnp.where(mine, value, 0.0), axis=1, keepdims=True)
                for value in (resistance, heat_ref[...][None, :])
            ]
        )
    moves[4].wait()
    partial = [0.0, 0.0]
    for p in range(pairs):
        along = product(shared_x, frac_ref[p], 0) * scale_x
        if p + 1 < pairs:
            along_ref[p * TBLK : (p + 1) * TBLK, :] = along
        else:
            even = lax.rem(lax.axis_index("col"), 2) == 0
            along_ref[KEPT - HALF : KEPT, :] = jnp.where(even, along[0:HALF], along[HALF:])
        partial = [total + factor * along for total, factor in zip(partial, factors[p])]
    for n, total in enumerate(partial):
        along_ref[LANES + n * TBLK : LANES + (n + 1) * TBLK, :] = total
    per, unit = 4, 64
    width = per * SBLK
    shared_y, scale_y = [], []
    for q in range(row_count // per):
        src_lo = edges_ref[3:4, q * width : (q + 1) * width]
        src_hi = edges_ref[3:4, q * width + 1 : (q + 1) * width + 1]
        parts, scales = [], []
        for start in range(q * per * TBLK, (q + 1) * per * TBLK, unit):
            g, at = divmod(start, LANES)
            low = columns[at : at + unit, g : g + 1]
            high = columns[at : at + unit, groups + g : groups + g + 1]
            parts.append(shared(src_lo, src_hi, low, high))
            scales.append(1.0 / (high - low))
        shared_y.append(jnp.concatenate(parts, axis=0))
        scale_y.append(jnp.concatenate(scales, axis=0))
    row = lax.broadcasted_iota(jnp.int32, (8, LANES), 0)
    leaving, firsts, lasts, sent = [], [], [], 0
    for q in range(row_count // per):
        block = product(shared_y[q], along_ref[:, q * width : (q + 1) * width], 1) * scale_y[q]
        for n in range(per):
            r = q * per + n
            mine = block[n * TBLK : (n + 1) * TBLK]
            mine_own = mine[:, 0:LANES]
            if compact(breadth):
                mine_own = mine_own + jnp.where(r > me, rims[1][0], rims[0][0])
            out_ref[r, 0:TBLK, :] = mine_own
            firsts.append(mine[0:8, LANES:])
            lasts.append(mine[TBLK - 8 :, LANES:])
        ready = row_count if r + 1 == row_count else r
        for r in range(sent, ready):
            edge = jnp.zeros((8, LANES), F32)
            if r + 1 < row_count:
                edge = jnp.where(row < RIM, firsts[r + 1], edge)
            if r:
                edge = jnp.where(row >= 8 - RIM, lasts[r - 1], edge)
            edge = jnp.where(lane < 2 * TBLK, edge, 0.0)
            if compact(breadth):
                edge = edge + jnp.where(r > me, rims[1][1], rims[0][1])
            out_ref[r, TBLK:ROWS, :] = edge
        done = pl.ds(sent, ready - sent)
        leaving.append(pltpu.make_async_copy(out_ref.at[done], out_hbm.at[done], out_sems.at[q]))
        leaving[-1].start()
        sent = ready
    for move in leaving:
        move.wait()


def table_kernel(cond_ref, heat_ref, table_ref):
    resistance = 16.0 / cond_ref[...].astype(F32)[None, :]
    heat = heat_ref[...][None, :]
    middle = 5.0 * M / jnp.sum(resistance, axis=1, keepdims=True)
    shift = jnp.sum(heat, axis=1, keepdims=True) / M + middle
    rest = jnp.zeros((1, LANES - 2 * M - 3), F32)
    table = jnp.concatenate([resistance, heat, shift, 1.0 / middle, middle, rest], axis=1)
    table = jnp.transpose(jnp.broadcast_to(table, (LANES, LANES)))
    table_ref[...] = table[0 : table_ref.shape[0]]


def extend_rows(row_count, got_ref, field_ref, ext_ref):
    my_row = lax.axis_index("row")
    zlayers, height, breadth = field_ref.shape
    ext_ref[...] = jnp.zeros_like(ext_ref)
    below, above = jnp.maximum(my_row - 1, 0), jnp.minimum(my_row + 1, row_count - 1)
    count = zlayers * RIM
    for block, there, at in (
        (above, my_row < row_count - 1, height),
        (below, my_row > 0, ROWS - RIM),
    ):
        if compact(breadth):
            rims = unpack_rims(got_ref[block, 0:TBLK], got_ref[block, TBLK:ROWS], count)
        else:
            parts = [got_ref[block, BODY + 8 * t : BODY + 8 * t + count] for t in range(tiles(breadth))]
            rims = jnp.concatenate(parts, axis=1)[:, 0:breadth]
        rims = jnp.where(there, rims, 0.0)
        for layer in range(zlayers):
            ext_ref[layer, at : at + RIM, 0:breadth] = rims[layer * RIM : (layer + 1) * RIM]
    for layer in range(zlayers):
        ext_ref[layer, 0:height, 0:breadth] = field_ref[layer]


def regroup_kernel(row_count, col_count, masks, got_ref, field_ref, *refs):
    my_col = lax.axis_index("col")
    zlayers, _, breadth = field_ref.shape
    ext_ref, out_refs = refs[0], refs[1:]
    width = out_refs[0].shape[1]
    pairs = out_refs[0].shape[0] // TBLK
    per_col = row_count // col_count
    if col_count // 2 in masks:
        extend_rows(row_count, got_ref, field_ref, ext_ref)

    def own(block, pair, first, last):
        start = pair * TBLK
        if pair + 1 < pairs:
            return got_ref[block, 0:TBLK, start + first : start + last]
        if last - first == TBLK:
            half = got_ref[block, 0:TBLK, start : start + HALF]
            return jnp.concatenate([half, half], axis=1)
        first = first % HALF
        return got_ref[block, 0:TBLK, start + first : start + first + RIM]

    def edge(block, which, first, last):
        return got_ref[block, TBLK:ROWS, which * TBLK + first : which * TBLK + last]

    for mask, out_ref in zip(masks, out_refs):
        c = my_col ^ mask
        start = c * per_col
        left, right = jnp.maximum(start - 1, 0), jnp.minimum(start + per_col, row_count - 1)

        def line(cells, rows, kind, layer):
            parts = [cells(start + j, kind, 0, TBLK) for j in range(per_col)]
            count = parts[0].shape[0]
            parts.append(jnp.where(c < col_count - 1, cells(right, kind, 0, RIM), 0.0))
            if layer < zlayers and mask:
                whole = ext_ref[layer, rows]
                parts.append(
                    jnp.where(c > my_col, whole[:, breadth - RIM : breadth], whole[:, 0:RIM])
                )
            else:
                parts.append(jnp.zeros((count, RIM), F32))
            parts.append(jnp.zeros((count, width - breadth - 3 * RIM), F32))
            parts.append(jnp.where(c > 0, cells(left, kind, TBLK - RIM, TBLK), 0.0))
            return jnp.concatenate(parts, axis=1)

        for p in range(pairs):
            out_ref[p * TBLK : (p + 1) * TBLK] = line(own, slice(0, TBLK), p, p)
        for n in range(2):
            at = pairs * TBLK + EDGE * n
            out_ref[at : at + EDGE] = line(edge, slice(TBLK, ROWS), n, n)


def basis_kernel(col_count, height, breadth, table_ref, ext_ref, *refs):
    arrivals, refs = refs[:col_count], refs[col_count:]
    shares_ref, basis_ref, sums_ref, got_ref = refs
    my_col = lax.axis_index("col")
    pairs = arrivals[0].shape[0] // TBLK
    for mask, arrival in enumerate(arrivals):
        got_ref[my_col ^ mask] = arrival[...]
    zlayers = ext_ref.shape[0]
    rows, width = ext_ref.shape[1:]
    lane = lax.broadcasted_iota(jnp.int32, (rows, width), 1)
    before, after = jnp.maximum(my_col - 1, 0), jnp.minimum(my_col + 1, col_count - 1)

    def ahead(array, axis):
        return pltpu.roll(array, array.shape[axis] - 1, axis)

    def behind(array, axis):
        return pltpu.roll(array, 1, axis)

    def face(one, other):
        return 2.0 * one * other / jnp.maximum(one + other, TINY)

    def entry(n):
        return table_ref[n : n + 1, 0:1]

    row = lax.broadcasted_iota(jnp.int32, (rows, width), 0)
    to_right = (lane >= breadth) & (lane < breadth + RIM)
    to_left = lane >= width - RIM
    inside = (lane < breadth) | (to_right & (my_col < col_count - 1)) | (to_left & (my_col > 0))
    inside = inside & ((row < TBLK + RIM) | (row >= ROWS - RIM))
    early = ((lane < breadth) & (lax.rem(lane, TBLK) < HALF)) | to_right
    early = early[0:TBLK]

    cell_k, heat, field = [], [], []
    for z in range(zlayers):
        inverse, total = 0.0, 0.0
        shares = []
        for m in range(M):
            c, p = divmod(z * M + m, pairs)
            shares.append(got_ref[c, p * TBLK : (p + 1) * TBLK])
        known = jnp.where(early, shares[pairs - 1], shares[M - 1])
        missing = 1.0 - known
        for m in range(M):
            if m not in (pairs - 1, M - 1):
                missing = missing - shares[m]
        shares[pairs - 1] = jnp.where(early, known, missing)
        shares[M - 1] = jnp.where(early, missing, known)
        for m, share in enumerate(shares):
            shares_ref[z * M + m] = share[:, 0:breadth]
            inverse = inverse + share * entry(m)
            total = total + share * entry(M + m)
        edge_inverse, edge_total = 0.0, 0.0
        for c in range(z * M // pairs, (z + 1) * M // pairs):
            edge_inverse = edge_inverse + got_ref[c, pairs * TBLK : pairs * TBLK + EDGE]
            edge_total = edge_total + got_ref[c, pairs * TBLK + EDGE :]
        inverse = jnp.concatenate([inverse, edge_inverse], axis=0)
        total = jnp.concatenate([total, edge_total], axis=0)
        inverse, total = (jnp.where(inside, value, 0.0) for value in (inverse, total))
        cell_k.append(jnp.where(inverse > 0.0, 1.0 / jnp.where(inverse > 0.0, inverse, 1.0), 0.0))
        heat.append(total)
        left, right = (
            jnp.concatenate(
                [
                    got_ref[c, z * TBLK : (z + 1) * TBLK],
                    got_ref[c, pairs * TBLK + EDGE * z : pairs * TBLK + EDGE * (z + 1)],
                ],
                axis=0,
            )
            for c in (before, after)
        )
        left = pltpu.roll(left, width - (breadth + 2 * RIM), 1)
        right = pltpu.roll(right, width - RIM, 1)
        value = ext_ref[z]
        value = jnp.where(
            (lane >= breadth) & (lane < breadth + RIM) & (my_col < col_count - 1), right, value
        )
        value = jnp.where((lane >= width - RIM) & (my_col > 0), left, value)
        field.append(value)
    face_x = [face(k, ahead(k, 1)) for k in cell_k]
    face_y = [face(k, ahead(k, 0)) for k in cell_k]
    face_z = [face(cell_k[z], cell_k[z + 1]) for z in range(zlayers - 1)]

    def operate(w):
        result = []
        for z in range(zlayers):
            flow_x = face_x[z] * (w[z] - ahead(w[z], 1))
            flow_y = face_y[z] * (w[z] - ahead(w[z], 0))
            value = heat[z] * w[z] + (flow_x - behind(flow_x, 1)) + (flow_y - behind(flow_y, 0))
            if z + 1 < zlayers:
                value = value + face_z[z] * (w[z] - w[z + 1])
            if z:
                value = value - face_z[z - 1] * (w[z - 1] - w[z])
            result.append(value)
        return result

    shift, scale = entry(2 * M), entry(2 * M + 1)

    def shifted(w):
        return [(a - shift * b) * scale for a, b in zip(operate(w), w)]

    basis = [field, shifted(field)]
    for _ in range(ITERS - 1):
        basis.append([2.0 * a - b for a, b in zip(shifted(basis[-1]), basis[-2])])
    own = [
        [jnp.where(lane < breadth, layer, 0.0)[0:height] for layer in vector] for vector in basis
    ]
    for n in range(ITERS):
        for z in range(zlayers):
            basis_ref[n, z] = own[n + 1][z][:, 0:breadth]
    slot = lax.broadcasted_iota(jnp.int32, (1, LANES), 1)
    packed = jnp.zeros((1, LANES), F32)
    at = 0
    for a in range(ITERS + 1):
        for b in range(a, ITERS + 1):
            product = own[a][0] * own[b][0]
            for z in range(1, zlayers):
                product = product + own[a][z] * own[b][z]
            value = jnp.sum(product, axis=0, keepdims=True)
            value = jnp.sum(value, axis=1, keepdims=True)
            packed = packed + jnp.where(slot == at, value, 0.0)
            at += 1
    sums_ref[...] = jnp.broadcast_to(packed[None], sums_ref.shape)


def finish_kernel(
    table_ref,
    sums_ref,
    field_ref,
    basis_ref,
    shares_ref,
    shares_hbm,
    iterate_hbm,
    defect_hbm,
    iterate_ref,
    defect_ref,
    sems,
):
    pairs = (shares_ref, shares_hbm), (iterate_ref, iterate_hbm), (defect_ref, defect_hbm)
    leaving = [pltpu.make_async_copy(*pair, sems.at[n]) for n, pair in enumerate(pairs)]
    leaving[0].start()
    total = jnp.sum(sums_ref[...], axis=0)
    gram = {}
    at = 0
    for a in range(ITERS + 1):
        for b in range(a, ITERS + 1):
            gram[a, b] = gram[b, a] = total[:, at : at + 1]
            at += 1
    shift, scale = (table_ref[n : n + 1, 0:1] for n in (2 * M, 2 * M + 2))

    def inner(left, right):
        rows = []
        for a, one in left.items():
            rows.append(one * total_of([other * gram[a, b] for b, other in right.items()]))
        return total_of(rows)

    def total_of(terms):
        while len(terms) > 1:
            terms = [sum(terms[n : n + 2][1:], terms[n]) for n in range(0, len(terms), 2)]
        return terms[0]

    def combine(left, factor, right):
        result = dict(left)
        for a, one in right.items():
            result[a] = result[a] + factor * one if a in result else factor * one
        return result

    def apply(vector):
        result = {}
        for a, one in vector.items():
            if a:
                moved = {a - 1: 0.5 * scale * one, a: shift * one, a + 1: 0.5 * scale * one}
            else:
                moved = {0: shift * one, 1: scale * one}
            for b, other in moved.items():
                result[b] = result[b] + other if b in result else other
        return result

    one = jnp.ones((1, 1), F32)
    iterate, defect, direction = {}, {0: one}, {0: one}
    norm = gram[0, 0]
    for iteration in range(ITERS):
        applied = apply(direction)
        step = norm / inner(direction, applied)
        iterate = combine(iterate, step, direction)
        defect = combine(defect, -step, applied)
        if iteration + 1 < ITERS:
            following = inner(defect, defect)
            direction = combine(defect, following / norm, direction)
            norm = following
    for ref, weights, move in ((iterate_ref, iterate, leaving[1]), (defect_ref, defect, leaving[2])):
        for z in range(field_ref.shape[0]):
            vectors = [field_ref[z]] + [basis_ref[n, z] for n in range(ITERS)]
            ref[z] = total_of([weight * vectors[a] for a, weight in weights.items()])
        move.start()
    for move in leaving:
        move.wait()


def per_device(
    row_count,
    col_count,
    fractions_source,
    x_source_edges,
    x_target_edges,
    y_source_edges,
    y_target_edges,
    conductivity_table,
    capacity,
    thermal_source_term,
):
    pairs, _, source_cells = fractions_source.shape
    zlayers, height, breadth = thermal_source_term.shape
    width = LANES * tiles(breadth + 4 * RIM)
    send_rows = BODY + (0 if compact(breadth) else 8 * tiles(breadth))
    params = pltpu.CompilerParams(vmem_limit_bytes=VMEM)

    vmem = pl.BlockSpec(memory_space=pltpu.VMEM)
    hbm = pl.BlockSpec(memory_space=pltpu.HBM)
    along_rows = 2 * LANES
    small = [
        x_source_edges,
        x_target_edges,
        y_source_edges,
        y_target_edges,
        conductivity_table,
        capacity,
    ]
    outgoing = jax.ShapeDtypeStruct((row_count, send_rows, LANES), F32)
    outgoing = pl.pallas_call(
        functools.partial(rezone_kernel, row_count),
        out_shape=outgoing,
        in_specs=[hbm] * 8,
        out_specs=hbm,
        scratch_shapes=[pltpu.VMEM(e.shape, e.dtype) for e in small]
        + [
            pltpu.VMEM(fractions_source.shape, F32),
            pltpu.VMEM(thermal_source_term.shape, F32),
            pltpu.VMEM((8, LANES * (tiles(source_cells + 1) + 1)), F32),
            pltpu.VMEM((along_rows, source_cells), F32),
            pltpu.VMEM(outgoing.shape, F32),
            pltpu.SemaphoreType.DMA((8,)),
            pltpu.SemaphoreType.DMA((row_count // 4,)),
        ],
        compiler_params=pltpu.CompilerParams(vmem_limit_bytes=FULL),
        name="rezone",
    )(*small, fractions_source, thermal_source_term)
    arrived = lax.all_to_all(outgoing, "row", split_axis=0, concat_axis=0, tiled=True)
    table = pl.pallas_call(
        table_kernel,
        out_shape=jax.ShapeDtypeStruct((-(-(2 * M + 3) // 8) * 8, LANES), F32),
        in_specs=[vmem] * 2,
        out_specs=vmem,
        compiler_params=params,
        name="table",
    )(conductivity_table, capacity)
    message = jax.ShapeDtypeStruct((pairs * TBLK + 2 * EDGE, width), F32)
    half = col_count // 2
    near, far = range(half), range(half, col_count)
    extended, *far_parts = pl.pallas_call(
        functools.partial(regroup_kernel, row_count, col_count, far),
        out_shape=[jax.ShapeDtypeStruct((zlayers, ROWS, width), F32)] + [message] * half,
        in_specs=[vmem] * 2,
        out_specs=[vmem] * (1 + half),
        compiler_params=params,
        name="regroup_far",
    )(arrived, thermal_source_term)

    def swap(part, mask):
        return lax.ppermute(part, "col", [(c, c ^ mask) for c in range(col_count)])

    far_parts = [swap(part, mask) for part, mask in zip(far_parts, far)]
    near_parts = pl.pallas_call(
        functools.partial(regroup_kernel, row_count, col_count, near),
        out_shape=[message] * half,
        in_specs=[vmem] * 3,
        out_specs=[vmem] * half,
        compiler_params=params,
        cost_estimate=pl.CostEstimate(flops=10**6, bytes_accessed=2 * 10**6, transcendentals=0),
        name="regroup_near",
    )(arrived, thermal_source_term, extended)
    parts = [swap(part, mask) if mask else part for part, mask in zip(near_parts, near)] + far_parts
    shares, basis, sums = pl.pallas_call(
        functools.partial(basis_kernel, col_count, height, breadth),
        out_shape=[
            jax.ShapeDtypeStruct((zlayers * M, height, breadth), F32),
            jax.ShapeDtypeStruct((ITERS, zlayers, height, breadth), F32),
            jax.ShapeDtypeStruct((row_count * col_count, 1, LANES), F32),
        ],
        in_specs=[vmem] * (2 + col_count),
        out_specs=[vmem] * 3,
        scratch_shapes=[pltpu.VMEM((col_count, *message.shape), F32)],
        compiler_params=params,
        name="basis",
    )(table, extended, *parts)
    sums = lax.all_to_all(sums, ("row", "col"), split_axis=0, concat_axis=0, tiled=True)
    rezoned_occupancy_shares, thermal_iterate, remaining_defect = pl.pallas_call(
        finish_kernel,
        out_shape=[jax.ShapeDtypeStruct(shares.shape, F32)]
        + [jax.ShapeDtypeStruct((zlayers, height, breadth), F32)] * 2,
        in_specs=[vmem] * 5,
        out_specs=[hbm] * 3,
        scratch_shapes=[pltpu.VMEM((zlayers, height, breadth), F32)] * 2
        + [pltpu.SemaphoreType.DMA((3,))],
        compiler_params=params,
        name="finish",
    )(table, sums, thermal_source_term, basis, shares)
    return rezoned_occupancy_shares, thermal_iterate, remaining_defect


def solution(mesh):
    placed = (P("col", "row", None), P(), P(), P(), P(), P(), P(), P(None, "row", "col"))
    return jax.shard_map(
        functools.partial(per_device, mesh.shape["row"], mesh.shape["col"]),
        mesh=mesh,
        in_specs=placed,
        out_specs=(P(None, "row", "col"), P(None, "row", "col"), P(None, "row", "col")),
        check_vma=False,
    )
```

```python
import functools

import jax
import jax.numpy as jnp
from jax import lax
from jax.experimental import pallas as pl
from jax.experimental.pallas import tpu as pltpu
from jax.sharding import PartitionSpec as P

M = 6
SBLK = 64
TBLK = 48
ITERS = 3
RIM = ITERS
ROWS = 56
LANES = 128
EDGE = ROWS - TBLK
HALF = TBLK // 2
KEPT = 2 * TBLK + HALF
CHUNK = LANES - 2 * TBLK
BODY = ROWS
VMEM = 48 * 1024 * 1024
FULL = 63 * 1024 * 1024
TINY = 1e-30
F32 = jnp.float32
BF16 = jnp.bfloat16


def tiles(cells):
    return -(-cells // LANES)


def compact(breadth):
    return breadth == 3 * CHUNK


def pack_rims(rims):
    count, spare = rims.shape[0], LANES - KEPT
    below = jnp.zeros((8 - count, LANES), F32)
    side = jnp.zeros((count, KEPT), F32)
    own = []
    for at in range(CHUNK, 2 * CHUNK, spare):
        own += [jnp.concatenate([side, rims[:, at : at + spare]], axis=1), below]
    own.append(jnp.zeros((TBLK - 8 * CHUNK // spare, LANES), F32))
    edge = jnp.concatenate([jnp.zeros((count, LANES - CHUNK), F32), rims[:, 0:CHUNK]], axis=1)
    lines = []
    for at in (0, RIM):
        parts = [rims[at + n : at + n + 1, 2 * CHUNK :] for n in range(RIM)]
        lines.append(jnp.concatenate(parts + [jnp.zeros((1, CHUNK), F32)], axis=1))
    gap = [jnp.zeros((RIM, LANES), F32)] + lines + [jnp.zeros((EDGE - RIM - 2, LANES), F32)]
    return (
        jnp.concatenate(own, axis=0),
        jnp.concatenate([edge, below], axis=0) + jnp.concatenate(gap, axis=0),
    )


def unpack_rims(own, edge, count):
    spare = LANES - KEPT
    last = [
        edge[RIM + n // RIM : RIM + n // RIM + 1, CHUNK * (n % RIM) : CHUNK * (n % RIM + 1)]
        for n in range(count)
    ]
    middle = [own[8 * n : 8 * n + count, KEPT:] for n in range(CHUNK // spare)]
    parts = [edge[0:count, LANES - CHUNK :]] + middle + [jnp.concatenate(last, axis=0)]
    return jnp.concatenate(parts, axis=1)


def product(lengths, dense, contract):
    count = lengths.shape[0]
    high = lengths.astype(BF16)
    low = (lengths - high.astype(F32)).astype(BF16)
    both = jnp.concatenate([high, low], axis=0)
    first = dense.astype(BF16)
    rest = dense - first.astype(F32)
    second = rest.astype(BF16)
    third = (rest - second.astype(F32)).astype(BF16)

    def dot(left, right):
        return lax.dot_general(
            left, right, (((1,), (contract,)), ((), ())), preferred_element_type=F32
        )

    total = dot(high, third)
    for piece in (second, first):
        part = dot(both, piece)
        total = (total + part[count:]) + part[:count]
    return total


def rezone_kernel(
    row_count,
    xs_hbm,
    xt_hbm,
    ys_hbm,
    yt_hbm,
    cond_hbm,
    heat_hbm,
    frac_hbm,
    field_hbm,
    out_hbm,
    xs_ref,
    xt_ref,
    ys_ref,
    yt_ref,
    cond_ref,
    heat_ref,
    frac_ref,
    field_ref,
    edges_ref,
    along_ref,
    out_ref,
    sems,
    out_sems,
):
    me = lax.axis_index("row")
    pairs = frac_ref.shape[0]
    moves = [
        pltpu.make_async_copy(here, there, sems.at[n])
        for n, (here, there) in enumerate(
            (
                (yt_hbm, yt_ref),
                (xt_hbm, xt_ref),
                (xs_hbm, xs_ref),
                (ys_hbm, ys_ref),
                (frac_hbm, frac_ref),
                (field_hbm, field_ref),
                (cond_hbm, cond_ref),
                (heat_hbm, heat_ref),
            )
        )
    ]
    for move in moves:
        move.start()
    edges_ref[...] = jnp.zeros_like(edges_ref)
    for rows in (slice(KEPT, LANES), slice(LANES + 2 * TBLK, along_ref.shape[0])):
        along_ref[rows, :] = jnp.zeros_like(along_ref[rows, :])
    for n, ref in enumerate((yt_ref, xt_ref, xs_ref, ys_ref)):
        moves[n].wait()
        edges_ref[n : n + 1, 0 : ref.shape[0]] = ref[...].astype(F32)[None, :]

    def from_here(row, start, lane):
        base = start // LANES * LANES
        if not isinstance(base, int):
            base = pl.multiple_of(base, LANES)
        window = edges_ref[row : row + 1, pl.ds(base, 2 * LANES)]
        return pltpu.roll(window, (lane - (start - base) + 2 * LANES) % (2 * LANES), 1)

    groups = tiles(row_count * TBLK)
    mine = from_here(1, me * TBLK, 0)
    lines = [
        edges_ref[0:1, LANES * g + ahead : LANES * (g + 1) + ahead]
        for ahead in (0, 1)
        for g in range(groups)
    ] + [turned[:, 0:LANES] for turned in (mine, pltpu.roll(mine, 2 * LANES - 1, 1))]
    spare = -len(lines) % 8
    if spare:
        lines.append(jnp.zeros((spare, LANES), F32))
    columns = jnp.transpose(jnp.concatenate(lines, axis=0))

    def shared(src_lo, src_hi, low, high):
        return jnp.maximum(jnp.minimum(src_hi, high) - jnp.maximum(src_lo, low), 0.0)

    lane = lax.broadcasted_iota(jnp.int32, (1, LANES), 1)
    x_lo = from_here(2, me * SBLK, 0)
    x_hi = pltpu.roll(x_lo, 2 * LANES - 1, 1)
    low = columns[0:TBLK, 2 * groups : 2 * groups + 1]
    high = columns[0:TBLK, 2 * groups + 1 : 2 * groups + 2]
    shared_x = shared(x_lo[:, 0:SBLK], x_hi[:, 0:SBLK], low, high)
    scale_x = 1.0 / (high - low)
    moves[5].wait()
    moves[6].wait()
    moves[7].wait()
    zlayers, height, breadth = field_ref.shape
    rims = []
    for rows in (slice(0, RIM), slice(height - RIM, height)):
        rims.append(jnp.concatenate([field_ref[layer, rows] for layer in range(zlayers)], axis=0))
    if compact(breadth):
        rims = [pack_rims(rim) for rim in rims]
    else:
        for r in range(row_count):
            rim = jnp.where(r > me, rims[1], rims[0])
            for t in range(tiles(breadth)):
                lo, hi = t * LANES, min((t + 1) * LANES, breadth)
                at = BODY + 8 * t
                out_ref[r, at : at + zlayers * RIM, 0 : hi - lo] = rim[:, lo:hi]
    resistance = 16.0 / cond_ref[...].astype(F32)[None, :]
    material = lax.broadcasted_iota(jnp.int32, (1, M), 1)
    factors = []
    for p in range(pairs):
        mine = material == lax.rem(lax.axis_index("col") * pairs + p, M)
        factors.append(
            [
                jnp.sum(jnp.where(mine, value, 0.0), axis=1, keepdims=True)
                for value in (resistance, heat_ref[...][None, :])
            ]
        )
    moves[4].wait()
    partial = [0.0, 0.0]
    for p in range(pairs):
        along = product(shared_x, frac_ref[p], 0) * scale_x
        if p + 1 < pairs:
            along_ref[p * TBLK : (p + 1) * TBLK, :] = along
        else:
            even = lax.rem(lax.axis_index("col"), 2) == 0
            along_ref[KEPT - HALF : KEPT, :] = jnp.where(even, along[0:HALF], along[HALF:])
        partial = [total + factor * along for total, factor in zip(partial, factors[p])]
    for n, total in enumerate(partial):
        along_ref[LANES + n * TBLK : LANES + (n + 1) * TBLK, :] = total
    per, unit = 4, 64
    width = per * SBLK
    shared_y, scale_y = [], []
    for q in range(row_count // per):
        src_lo = edges_ref[3:4, q * width : (q + 1) * width]
        src_hi = edges_ref[3:4, q * width + 1 : (q + 1) * width + 1]
        parts, scales = [], []
        for start in range(q * per * TBLK, (q + 1) * per * TBLK, unit):
            g, at = divmod(start, LANES)
            low = columns[at : at + unit, g : g + 1]
            high = columns[at : at + unit, groups + g : groups + g + 1]
            parts.append(shared(src_lo, src_hi, low, high))
            scales.append(1.0 / (high - low))
        shared_y.append(jnp.concatenate(parts, axis=0))
        scale_y.append(jnp.concatenate(scales, axis=0))
    row = lax.broadcasted_iota(jnp.int32, (8, LANES), 0)
    leaving, firsts, lasts, sent = [], [], [], 0
    for q in range(row_count // per):
        block = product(shared_y[q], along_ref[:, q * width : (q + 1) * width], 1) * scale_y[q]
        for n in range(per):
            r = q * per + n
            mine = block[n * TBLK : (n + 1) * TBLK]
            mine_own = mine[:, 0:LANES]
            if compact(breadth):
                mine_own = mine_own + jnp.where(r > me, rims[1][0], rims[0][0])
            out_ref[r, 0:TBLK, :] = mine_own
            firsts.append(mine[0:8, LANES:])
            lasts.append(mine[TBLK - 8 :, LANES:])
        ready = row_count if r + 1 == row_count else r
        for r in range(sent, ready):
            edge = jnp.zeros((8, LANES), F32)
            if r + 1 < row_count:
                edge = jnp.where(row < RIM, firsts[r + 1], edge)
            if r:
                edge = jnp.where(row >= 8 - RIM, lasts[r - 1], edge)
            edge = jnp.where(lane < 2 * TBLK, edge, 0.0)
            if compact(breadth):
                edge = edge + jnp.where(r > me, rims[1][1], rims[0][1])
            out_ref[r, TBLK:ROWS, :] = edge
        done = pl.ds(sent, ready - sent)
        leaving.append(pltpu.make_async_copy(out_ref.at[done], out_hbm.at[done], out_sems.at[q]))
        leaving[-1].start()
        sent = ready
    for move in leaving:
        move.wait()


def table_kernel(cond_ref, heat_ref, table_ref):
    resistance = 16.0 / cond_ref[...].astype(F32)[None, :]
    heat = heat_ref[...][None, :]
    middle = 5.0 * M / jnp.sum(resistance, axis=1, keepdims=True)
    shift = jnp.sum(heat, axis=1, keepdims=True) / M + middle
    rest = jnp.zeros((1, LANES - 2 * M - 3), F32)
    table = jnp.concatenate([resistance, heat, shift, 1.0 / middle, middle, rest], axis=1)
    table = jnp.transpose(jnp.broadcast_to(table, (LANES, LANES)))
    table_ref[...] = table[0 : table_ref.shape[0]]


def extend_rows(row_count, got_ref, field_ref, ext_ref):
    my_row = lax.axis_index("row")
    zlayers, height, breadth = field_ref.shape
    ext_ref[...] = jnp.zeros_like(ext_ref)
    below, above = jnp.maximum(my_row - 1, 0), jnp.minimum(my_row + 1, row_count - 1)
    count = zlayers * RIM
    for block, there, at in (
        (above, my_row < row_count - 1, height),
        (below, my_row > 0, ROWS - RIM),
    ):
        if compact(breadth):
            rims = unpack_rims(got_ref[block, 0:TBLK], got_ref[block, TBLK:ROWS], count)
        else:
            parts = [got_ref[block, BODY + 8 * t : BODY + 8 * t + count] for t in range(tiles(breadth))]
            rims = jnp.concatenate(parts, axis=1)[:, 0:breadth]
        rims = jnp.where(there, rims, 0.0)
        for layer in range(zlayers):
            ext_ref[layer, at : at + RIM, 0:breadth] = rims[layer * RIM : (layer + 1) * RIM]
    for layer in range(zlayers):
        ext_ref[layer, 0:height, 0:breadth] = field_ref[layer]


def regroup_kernel(row_count, col_count, pairs, masks, got_ref, field_ref, *refs):
    my_col = lax.axis_index("col")
    zlayers, _, breadth = field_ref.shape
    ext_ref, out_refs = refs[0], refs[1:]
    width = out_refs[0].shape[1]
    per_col = row_count // col_count
    if col_count // 2 in masks:
        extend_rows(row_count, got_ref, field_ref, ext_ref)

    def own(block, pair, first, last):
        start = pair * TBLK
        if pair + 1 < pairs:
            return got_ref[block, 0:TBLK, start + first : start + last]
        if last - first == TBLK:
            half = got_ref[block, 0:TBLK, start : start + HALF]
            return jnp.concatenate([half, half], axis=1)
        first = first % HALF
        return got_ref[block, 0:TBLK, start + first : start + first + RIM]

    def edge(block, which, first, last):
        return got_ref[block, TBLK:ROWS, which * TBLK + first : which * TBLK + last]

    for mask, out_ref in zip(masks, out_refs):
        c = my_col ^ mask
        start = c * per_col
        left, right = jnp.maximum(start - 1, 0), jnp.minimum(start + per_col, row_count - 1)

        def short(cells, kind, extra):
            parts = [cells(start + j, kind, 0, TBLK) for j in range(per_col)]
            count = parts[0].shape[0]
            parts.append(jnp.where(c < col_count - 1, cells(right, kind, 0, RIM), 0.0))
            parts.append(extra)
            used = breadth + 2 * RIM + extra.shape[1]
            parts.append(jnp.zeros((count, width - used), F32))
            parts.append(jnp.where(c > 0, cells(left, kind, TBLK - RIM, TBLK), 0.0))
            return jnp.concatenate(parts, axis=1)

        if compact(breadth):
            last = (pairs - 1) * TBLK
            for p in range(pairs - 1):
                extra = got_ref[start + p, 0:TBLK, last : last + HALF]
                out_ref[p * TBLK : (p + 1) * TBLK] = short(own, p, extra)
            for n in range(2):
                at = last + EDGE * n
                out_ref[at : at + EDGE] = short(edge, n, jnp.zeros((EDGE, RIM), F32))
            even = lax.rem(my_col, 2) == 0
            rim = jnp.where(
                even, own(right, pairs - 1, 0, RIM), own(left, pairs - 1, TBLK - RIM, TBLK)
            )
            parts = [rim[8 * g : 8 * g + 8] for g in range(TBLK // 8)]
            for layer in range(zlayers if mask else 0):
                whole = ext_ref[layer]
                cols = jnp.where(c > my_col, whole[:, breadth - RIM : breadth], whole[:, 0:RIM])
                parts += [cols[8 * g : 8 * g + 8] for g in range(ROWS // 8)]
            parts.append(jnp.zeros((8, width - RIM * len(parts)), F32))
            out_ref[last + 2 * EDGE :] = jnp.concatenate(parts, axis=1)
            continue

        def line(cells, rows, kind, layer):
            parts = [cells(start + j, kind, 0, TBLK) for j in range(per_col)]
            count = parts[0].shape[0]
            parts.append(jnp.where(c < col_count - 1, cells(right, kind, 0, RIM), 0.0))
            if layer < zlayers and mask:
                whole = ext_ref[layer, rows]
                parts.append(
                    jnp.where(c > my_col, whole[:, breadth - RIM : breadth], whole[:, 0:RIM])
                )
            else:
                parts.append(jnp.zeros((count, RIM), F32))
            parts.append(jnp.zeros((count, width - breadth - 3 * RIM), F32))
            parts.append(jnp.where(c > 0, cells(left, kind, TBLK - RIM, TBLK), 0.0))
            return jnp.concatenate(parts, axis=1)

        for p in range(pairs):
            out_ref[p * TBLK : (p + 1) * TBLK] = line(own, slice(0, TBLK), p, p)
        for n in range(2):
            at = pairs * TBLK + EDGE * n
            out_ref[at : at + EDGE] = line(edge, slice(TBLK, ROWS), n, n)


def basis_kernel(col_count, pairs, height, breadth, table_ref, ext_ref, *refs):
    arrivals, refs = refs[:col_count], refs[col_count:]
    shares_ref, basis_ref, sums_ref, got_ref = refs
    my_col = lax.axis_index("col")
    rows, width = ext_ref.shape[1:]
    last = (pairs - 1) * TBLK
    end = pairs * TBLK + 2 * EDGE
    for mask, arrival in enumerate(arrivals):
        c = my_col ^ mask
        if not compact(breadth):
            got_ref[c] = arrival[...]
            continue
        got_ref[c, 0:last] = arrival[0:last]
        got_ref[c, pairs * TBLK :] = arrival[last:]
        parts = []
        for p in range(pairs - 1):
            at = breadth + RIM
            parts += [arrival[p * TBLK : (p + 1) * TBLK, at : at + HALF]] * 2
        tile = arrival[last + 2 * EDGE :]
        rim = [tile[:, RIM * g : RIM * (g + 1)] for g in range(TBLK // 8)]
        rim = jnp.concatenate(rim, axis=0)
        parts += [rim, jnp.zeros((TBLK, width - breadth - 2 * RIM), F32), rim]
        got_ref[c, last : pairs * TBLK] = jnp.concatenate(parts, axis=1)
    zlayers = ext_ref.shape[0]
    lane = lax.broadcasted_iota(jnp.int32, (rows, width), 1)
    before, after = jnp.maximum(my_col - 1, 0), jnp.minimum(my_col + 1, col_count - 1)

    def ahead(array, axis):
        return pltpu.roll(array, array.shape[axis] - 1, axis)

    def behind(array, axis):
        return pltpu.roll(array, 1, axis)

    def face(one, other):
        return 2.0 * one * other / jnp.maximum(one + other, TINY)

    def entry(n):
        return table_ref[n : n + 1, 0:1]

    row = lax.broadcasted_iota(jnp.int32, (rows, width), 0)
    to_right = (lane >= breadth) & (lane < breadth + RIM)
    to_left = lane >= width - RIM
    inside = (lane < breadth) | (to_right & (my_col < col_count - 1)) | (to_left & (my_col > 0))
    inside = inside & ((row < TBLK + RIM) | (row >= ROWS - RIM))
    early = ((lane < breadth) & (lax.rem(lane, TBLK) < HALF)) | to_right
    early = early[0:TBLK]

    cell_k, heat, field = [], [], []
    for z in range(zlayers):
        inverse, total = 0.0, 0.0
        shares = []
        for m in range(M):
            c, p = divmod(z * M + m, pairs)
            shares.append(got_ref[c, p * TBLK : (p + 1) * TBLK])
        known = jnp.where(early, shares[pairs - 1], shares[M - 1])
        missing = 1.0 - known
        for m in range(M):
            if m not in (pairs - 1, M - 1):
                missing = missing - shares[m]
        shares[pairs - 1] = jnp.where(early, known, missing)
        shares[M - 1] = jnp.where(early, missing, known)
        for m, share in enumerate(shares):
            shares_ref[z * M + m] = share[:, 0:breadth]
            inverse = inverse + share * entry(m)
            total = total + share * entry(M + m)
        edge_inverse, edge_total = 0.0, 0.0
        for c in range(z * M // pairs, (z + 1) * M // pairs):
            edge_inverse = edge_inverse + got_ref[c, pairs * TBLK : pairs * TBLK + EDGE]
            edge_total = edge_total + got_ref[c, pairs * TBLK + EDGE : end]
        inverse = jnp.concatenate([inverse, edge_inverse], axis=0)
        total = jnp.concatenate([total, edge_total], axis=0)
        inverse, total = (jnp.where(inside, value, 0.0) for value in (inverse, total))
        cell_k.append(jnp.where(inverse > 0.0, 1.0 / jnp.where(inverse > 0.0, inverse, 1.0), 0.0))
        heat.append(total)
        if compact(breadth):
            sides = []
            for c in (before, after):
                at = RIM * (TBLK // 8 + z * ROWS // 8)
                parts = [
                    got_ref[c, end : end + 8, at + RIM * g : at + RIM * (g + 1)]
                    for g in range(ROWS // 8)
                ]
                sides.append(jnp.concatenate(parts, axis=0))
            left = jnp.concatenate([jnp.zeros((rows, width - RIM), F32), sides[0]], axis=1)
            right = jnp.concatenate(
                [
                    jnp.zeros((rows, breadth), F32),
                    sides[1],
                    jnp.zeros((rows, width - breadth - RIM), F32),
                ],
                axis=1,
            )
        else:
            left, right = (
                jnp.concatenate(
                    [
                        got_ref[c, z * TBLK : (z + 1) * TBLK],
                        got_ref[c, pairs * TBLK + EDGE * z : pairs * TBLK + EDGE * (z + 1)],
                    ],
                    axis=0,
                )
                for c in (before, after)
            )
            left = pltpu.roll(left, width - (breadth + 2 * RIM), 1)
            right = pltpu.roll(right, width - RIM, 1)
        value = ext_ref[z]
        value = jnp.where(
            (lane >= breadth) & (lane < breadth + RIM) & (my_col < col_count - 1), right, value
        )
        value = jnp.where((lane >= width - RIM) & (my_col > 0), left, value)
        field.append(value)
    face_x = [face(k, ahead(k, 1)) for k in cell_k]
    face_y = [face(k, ahead(k, 0)) for k in cell_k]
    face_z = [face(cell_k[z], cell_k[z + 1]) for z in range(zlayers - 1)]

    def operate(w):
        result = []
        for z in range(zlayers):
            flow_x = face_x[z] * (w[z] - ahead(w[z], 1))
            flow_y = face_y[z] * (w[z] - ahead(w[z], 0))
            value = heat[z] * w[z] + (flow_x - behind(flow_x, 1)) + (flow_y - behind(flow_y, 0))
            if z + 1 < zlayers:
                value = value + face_z[z] * (w[z] - w[z + 1])
            if z:
                value = value - face_z[z - 1] * (w[z - 1] - w[z])
            result.append(value)
        return result

    shift, scale = entry(2 * M), entry(2 * M + 1)

    def shifted(w):
        return [(a - shift * b) * scale for a, b in zip(operate(w), w)]

    basis = [field, shifted(field)]
    for _ in range(ITERS - 1):
        basis.append([2.0 * a - b for a, b in zip(shifted(basis[-1]), basis[-2])])
    own = [
        [jnp.where(lane < breadth, layer, 0.0)[0:height] for layer in vector] for vector in basis
    ]
    for n in range(ITERS):
        for z in range(zlayers):
            basis_ref[n, z] = own[n + 1][z][:, 0:breadth]
    slot = lax.broadcasted_iota(jnp.int32, (1, LANES), 1)
    packed = jnp.zeros((1, LANES), F32)
    at = 0
    for a in range(ITERS + 1):
        for b in range(a, ITERS + 1):
            product = own[a][0] * own[b][0]
            for z in range(1, zlayers):
                product = product + own[a][z] * own[b][z]
            value = jnp.sum(product, axis=0, keepdims=True)
            value = jnp.sum(value, axis=1, keepdims=True)
            packed = packed + jnp.where(slot == at, value, 0.0)
            at += 1
    sums_ref[...] = jnp.broadcast_to(packed[None], sums_ref.shape)


def finish_kernel(
    table_ref,
    sums_ref,
    field_ref,
    basis_ref,
    shares_ref,
    shares_hbm,
    iterate_hbm,
    defect_hbm,
    iterate_ref,
    defect_ref,
    sems,
):
    pairs = (shares_ref, shares_hbm), (iterate_ref, iterate_hbm), (defect_ref, defect_hbm)
    leaving = [pltpu.make_async_copy(*pair, sems.at[n]) for n, pair in enumerate(pairs)]
    leaving[0].start()
    total = jnp.sum(sums_ref[...], axis=0)
    gram = {}
    at = 0
    for a in range(ITERS + 1):
        for b in range(a, ITERS + 1):
            gram[a, b] = gram[b, a] = total[:, at : at + 1]
            at += 1
    shift, scale = (table_ref[n : n + 1, 0:1] for n in (2 * M, 2 * M + 2))

    def inner(left, right):
        rows = []
        for a, one in left.items():
            rows.append(one * total_of([other * gram[a, b] for b, other in right.items()]))
        return total_of(rows)

    def total_of(terms):
        while len(terms) > 1:
            terms = [sum(terms[n : n + 2][1:], terms[n]) for n in range(0, len(terms), 2)]
        return terms[0]

    def combine(left, factor, right):
        result = dict(left)
        for a, one in right.items():
            result[a] = result[a] + factor * one if a in result else factor * one
        return result

    def apply(vector):
        result = {}
        for a, one in vector.items():
            if a:
                moved = {a - 1: 0.5 * scale * one, a: shift * one, a + 1: 0.5 * scale * one}
            else:
                moved = {0: shift * one, 1: scale * one}
            for b, other in moved.items():
                result[b] = result[b] + other if b in result else other
        return result

    one = jnp.ones((1, 1), F32)
    iterate, defect, direction = {}, {0: one}, {0: one}
    norm = gram[0, 0]
    for iteration in range(ITERS):
        applied = apply(direction)
        step = norm / inner(direction, applied)
        iterate = combine(iterate, step, direction)
        defect = combine(defect, -step, applied)
        if iteration + 1 < ITERS:
            following = inner(defect, defect)
            direction = combine(defect, following / norm, direction)
            norm = following
    for ref, weights, move in ((iterate_ref, iterate, leaving[1]), (defect_ref, defect, leaving[2])):
        for z in range(field_ref.shape[0]):
            vectors = [field_ref[z]] + [basis_ref[n, z] for n in range(ITERS)]
            ref[z] = total_of([weight * vectors[a] for a, weight in weights.items()])
        move.start()
    for move in leaving:
        move.wait()


def per_device(
    row_count,
    col_count,
    fractions_source,
    x_source_edges,
    x_target_edges,
    y_source_edges,
    y_target_edges,
    conductivity_table,
    capacity,
    thermal_source_term,
):
    pairs, _, source_cells = fractions_source.shape
    zlayers, height, breadth = thermal_source_term.shape
    width = LANES * tiles(breadth + 4 * RIM)
    send_rows = BODY + (0 if compact(breadth) else 8 * tiles(breadth))
    params = pltpu.CompilerParams(vmem_limit_bytes=VMEM)

    vmem = pl.BlockSpec(memory_space=pltpu.VMEM)
    hbm = pl.BlockSpec(memory_space=pltpu.HBM)
    along_rows = 2 * LANES
    small = [
        x_source_edges,
        x_target_edges,
        y_source_edges,
        y_target_edges,
        conductivity_table,
        capacity,
    ]
    outgoing = jax.ShapeDtypeStruct((row_count, send_rows, LANES), F32)
    outgoing = pl.pallas_call(
        functools.partial(rezone_kernel, row_count),
        out_shape=outgoing,
        in_specs=[hbm] * 8,
        out_specs=hbm,
        scratch_shapes=[pltpu.VMEM(e.shape, e.dtype) for e in small]
        + [
            pltpu.VMEM(fractions_source.shape, F32),
            pltpu.VMEM(thermal_source_term.shape, F32),
            pltpu.VMEM((8, LANES * (tiles(source_cells + 1) + 1)), F32),
            pltpu.VMEM((along_rows, source_cells), F32),
            pltpu.VMEM(outgoing.shape, F32),
            pltpu.SemaphoreType.DMA((8,)),
            pltpu.SemaphoreType.DMA((row_count // 4,)),
        ],
        compiler_params=pltpu.CompilerParams(vmem_limit_bytes=FULL),
        name="rezone",
    )(*small, fractions_source, thermal_source_term)
    arrived = lax.all_to_all(outgoing, "row", split_axis=0, concat_axis=0, tiled=True)
    table = pl.pallas_call(
        table_kernel,
        out_shape=jax.ShapeDtypeStruct((-(-(2 * M + 3) // 8) * 8, LANES), F32),
        in_specs=[vmem] * 2,
        out_specs=vmem,
        compiler_params=params,
        name="table",
    )(conductivity_table, capacity)
    plain = pairs * TBLK + 2 * EDGE
    message = jax.ShapeDtypeStruct((plain + 8 - TBLK if compact(breadth) else plain, width), F32)
    half = col_count // 2
    near, far = range(half), range(half, col_count)
    extended, *far_parts = pl.pallas_call(
        functools.partial(regroup_kernel, row_count, col_count, pairs, far),
        out_shape=[jax.ShapeDtypeStruct((zlayers, ROWS, width), F32)] + [message] * half,
        in_specs=[vmem] * 2,
        out_specs=[vmem] * (1 + half),
        compiler_params=params,
        name="regroup_far",
    )(arrived, thermal_source_term)

    def swap(part, mask):
        return lax.ppermute(part, "col", [(c, c ^ mask) for c in range(col_count)])

    far_parts = [swap(part, mask) for part, mask in zip(far_parts, far)]
    near_parts = pl.pallas_call(
        functools.partial(regroup_kernel, row_count, col_count, pairs, near),
        out_shape=[message] * half,
        in_specs=[vmem] * 3,
        out_specs=[vmem] * half,
        compiler_params=params,
        cost_estimate=pl.CostEstimate(flops=10**6, bytes_accessed=2 * 10**6, transcendentals=0),
        name="regroup_near",
    )(arrived, thermal_source_term, extended)
    parts = [swap(part, mask) if mask else part for part, mask in zip(near_parts, near)] + far_parts
    shares, basis, sums = pl.pallas_call(
        functools.partial(basis_kernel, col_count, pairs, height, breadth),
        out_shape=[
            jax.ShapeDtypeStruct((zlayers * M, height, breadth), F32),
            jax.ShapeDtypeStruct((ITERS, zlayers, height, breadth), F32),
            jax.ShapeDtypeStruct((row_count * col_count, 1, LANES), F32),
        ],
        in_specs=[vmem] * (2 + col_count),
        out_specs=[vmem] * 3,
        scratch_shapes=[pltpu.VMEM((col_count, plain + 8 * compact(breadth), width), F32)],
        compiler_params=params,
        name="basis",
    )(table, extended, *parts)
    sums = lax.all_to_all(sums, ("row", "col"), split_axis=0, concat_axis=0, tiled=True)
    rezoned_occupancy_shares, thermal_iterate, remaining_defect = pl.pallas_call(
        finish_kernel,
        out_shape=[jax.ShapeDtypeStruct(shares.shape, F32)]
        + [jax.ShapeDtypeStruct((zlayers, height, breadth), F32)] * 2,
        in_specs=[vmem] * 5,
        out_specs=[hbm] * 3,
        scratch_shapes=[pltpu.VMEM((zlayers, height, breadth), F32)] * 2
        + [pltpu.SemaphoreType.DMA((3,))],
        compiler_params=params,
        name="finish",
    )(table, sums, thermal_source_term, basis, shares)
    return rezoned_occupancy_shares, thermal_iterate, remaining_defect


def solution(mesh):
    placed = (P("col", "row", None), P(), P(), P(), P(), P(), P(), P(None, "row", "col"))
    return jax.shard_map(
        functools.partial(per_device, mesh.shape["row"], mesh.shape["col"]),
        mesh=mesh,
        in_specs=placed,
        out_specs=(P(None, "row", "col"), P(None, "row", "col"), P(None, "row", "col")),
        check_vma=False,
    )
```
